32 devices in a mesh: tm: 8 (over z, x), space: 4 (over y, core).
Axes of the slice: x: 2, y: 2, z: 4, core: 2. Of those that a mesh axis runs over, the one named last changes fastest.
Arguments:
- layer_input: bfloat16 [8, 512, 2048], P('tm', 'space'), may hold values from -6 to 6
- frame_real: int32 [8], replicated, may hold values from 0 to 1, as said below
- gain_attn: bfloat16 [2048], P(('tm', 'space')), may hold values from 0.5 to 1.5
- w_qkv: bfloat16 [2048, 6144], P(('tm', 'space')), may hold values from -0.125 to 0.125
- w_out: bfloat16 [2048, 2048], P(('tm', 'space')), may hold values from -1.5 to 1.5
- gain_mlp: bfloat16 [2048], P(('tm', 'space')), may hold values from 0.5 to 1.5
- w_up: bfloat16 [2048, 8192], P(('tm', 'space')), may hold values from -0.125 to 0.125
- w_down: bfloat16 [2048, 8192], P(('tm', 'space')), may hold values from -0.0625 to 0.0625
- cotangent: bfloat16 [8, 512, 2048], P('tm', 'space'), may hold values from -6 to 6
Outputs:
- out: bfloat16 [8, 512, 2048], P('tm', 'space')
- grad_input: float32 [8, 512, 2048], P('tm', 'space')
- grad_gain_attn: float32 [2048], P(('tm', 'space'))
- grad_w_qkv: float32 [2048, 6144], P(('tm', 'space'))
- grad_w_out: float32 [2048, 2048], P(('tm', 'space'))
- grad_gain_mlp: float32 [2048], P(('tm', 'space'))
- grad_w_up: float32 [2048, 8192], P(('tm', 'space'))
- grad_w_down: float32 [2048, 8192], P(('tm', 'space'))
The draws below stay inside these ranges and needn't reach their ends.
Inputs may be any that keep to these rules, and one draw needn't show every extreme that they name: `frame_real`: in every clip of 8 slots the first two frames and the last frame are real.
All inputs are finite; a program needn't handle non-finite values.
Results may differ from the reference program's by a relative error of at most 0.015.
Values may be sent and summed in bfloat16 or wider, within the bound.
No kernel may reach another device: no remote copies, remote signals or barrier semaphores. Data moves between devices by JAX's collectives and lax.ppermute only.
A program may use at most 512 MiB of HBM per device.

```python
import jax
import jax.numpy as jnp
from jax import lax

D = 2048
HEADS = 16
HEAD = 128
FF = 8192
FRAME = 512
GROUP = 8
SLOTS = 8


def draw_frame_real(key, part):
    key = jax.random.fold_in(key, 11)
    slot_index = jnp.arange(SLOTS, dtype=jnp.int32)
    coin_flip = jax.random.randint(key, (SLOTS,), 0, 3)
    local_place = slot_index % GROUP
    border = (local_place == 0) | (local_place == 1) | (local_place == GROUP - 1)
    return jnp.where(border | (coin_flip > 0), 1, 0).astype(jnp.int32)


def strengthened(drawn, own_key, source, target, blocks, factor):
    owner, partner = [(jnp.arange(drawn.shape[dim]) // (drawn.shape[dim] // blocks)).reshape([-1 if axis == dim else 1 for axis in range(drawn.ndim)]) for dim in (source, target)]
    chosen = jax.random.permutation(own_key, blocks)[partner]
    strong = (owner == chosen) | (owner == (partner + blocks // 2) % blocks)
    return jnp.where(strong, factor * drawn, drawn)


def block_scale(key, extent, shards, low, top_value):
    def one(axis_at, blocks):
        draws = jax.random.uniform(jax.random.fold_in(jax.random.fold_in(key, 6), axis_at), (blocks,), jnp.float32, low / len(shards), top_value / len(shards))
        return jnp.repeat(jnp.exp(draws), extent[axis_at] // blocks).reshape((-1,) + (1,) * (len(extent) - axis_at - 1))

    factor_of = one(*shards[0])
    for cut in shards[1:]:
        factor_of = factor_of * one(*cut)
    return factor_of


def scatter_about(stream_key, shape, scale, most, pieces=(), held_as=jnp.bfloat16):
    drawn = jax.random.normal(stream_key, shape, jnp.float32) * scale
    if len(pieces) > 0:
        drawn = block_scale(stream_key, shape, pieces, -0.22, 0.18) * drawn
    return jnp.clip(drawn, min=-most, max=most).astype(held_as)


def noise_with(rng, dims, scale, limit, split, heavy, kind=jnp.bfloat16):
    values = scale * jax.random.normal(rng, dims, jnp.float32)
    if split:
        values = values * block_scale(rng, dims, split, -0.22, 0.18)
    return jnp.clip(strengthened(values, jax.random.fold_in(rng, 3), *heavy), -limit, limit).astype(kind)


def setup_inputs(seed: int = 0) -> dict:
    key_of = jax.random.split(jax.random.key(seed), 10)
    return {
        "layer_input": scatter_about(key_of[0], (SLOTS, FRAME, D), 1.0, 6.0, ((0, 8), (1, 4))),
        "frame_real": draw_frame_real(jax.random.fold_in(key_of[9], 71), 0),
        "gain_attn": jnp.clip(1.0 + 0.1 * jax.random.normal(key_of[2], (D,), jnp.float32), 0.5, 1.5).astype(jnp.bfloat16),
        "w_qkv": scatter_about(key_of[3], (D, 3 * D), D ** -0.5, 0.125, ((0, 32),)),
        "w_out": scatter_about(key_of[4], (D, D), (max(D // 128, 1)) ** -0.5, 1.5, ((0, 32),)),
        "gain_mlp": jnp.clip(1.0 + 0.1 * jax.random.normal(key_of[5], (D,), jnp.float32), 0.5, 1.5).astype(jnp.bfloat16),
        "w_up": scatter_about(key_of[6], (D, FF), D ** -0.5, 0.125, ((0, 32),)),
        "w_down": scatter_about(key_of[7], (D, FF), FF ** -0.5, 0.0625, ((0, 32),)),
        "cotangent": noise_with(key_of[8], (SLOTS, FRAME, D), 1.0, 6.0, ((0, 8), (1, 4)), (0, 2, 8, 2.0)),
    }


highest = lax.Precision.HIGHEST
epsilon = 1e-05
masked_value = -1e+30

@jax.custom_vjp
def low(v):
    return lax.optimization_barrier(v.astype(jnp.bfloat16)).astype(jnp.float32)

@jax.custom_vjp
def low_back(v):
    return v

def low_keep(v):
    return (low(v), None)

def low_pass(kept, grad):
    return (grad,)

def back_keep(v):
    return (v, None)

def back_low(kept, grad):
    return (low(grad),)
low.defvjp(low_keep, low_pass)
low_back.defvjp(back_keep, back_low)

def layer_norm(values):
    center = lax.optimization_barrier(jnp.mean(values, axis=-1, keepdims=True))
    shifted = values - center
    spread = lax.optimization_barrier(jnp.mean(shifted * shifted, axis=-1, keepdims=True))
    return shifted * lax.rsqrt(spread + epsilon)

def rope_tables(positions):
    half_dim = HEAD // 2
    inverse_freq = jnp.exp(-jnp.log(10000.0) * jnp.arange(half_dim, dtype=jnp.float32) * 2.0 / HEAD)
    angles = positions.astype(jnp.float32)[:, None] * inverse_freq[None, :]
    angles = jnp.concatenate([angles, angles], axis=-1)
    return (jnp.cos(angles), jnp.sin(angles))

def rotate(tensor, cosine_table, sine_table):
    half_dim = HEAD // 2
    turned = jnp.concatenate([-tensor[..., half_dim:], tensor[..., :half_dim]], axis=-1)
    return tensor * cosine_table[:, None, :] + turned * sine_table[:, None, :]

def attend(queries, keys, values, frame_real):
    span = GROUP * FRAME
    clip_count = SLOTS // GROUP
    query_blocks = queries.reshape(SLOTS, FRAME, HEADS, HEAD)
    key_blocks = keys.reshape(clip_count, span, HEADS, HEAD)
    value_blocks = values.reshape(clip_count, span, HEADS, HEAD)
    real_clip = frame_real.reshape(clip_count, GROUP)
    key_frame = jnp.arange(span, dtype=jnp.int32) // FRAME
    key_place = jnp.arange(span, dtype=jnp.int32) % FRAME
    query_place = jnp.arange(FRAME, dtype=jnp.int32)

    def one_item(item_index):
        slot_index = item_index // HEADS
        head_index = item_index % HEADS
        clip_index = slot_index // GROUP
        local_slot = slot_index % GROUP
        query_tile = query_blocks[slot_index, :, head_index, :]
        key_tile = key_blocks[clip_index, :, head_index, :]
        value_tile = value_blocks[clip_index, :, head_index, :]
        scores = jnp.dot(query_tile, key_tile.T, precision=highest) * HEAD ** (-0.5)
        scores = low_back(scores)
        real_keys = real_clip[clip_index][key_frame]
        earlier = (key_frame < local_slot) & (frame_real[slot_index] > 0) & (real_keys > 0)
        own_frame = (key_frame == local_slot)[None, :] & (key_place[None, :] <= query_place[:, None])
        allowed = own_frame | earlier[None, :]
        scores = jnp.where(allowed, scores, masked_value)
        row_max = lax.optimization_barrier(jnp.max(scores, axis=-1, keepdims=True))
        weights = jnp.exp(scores - row_max)
        probs = weights / lax.optimization_barrier(jnp.sum(weights, axis=-1, keepdims=True))
        return jnp.dot(low(probs), value_tile, precision=highest)
    outputs = lax.map(jax.checkpoint(one_item), jnp.arange(SLOTS * HEADS, dtype=jnp.int32))
    outputs = outputs.reshape(SLOTS, HEADS, FRAME, HEAD).transpose(0, 2, 1, 3)
    return outputs.reshape(SLOTS * FRAME, HEADS, HEAD)

def reference(layer_input, frame_real, gain_attn, w_qkv, w_out, gain_mlp, w_up, w_down, cotangent):
    token_index = jnp.arange(SLOTS * FRAME, dtype=jnp.int32)
    positions = token_index // FRAME % GROUP * FRAME + token_index % FRAME
    cosine_table, sine_table = rope_tables(positions)

    def forward(inputs, gain_one, weight_qkv, weight_out, gain_two, weight_up, weight_down):
        flat = inputs.reshape(SLOTS * FRAME, D)
        normed = low(layer_norm(flat) * gain_one)
        mixed = low_back(jnp.dot(normed, weight_qkv, precision=highest))
        queries = low(rotate(mixed[:, :D].reshape(-1, HEADS, HEAD), cosine_table, sine_table))
        keys = low(rotate(mixed[:, D:2 * D].reshape(-1, HEADS, HEAD), cosine_table, sine_table))
        values = low(mixed[:, 2 * D:].reshape(-1, HEADS, HEAD))
        attended = attend(queries, keys, values, frame_real).reshape(-1, D)
        attended = low(low_back(attended))
        branch = low_back(jnp.dot(attended, weight_out, precision=highest))
        middle = flat + branch
        second = low(layer_norm(middle) * gain_two)
        hidden = low_back(jnp.dot(second, weight_up, precision=highest))
        activated = low(jax.nn.gelu(hidden))
        result = middle + jnp.dot(activated, weight_down.T, precision=highest)
        return result.reshape(SLOTS, FRAME, D)
    output, backward = jax.vjp(forward, layer_input.astype(jnp.float32), gain_attn.astype(jnp.float32), w_qkv.astype(jnp.float32), w_out.astype(jnp.float32), gain_mlp.astype(jnp.float32), w_up.astype(jnp.float32), w_down.astype(jnp.float32))
    grads = backward(cotangent.astype(jnp.float32))
    return (output.astype(jnp.bfloat16), grads[0], grads[1], grads[2], grads[3], grads[4], grads[5], grads[6])
```

```python
import functools

import jax
import jax.numpy as jnp
import numpy as np
from jax import lax
from jax.experimental import pallas as pl
from jax.experimental.pallas import tpu as pltpu
from jax.sharding import PartitionSpec as P

HEADS = 16
HEAD = 128
AXES = ("tm", "space")
BLOCK = 128

epsilon = 1e-05
masked_value = -1e30
inv_root = HEAD ** (-0.5)
to_log2 = inv_root * 1.4426950408889634

bf16 = jnp.bfloat16
f32 = jnp.float32


def matmul(left, right, dims=((1,), (0,))):
    return lax.dot_general(left, right, (dims, ((), ())), preferred_element_type=f32)


def tied(*values):
    return lax.optimization_barrier(values)


class Plan:
    def __init__(self, tm, space, frame_rows):
        self.count = tm * space
        self.space = space
        self.slots = tm
        self.clip = min(16, tm)
        count = self.count
        self.team = (count // 4, space // 2)
        self.heads = (count // 2, count // 8)
        bits = [1 << i for i in range(count.bit_length() - 1)]
        taken = set(self.team + self.heads)
        self.parts = [b for b in reversed(bits) if b not in taken]
        self.gather = [self.heads[0], self.heads[1]] + [b for b in self.parts if b != 1]
        self.team_rel = [0, self.team[1], self.team[0], self.team[0] | self.team[1]]
        self.head_rel = [0, self.heads[1], self.heads[0], self.heads[0] | self.heads[1]]
        self.block_rel = [h | t for h in self.head_rel for t in self.team_rel]
        self.part_rel = [
            sum(b for j, b in enumerate(self.parts) if (i >> j) & 1)
            for i in range(1 << len(self.parts))
        ]
        devices = range(count)
        octet = self.team[0] | self.team[1] | 1
        self.octets = self.groups(octet)
        self.square = sum(self.team) + sum(self.heads)
        self.squares = self.groups(self.square)
        self.square_bits = [b for b in reversed(bits) if b & self.square]
        self.devices = devices

    def groups(self, mask):
        held = {}
        for d in range(self.count):
            held.setdefault(d & ~mask, []).append(d)
        return list(held.values())

    def swap(self, value, mask):
        return lax.ppermute(value, AXES, [(d, d ^ mask) for d in self.devices])


def layer_norm(values):
    center = jnp.mean(values, axis=-1, keepdims=True)
    shifted = values - center
    spread = jnp.mean(shifted * shifted, axis=-1, keepdims=True)
    scale = lax.rsqrt(spread + epsilon)
    return shifted * scale, scale


def layer_norm_back(grads, normed, scale):
    inner = jnp.mean(grads * normed, axis=-1, keepdims=True)
    return (grads - jnp.mean(grads, axis=-1, keepdims=True) - normed * inner) * scale


def transposed(tile):
    return tile.astype(f32).T.astype(tile.dtype)


def attend_kernel(plan, info, real, own, other, out, out_t, lse, keys, values, values_t):
    me = info[0]
    n_blocks = len(plan.block_rel)
    for part, part_rel in enumerate(plan.part_rel):

        def place(b, _, part=part, part_rel=part_rel):
            home = me ^ part_rel ^ info[24 + b]
            if part == 0:
                key, value = own[b, :, HEAD : 2 * HEAD], own[b, :, 2 * HEAD :]
            else:
                key, value = other[part - 1, b, :, :HEAD], other[part - 1, b, :, HEAD:]
            rows = pl.ds(pl.multiple_of(home * BLOCK, BLOCK), BLOCK)
            keys[rows, :] = key
            values[rows, :] = value
            values_t[home] = transposed(value)
            return 0

        lax.fori_loop(0, n_blocks, place, 0)

    frame = plan.space * BLOCK
    two = 2 * BLOCK
    lane = lax.broadcasted_iota(jnp.int32, (1, two), 1)
    q_place = jnp.where(lane < BLOCK, info[1] + lane, info[2] + lane - BLOCK)

    def tile(i, _):
        slot, first = info[8 + i], info[16 + i]
        q = jnp.concatenate([own[2 * i, :, :HEAD], own[2 * i + 1, :, :HEAD]], axis=0)

        def scores(g):
            key = keys[pl.ds(pl.multiple_of(g * frame, frame), frame), :]
            return matmul(key, q, ((1,), (1,)))

        def value_t(g):
            return jnp.concatenate(
                [values_t[g * plan.space + s] for s in range(plan.space)], axis=1
            )

        s = scores(slot)
        k_place = lax.broadcasted_iota(jnp.int32, (frame, two), 0)
        s = jnp.where(k_place <= q_place, s, masked_value)
        top = jnp.max(s, axis=0, keepdims=True)
        p = jnp.exp2((s - top) * to_log2)
        total = jnp.sum(p, axis=0, keepdims=True)
        acc = matmul(value_t(slot), p.astype(bf16))

        def step(g, carry):
            def use(carry):
                top, total, acc = carry
                s = scores(g)
                new = jnp.maximum(top, jnp.max(s, axis=0, keepdims=True))
                fade = jnp.exp2((top - new) * to_log2)
                p = jnp.exp2((s - new) * to_log2)
                total = total * fade + jnp.sum(p, axis=0, keepdims=True)
                acc = acc * fade + matmul(value_t(g), p.astype(bf16))
                return new, total, acc

            return lax.cond(real[g] > 0, use, lambda c: c, carry)

        first = jnp.where(real[slot] > 0, first, slot)
        top, total, acc = lax.fori_loop(first, slot, step, (top, total, acc))
        lse[i] = top * to_log2 + jnp.log2(total)
        acc = acc / total
        out_t[i] = acc
        back = acc.T.astype(bf16)
        out[info[40 + 2 * i]] = back[:BLOCK]
        out[info[40 + 2 * i + 1]] = back[BLOCK:]
        return 0

    lax.fori_loop(0, n_blocks // 2, tile, 0)


def attend_back_kernel(
    plan, info, real, own, keys, values, grads, out_t, lse, dq, dkv_own, dkv_other, dk, dv, keys_t
):
    me = info[0]
    n_blocks = len(plan.block_rel)

    def clear(b, _):
        rows = pl.ds(pl.multiple_of(b * BLOCK, BLOCK), BLOCK)
        dk[rows, :] = jnp.zeros((BLOCK, HEAD), f32)
        dv[rows, :] = jnp.zeros((BLOCK, HEAD), f32)
        keys_t[b] = transposed(keys[rows, :])
        return 0

    lax.fori_loop(0, plan.count, clear, 0)

    frame = plan.space * BLOCK
    two = 2 * BLOCK
    lane = lax.broadcasted_iota(jnp.int32, (1, two), 1)
    q_place = jnp.where(lane < BLOCK, info[1] + lane, info[2] + lane - BLOCK)

    def tile(i, _):
        slot, first = info[8 + i], info[16 + i]
        q = jnp.concatenate([own[2 * i, :, :HEAD], own[2 * i + 1, :, :HEAD]], axis=0)
        do = jnp.concatenate([grads[info[40 + 2 * i]], grads[info[40 + 2 * i + 1]]], axis=0)
        delta = jnp.sum(do.astype(f32).T * out_t[i], axis=0, keepdims=True)
        log_total = lse[i]

        def turn(g, mask):
            rows = pl.ds(pl.multiple_of(g * frame, frame), frame)
            key, value = keys[rows, :], values[rows, :]
            s = matmul(key, q, ((1,), (1,)))
            dp = matmul(value, do, ((1,), (1,)))
            p = jnp.exp2(s * to_log2 - log_total)
            if mask:
                k_place = lax.broadcasted_iota(jnp.int32, (frame, two), 0)
                p = jnp.where(k_place <= q_place, p, 0.0)
            ds = (p * (dp - delta)).astype(bf16)
            dv[rows, :] += matmul(p.astype(bf16), do)
            dk[rows, :] += matmul(ds, q)
            key_t = jnp.concatenate(
                [keys_t[g * plan.space + s] for s in range(plan.space)], axis=1
            )
            return matmul(key_t, ds)

        dq_t = turn(slot, True)

        def step(g, dq_t):
            return lax.cond(real[g] > 0, lambda c: c + turn(g, False), lambda c: c, dq_t)

        first = jnp.where(real[slot] > 0, first, slot)
        dq_t = lax.fori_loop(first, slot, step, dq_t)
        back = (dq_t * inv_root).T.astype(bf16)
        dq[2 * i] = back[:BLOCK]
        dq[2 * i + 1] = back[BLOCK:]
        return 0

    lax.fori_loop(0, n_blocks // 2, tile, 0)

    for part, part_rel in enumerate(plan.part_rel):

        def hand_out(b, _, part=part, part_rel=part_rel):
            home = me ^ part_rel ^ info[24 + b]
            rows = pl.ds(pl.multiple_of(home * BLOCK, BLOCK), BLOCK)
            pair = jnp.concatenate([dk[rows, :] * inv_root, dv[rows, :]], axis=1).astype(bf16)
            if part == 0:
                dkv_own[b] = pair
            else:
                dkv_other[part - 1, b] = pair
            return 0

        lax.fori_loop(0, n_blocks, hand_out, 0)


def call(kernel, n_scalar, n_in, outs, scratch, cost):
    return pl.pallas_call(
        kernel,
        out_shape=outs,
        in_specs=[pl.BlockSpec(memory_space=pltpu.SMEM)] * n_scalar
        + [pl.BlockSpec(memory_space=pltpu.VMEM)] * n_in,
        out_specs=tuple(pl.BlockSpec(memory_space=pltpu.VMEM) for _ in outs),
        scratch_shapes=scratch,
        cost_estimate=cost,
        compiler_params=pltpu.CompilerParams(vmem_limit_bytes=58 << 20),
    )


def attend(plan, info, real, own, other):
    blocks = len(plan.block_rel)
    tokens = plan.count * BLOCK
    work = blocks * BLOCK * min(plan.clip * plan.space * BLOCK, tokens) // 2
    shape = jax.ShapeDtypeStruct
    return call(
        functools.partial(attend_kernel, plan),
        2,
        2,
        (
            shape((blocks, BLOCK, HEAD), bf16),
            shape((blocks // 2, HEAD, 2 * BLOCK), f32),
            shape((blocks // 2, 1, 2 * BLOCK), f32),
            shape((tokens, HEAD), bf16),
            shape((tokens, HEAD), bf16),
        ),
        [pltpu.VMEM((plan.count, HEAD, BLOCK), bf16)],
        pl.CostEstimate(flops=8 * work * HEAD, bytes_accessed=8 << 20, transcendentals=work),
    )(info, real, own, other)


def attend_back(plan, info, real, own, keys, values, grads, out_t, lse):
    blocks = len(plan.block_rel)
    tokens = plan.count * BLOCK
    work = blocks * BLOCK * min(plan.clip * plan.space * BLOCK, tokens) // 2
    shape = jax.ShapeDtypeStruct
    return call(
        functools.partial(attend_back_kernel, plan),
        2,
        6,
        (
            shape((blocks, BLOCK, HEAD), bf16),
            shape((blocks, BLOCK, 2 * HEAD), bf16),
            shape((len(plan.part_rel) - 1, blocks, BLOCK, 2 * HEAD), bf16),
        ),
        [
            pltpu.VMEM((tokens, HEAD), f32),
            pltpu.VMEM((tokens, HEAD), f32),
            pltpu.VMEM((plan.count, HEAD, BLOCK), bf16),
        ],
        pl.CostEstimate(flops=20 * work * HEAD, bytes_accessed=8 << 20, transcendentals=work),
    )(info, real, own, keys, values, grads, out_t, lse)


def on_device(
    plan, layer_input, frame_real, gain_attn, w_qkv, w_out, gain_mlp, w_up, w_down, cotangent
):
    rows = layer_input.shape[1]
    width = layer_input.shape[2]
    shard = w_up.shape[0]
    count, space = plan.count, plan.space
    me = lax.axis_index("tm") * space + lax.axis_index("space")
    inputs = layer_input[0].astype(f32)
    grad_out = cotangent[0].astype(f32)
    swap = plan.swap
    team_hi, team_lo = plan.team
    n_gather = len(plan.gather)
    k_count = 1 << n_gather
    low_gather = min(plan.gather)
    chunk = low_gather * shard
    n_chunks = width // chunk

    def has(bit):
        return (me & bit) != 0

    order = [
        (
            sum(b for j, b in enumerate(plan.gather) if (i >> j) & 1) + (team_hi if t else 0)
        )
        // low_gather
        for i in range(k_count)
        for t in range(2)
    ]
    inverse = [order.index(m) for m in range(n_chunks)]

    def flipped(pieces):
        for bit in plan.gather:
            step = bit // low_gather
            pieces = [
                jnp.where(has(bit), pieces[m ^ step], pieces[m]) for m in range(n_chunks)
            ]
        return pieces

    def to_rel(value):
        pieces = flipped([value[:, m * chunk : (m + 1) * chunk] for m in range(n_chunks)])
        return jnp.concatenate([pieces[m] for m in order], axis=1)

    def from_rel(value):
        pieces = [value[:, m * chunk : (m + 1) * chunk] for m in range(n_chunks)]
        return jnp.concatenate(flipped([pieces[m] for m in inverse]), axis=1)

    half = rows // 2

    def team_gather(value):
        a, b = value[:half], value[half:]
        a_lo = swap(a, team_lo)
        b_hi = swap(b, team_hi)
        a_hi, a_both = jnp.split(swap(jnp.concatenate([a, a_lo]), team_hi), 2)
        b_lo, b_both = jnp.split(swap(jnp.concatenate([b, b_hi]), team_lo), 2)
        return jnp.concatenate([a, b, a_lo, b_lo, a_hi, b_hi, a_both, b_both])

    def team_scatter(parts):
        parts = parts.reshape(4, 2, half, width)
        a, b = parts[:, 0], parts[:, 1]
        a_got = swap(a[2:], team_hi)
        b_got = swap(jnp.stack([b[1], b[3]]), team_lo)
        a_lo = a[1].astype(f32) + a_got[1].astype(f32)
        b_hi = b[2].astype(f32) + b_got[1].astype(f32)
        a_last = swap(a_lo.astype(bf16), team_lo)
        b_last = swap(b_hi.astype(bf16), team_hi)
        a_sum = a[0].astype(f32) + a_got[0].astype(f32) + a_last.astype(f32)
        b_sum = b[0].astype(f32) + b_got[0].astype(f32) + b_last.astype(f32)
        return jnp.concatenate([a_sum, b_sum])

    def octet(value):
        return lax.all_to_all(value, AXES, 0, 0, axis_index_groups=plan.octets)

    def square(value):
        return lax.all_to_all(value, AXES, 0, 0, axis_index_groups=plan.squares)

    def spread(weight):
        block = octet(weight).reshape(8 * shard, -1)
        for bit in plan.gather:
            block = jnp.concatenate([block, swap(block, bit)])
        return block, swap(block, 1)

    def collected(mine, others):
        block = mine.astype(f32) + swap(others, 1).astype(f32)
        for bit in reversed(plan.gather):
            block = block.reshape(2, block.shape[0] // 2, -1)
            block = block[0] + swap(block[1].astype(bf16), bit).astype(f32)
        block = octet(block.astype(bf16).reshape(8, shard, -1))
        return block.astype(f32)

    gain_one = gain_attn.astype(f32)[:, None]
    gain_two = gain_mlp.astype(f32)[:, None]
    qkv_scaled = (w_qkv.astype(f32) * gain_one).astype(bf16)
    up_scaled = (w_up.astype(f32) * gain_two).astype(bf16)
    n_ff = w_up.shape[1] // 8
    qkv_sent = (
        qkv_scaled.reshape(shard, 3, 8, 2 * HEAD).transpose(2, 0, 1, 3).reshape(8, shard, 6 * HEAD)
    )
    up_sent = up_scaled.reshape(shard, 8, n_ff).transpose(1, 0, 2)
    down_sent = w_down.reshape(shard, 8, n_ff).transpose(1, 0, 2)

    normed_one, scale_one = layer_norm(inputs)
    first_all = team_gather(to_rel(normed_one.astype(bf16)))
    qkv_mine, qkv_other = spread(qkv_sent)
    out_matrix = lax.all_gather(w_out, AXES, axis=0, tiled=True)
    up_mine, up_other = spread(up_sent)
    down_mine, down_other = spread(down_sent)
    grad_all = team_gather(to_rel(cotangent[0]))

    team_device = me ^ jnp.array(plan.team_rel, jnp.int32)
    row_index = jnp.arange(rows, dtype=jnp.int32)
    positions = (
        ((team_device // space) % plan.clip * (space * rows) + (team_device % space) * rows)[:, None]
        + row_index[None, :]
    ).reshape(4 * rows)
    half_dim = HEAD // 2
    inverse_freq = jnp.exp(-jnp.log(10000.0) * jnp.arange(half_dim, dtype=f32) * 2.0 / HEAD)
    angles = positions.astype(f32)[:, None] * inverse_freq[None, :]
    angles = jnp.concatenate([angles, angles], axis=-1)
    cosine, sine = jnp.cos(angles), jnp.sin(angles)

    def rotate(value):
        turned = jnp.concatenate([-value[:, half_dim:], value[:, :half_dim]], axis=-1)
        return value * cosine + turned * sine

    def rotate_back(value):
        scaled = value * sine
        turned = jnp.concatenate([scaled[:, half_dim:], -scaled[:, :half_dim]], axis=-1)
        return value * cosine + turned

    def head_triples(mixed):
        found = []
        for j in range(2):
            q, k, v = (
                mixed[:, (2 * i + j) * HEAD : (2 * i + j + 1) * HEAD] for i in range(3)
            )
            found.append(jnp.concatenate([rotate(q), rotate(k), v], axis=1).astype(bf16))
        return found

    mixed_mine = matmul(first_all, qkv_mine)
    mixed_other = matmul(first_all, qkv_other)
    stack = jnp.stack(head_triples(mixed_mine) + head_triples(mixed_other))
    my_head = jnp.where(has(plan.heads[0]), 2, 0) + jnp.where(has(plan.heads[1]), 1, 0)
    core_flip = jnp.where(has(1), 2, 0)
    pick = [(my_head ^ r) ^ core_flip for r in range(4)]
    sent = [lax.dynamic_index_in_dim(stack, pick[r], 0, keepdims=False) for r in range(4)]
    own = jnp.stack([sent[0]] + [swap(sent[r], plan.head_rel[r]) for r in range(1, 4)])
    own = own.reshape(16, rows, 3 * HEAD)
    shared = own[:, :, HEAD:]
    other = jnp.stack([swap(shared, rel) for rel in plan.part_rel[1:]])

    block_rel = jnp.array(plan.block_rel, jnp.int32)
    tile_rel = jnp.array(plan.block_rel[::2], jnp.int32)
    tile_slot = (me ^ tile_rel) // space
    homes = me ^ block_rel
    place_in_square = jnp.zeros_like(homes)
    for i, bit in enumerate(reversed(plan.square_bits)):
        place_in_square = place_in_square + jnp.where((homes & bit) != 0, 1 << i, 0)
    info = jnp.concatenate(
        [
            jnp.stack([me, (me % space) * rows, ((me ^ team_lo) % space) * rows]),
            jnp.zeros((5,), jnp.int32),
            tile_slot,
            tile_slot // plan.clip * plan.clip,
            block_rel,
            place_in_square,
        ]
    ).astype(jnp.int32)

    attended, attended_t, log_total, keys, values = attend(plan, info, frame_real, own, other)
    square_bits = plan.square_bits
    by_head = [square_bits.index(b) for b in plan.team + plan.heads]
    heads_here = square(attended).reshape(2, 2, 2, 2, rows, HEAD)
    attended_low = heads_here.transpose(4, *by_head, 5).reshape(rows, width)
    middle = inputs + matmul(attended_low, out_matrix)
    normed_two, scale_two = layer_norm(middle)
    second_all = team_gather(to_rel(normed_two.astype(bf16)))

    def feed(up, down):
        hidden = matmul(second_all, up)
        grad_act = matmul(grad_all, down)
        activated, back = jax.vjp(functools.partial(jax.nn.gelu, approximate=True), hidden)
        return activated.astype(bf16), back(grad_act)[0].astype(bf16)

    act_mine, hid_mine = feed(up_mine, down_mine)
    act_other, hid_other = feed(up_other, down_other)
    second_parts = matmul(hid_mine, up_mine, ((1,), (1,))) + matmul(hid_other, up_other, ((1,), (1,)))
    grad_second = from_rel(team_scatter(second_parts.astype(bf16)))
    out_parts = matmul(act_mine, down_mine, ((1,), (1,))) + matmul(act_other, down_other, ((1,), (1,)))
    output = (middle + from_rel(team_scatter(out_parts.astype(bf16)))).astype(bf16)
    down_mine_grad = matmul(grad_all, act_mine, ((0,), (0,))).astype(bf16)
    down_other_grad = matmul(grad_all, act_other, ((0,), (0,))).astype(bf16)
    up_mine_grad = matmul(second_all, hid_mine, ((0,), (0,))).astype(bf16)
    up_other_grad = matmul(second_all, hid_other, ((0,), (0,))).astype(bf16)

    grad_middle = grad_out + layer_norm_back(grad_second, normed_two, scale_two)
    grad_middle_low = grad_middle.astype(bf16)
    grad_attended = matmul(grad_middle_low, out_matrix, ((1,), (1,))).astype(bf16)
    to_square = [0] * 4
    for i, axis in enumerate(by_head):
        to_square[axis] = i
    grad_sent = grad_attended.reshape(rows, 2, 2, 2, 2, HEAD).transpose(
        *[1 + i for i in to_square], 0, 5
    )
    grad_heads = square(grad_sent.reshape(16, rows, HEAD))
    dq, dkv_own, dkv_other = attend_back(
        plan, info, frame_real, own, keys, values, grad_heads, attended_t, log_total
    )
    dkv = dkv_own.astype(f32)
    for i, rel in enumerate(plan.part_rel[1:]):
        dkv = dkv + swap(dkv_other[i], rel).astype(f32)
    triple = jnp.concatenate([dq, dkv.astype(bf16)], axis=2).reshape(4, 4 * rows, 3 * HEAD)
    got = jnp.stack([triple[0]] + [swap(triple[r], plan.head_rel[r]) for r in range(1, 4)])

    def rejoin(first):
        pieces = [[], [], []]
        for j in range(2):
            place = ((first + j) ^ core_flip) ^ my_head
            t = lax.dynamic_index_in_dim(got, place, 0, keepdims=False).astype(f32)
            pieces[0].append(rotate_back(t[:, :HEAD]))
            pieces[1].append(rotate_back(t[:, HEAD : 2 * HEAD]))
            pieces[2].append(t[:, 2 * HEAD :])
        return jnp.concatenate(pieces[0] + pieces[1] + pieces[2], axis=1).astype(bf16)

    mixed_grad_mine, mixed_grad_other = rejoin(0), rejoin(2)
    first_parts = matmul(mixed_grad_mine, qkv_mine, ((1,), (1,))) + matmul(
        mixed_grad_other, qkv_other, ((1,), (1,))
    )
    grad_first = from_rel(team_scatter(first_parts.astype(bf16)))
    grad_inputs = grad_middle + layer_norm_back(grad_first, normed_one, scale_one)
    qkv_mine_grad = matmul(first_all, mixed_grad_mine, ((0,), (0,))).astype(bf16)
    qkv_other_grad = matmul(first_all, mixed_grad_other, ((0,), (0,))).astype(bf16)

    grad_down = collected(down_mine_grad, down_other_grad).transpose(1, 0, 2).reshape(shard, 8 * n_ff)
    raw_up = collected(up_mine_grad, up_other_grad).transpose(1, 0, 2).reshape(shard, 8 * n_ff)
    grad_w_out = lax.psum_scatter(
        matmul(attended_low, grad_middle_low, ((0,), (0,))).astype(bf16),
        AXES,
        scatter_dimension=0,
        tiled=True,
    ).astype(f32)
    raw_qkv = (
        collected(qkv_mine_grad, qkv_other_grad)
        .reshape(8, shard, 3, 2 * HEAD)
        .transpose(1, 2, 0, 3)
        .reshape(shard, 3 * width)
    )
    grad_gain_two = jnp.sum(raw_up * w_up.astype(f32), axis=1)
    grad_gain_one = jnp.sum(raw_qkv * w_qkv.astype(f32), axis=1)
    return (
        output[None],
        grad_inputs[None],
        grad_gain_one,
        raw_qkv * gain_one,
        grad_w_out,
        grad_gain_two,
        raw_up * gain_two,
        grad_down,
    )


def solution(mesh):
    plan = Plan(mesh.shape["tm"], mesh.shape["space"], BLOCK)
    tokens = P("tm", "space", None)
    line = P(("tm", "space"))
    table = P(("tm", "space"), None)
    return jax.shard_map(
        functools.partial(on_device, plan),
        mesh=mesh,
        in_specs=(tokens, P(), line, table, table, line, table, table, tokens),
        out_specs=(tokens, tokens, line, table, table, line, table, table),
        check_vma=False,
    )
```

```python
import functools

import jax
import jax.numpy as jnp
import numpy as np
from jax import lax
from jax.experimental import pallas as pl
from jax.experimental.pallas import tpu as pltpu
from jax.sharding import PartitionSpec as P

HEADS = 16
HEAD = 128
AXES = ("tm", "space")
BLOCK = 128

epsilon = 1e-05
masked_value = -1e30
inv_root = HEAD ** (-0.5)
to_log2 = inv_root * 1.4426950408889634

bf16 = jnp.bfloat16
f32 = jnp.float32


def matmul(left, right, dims=((1,), (0,))):
    return lax.dot_general(left, right, (dims, ((), ())), preferred_element_type=f32)


def tied(*values):
    return lax.optimization_barrier(values)


class Plan:
    def __init__(self, tm, space, frame_rows):
        self.count = tm * space
        self.space = space
        self.slots = tm
        self.clip = min(16, tm)
        count = self.count
        self.team = (count // 2, count // 16)
        self.heads = (count // 4, count // 8)
        self.feed_team = (count // 4, count // 16)
        bits = [1 << i for i in range(count.bit_length() - 1)]
        taken = set(self.team + self.heads)
        self.parts = [b for b in reversed(bits) if b not in taken]
        rest = [b for b in self.parts if b != 1]
        self.gather = [*self.heads, *rest]
        self.feed_gather = [count // 2, count // 8, *rest]
        self.team_rel = [0, self.team[1], self.team[0], self.team[0] | self.team[1]]
        self.head_rel = [0, self.heads[1], self.heads[0], self.heads[0] | self.heads[1]]
        self.block_rel = [h | t for h in self.head_rel for t in self.team_rel]
        self.part_rel = [
            sum(b for j, b in enumerate(self.parts) if (i >> j) & 1)
            for i in range(1 << len(self.parts))
        ]
        devices = range(count)
        self.octets = self.groups(sum(self.team) | 1)
        self.feed_octets = self.groups(sum(self.feed_team) | 1)
        self.tile_blocks = 2 if self.team[1] < space else 1
        self.devices = devices

    def groups(self, mask):
        held = {}
        for d in range(self.count):
            held.setdefault(d & ~mask, []).append(d)
        return list(held.values())

    def swap(self, value, mask):
        return lax.ppermute(value, AXES, [(d, d ^ mask) for d in self.devices])


def layer_norm(values):
    center = jnp.mean(values, axis=-1, keepdims=True)
    shifted = values - center
    spread = jnp.mean(shifted * shifted, axis=-1, keepdims=True)
    scale = lax.rsqrt(spread + epsilon)
    return shifted * scale, scale


def layer_norm_back(grads, normed, scale):
    inner = jnp.mean(grads * normed, axis=-1, keepdims=True)
    return (grads - jnp.mean(grads, axis=-1, keepdims=True) - normed * inner) * scale


def transposed(tile):
    return tile.astype(f32).T.astype(tile.dtype)


def attend_kernel(plan, info, real, own, other, out, out_t, lse, keys, values, values_t):
    me = info[0]
    n_blocks = len(plan.block_rel)
    for part, part_rel in enumerate(plan.part_rel):

        def place(b, _, part=part, part_rel=part_rel):
            home = me ^ part_rel ^ info[8 + b]
            if part == 0:
                key, value = own[b, :, HEAD : 2 * HEAD], own[b, :, 2 * HEAD :]
            else:
                key, value = other[part - 1, b, :, :HEAD], other[part - 1, b, :, HEAD:]
            rows = pl.ds(pl.multiple_of(home * BLOCK, BLOCK), BLOCK)
            keys[rows, :] = key
            values[rows, :] = value
            values_t[home] = transposed(value)
            return 0

        lax.fori_loop(0, n_blocks, place, 0)

    frame = plan.space * BLOCK
    per_tile = plan.tile_blocks
    two = per_tile * BLOCK
    lane = lax.broadcasted_iota(jnp.int32, (1, two), 1)
    q_place = jnp.where(lane < BLOCK, info[1] + lane, info[2] + lane - BLOCK)

    def tile(i, _):
        slot, first = info[24 + i], info[40 + i]
        q = jnp.concatenate([own[per_tile * i + j, :, :HEAD] for j in range(per_tile)], axis=0)

        def scores(g):
            key = keys[pl.ds(pl.multiple_of(g * frame, frame), frame), :]
            return matmul(key, q, ((1,), (1,)))

        def value_t(g):
            return jnp.concatenate(
                [values_t[g * plan.space + s] for s in range(plan.space)], axis=1
            )

        s = scores(slot)
        k_place = lax.broadcasted_iota(jnp.int32, (frame, two), 0)
        s = jnp.where(k_place <= q_place, s, masked_value)
        top = jnp.max(s, axis=0, keepdims=True)
        p = jnp.exp2((s - top) * to_log2)
        total = jnp.sum(p, axis=0, keepdims=True)
        acc = matmul(value_t(slot), p.astype(bf16))

        def step(g, carry):
            def use(carry):
                top, total, acc = carry
                s = scores(g)
                new = jnp.maximum(top, jnp.max(s, axis=0, keepdims=True))
                fade = jnp.exp2((top - new) * to_log2)
                p = jnp.exp2((s - new) * to_log2)
                total = total * fade + jnp.sum(p, axis=0, keepdims=True)
                acc = acc * fade + matmul(value_t(g), p.astype(bf16))
                return new, total, acc

            return lax.cond(real[g] > 0, use, lambda c: c, carry)

        first = jnp.where(real[slot] > 0, first, slot)
        top, total, acc = lax.fori_loop(first, slot, step, (top, total, acc))
        lse[i] = top * to_log2 + jnp.log2(total)
        acc = acc / total
        out_t[i] = acc
        back = acc.T.astype(bf16)
        for j in range(per_tile):
            out[per_tile * i + j] = back[j * BLOCK : (j + 1) * BLOCK]
        return 0

    lax.fori_loop(0, n_blocks // per_tile, tile, 0)


def attend_back_kernel(
    plan, info, real, own, keys, values, grads, out_t, lse, dq, dkv_own, dkv_other, dk, dv, keys_t
):
    me = info[0]
    n_blocks = len(plan.block_rel)

    def clear(b, _):
        rows = pl.ds(pl.multiple_of(b * BLOCK, BLOCK), BLOCK)
        dk[rows, :] = jnp.zeros((BLOCK, HEAD), f32)
        dv[rows, :] = jnp.zeros((BLOCK, HEAD), f32)
        keys_t[b] = transposed(keys[rows, :])
        return 0

    lax.fori_loop(0, plan.count, clear, 0)

    frame = plan.space * BLOCK
    per_tile = plan.tile_blocks
    two = per_tile * BLOCK
    lane = lax.broadcasted_iota(jnp.int32, (1, two), 1)
    q_place = jnp.where(lane < BLOCK, info[1] + lane, info[2] + lane - BLOCK)

    def tile(i, _):
        slot, first = info[24 + i], info[40 + i]
        q = jnp.concatenate([own[per_tile * i + j, :, :HEAD] for j in range(per_tile)], axis=0)
        do = jnp.concatenate([grads[per_tile * i + j] for j in range(per_tile)], axis=0)
        delta = jnp.sum(do.astype(f32).T * out_t[i], axis=0, keepdims=True)
        log_total = lse[i]

        def turn(g, mask):
            rows = pl.ds(pl.multiple_of(g * frame, frame), frame)
            key, value = keys[rows, :], values[rows, :]
            s = matmul(key, q, ((1,), (1,)))
            dp = matmul(value, do, ((1,), (1,)))
            p = jnp.exp2(s * to_log2 - log_total)
            if mask:
                k_place = lax.broadcasted_iota(jnp.int32, (frame, two), 0)
                p = jnp.where(k_place <= q_place, p, 0.0)
            ds = (p * (dp - delta)).astype(bf16)
            dv[rows, :] += matmul(p.astype(bf16), do)
            dk[rows, :] += matmul(ds, q)
            key_t = jnp.concatenate(
                [keys_t[g * plan.space + s] for s in range(plan.space)], axis=1
            )
            return matmul(key_t, ds)

        dq_t = turn(slot, True)

        def step(g, dq_t):
            return lax.cond(real[g] > 0, lambda c: c + turn(g, False), lambda c: c, dq_t)

        first = jnp.where(real[slot] > 0, first, slot)
        dq_t = lax.fori_loop(first, slot, step, dq_t)
        back = (dq_t * inv_root).T.astype(bf16)
        for j in range(per_tile):
            dq[per_tile * i + j] = back[j * BLOCK : (j + 1) * BLOCK]
        return 0

    lax.fori_loop(0, n_blocks // per_tile, tile, 0)

    for part, part_rel in enumerate(plan.part_rel):

        def hand_out(b, _, part=part, part_rel=part_rel):
            home = me ^ part_rel ^ info[8 + b]
            rows = pl.ds(pl.multiple_of(home * BLOCK, BLOCK), BLOCK)
            pair = jnp.concatenate([dk[rows, :] * inv_root, dv[rows, :]], axis=1).astype(bf16)
            if part == 0:
                dkv_own[b] = pair
            else:
                dkv_other[part - 1, b] = pair
            return 0

        lax.fori_loop(0, n_blocks, hand_out, 0)


def call(kernel, n_scalar, n_in, outs, scratch, cost):
    return pl.pallas_call(
        kernel,
        out_shape=outs,
        in_specs=[pl.BlockSpec(memory_space=pltpu.SMEM)] * n_scalar
        + [pl.BlockSpec(memory_space=pltpu.VMEM)] * n_in,
        out_specs=tuple(pl.BlockSpec(memory_space=pltpu.VMEM) for _ in outs),
        scratch_shapes=scratch,
        cost_estimate=cost,
        compiler_params=pltpu.CompilerParams(vmem_limit_bytes=50 << 20),
    )


def moving(n_bytes):
    return pl.CostEstimate(flops=n_bytes, bytes_accessed=n_bytes, transcendentals=0)


def arrange_kernel(normed, chunk, lanes, value, out, held):
    x = value[...].astype(f32)
    if normed:
        x = layer_norm(x)[0]
    held[...] = x.astype(bf16)
    for j in range(x.shape[1] // chunk):
        at = pl.multiple_of(lanes[j], chunk)
        out[:, j * chunk : (j + 1) * chunk] = held[:, pl.ds(at, chunk)]


def arrange(normed, chunk, lanes, value):
    shape = value.shape
    return call(
        functools.partial(arrange_kernel, normed, chunk),
        1,
        1,
        (jax.ShapeDtypeStruct(shape, bf16),),
        [pltpu.VMEM(shape, bf16)],
        moving(4 * value.size),
    )(lanes, value)[0]


def team_rows_kernel(a, b, a_lo, b_hi, a_far, b_far, out):
    one, two = a.shape[0], b.shape[0]
    pieces = (a[...], b[...], a_lo[...], b_far[:two], a_far[:one], b_hi[...], a_far[one:], b_far[two:])
    start = 0
    for piece in pieces:
        out[start : start + piece.shape[0]] = piece
        start += piece.shape[0]


def team_rows(*pieces):
    rows, width = pieces[0].shape[0] + pieces[1].shape[0], pieces[0].shape[1]
    return call(
        team_rows_kernel,
        0,
        6,
        (jax.ShapeDtypeStruct((4 * rows, width), bf16),),
        [],
        moving(16 * rows * width),
    )(*pieces)[0]


def turn_back_kernel(places, cosine, sine, *refs):
    heads, out = refs[:4], refs[4]
    half_dim = HEAD // 2
    cos, sin = cosine[...], sine[...]
    for r in range(4):
        found = []
        for i in range(2):
            t = heads[r][:, i * HEAD : (i + 1) * HEAD].astype(f32)
            scaled = t * sin
            turned = jnp.concatenate([scaled[:, half_dim:], -scaled[:, :half_dim]], axis=-1)
            found.append((t * cos + turned).astype(bf16))
        found.append(heads[r][:, 2 * HEAD :])
        whole = jnp.concatenate(found, axis=1)
        place = places[r]

        @pl.when(place % 2 == 0)
        def _():
            out[place // 2, :, : 3 * HEAD] = whole

        @pl.when(place % 2 == 1)
        def _():
            out[place // 2, :, 3 * HEAD :] = whole


def turn_back(places, cosine, sine, heads):
    rows = cosine.shape[0]
    return call(
        turn_back_kernel,
        1,
        6,
        (jax.ShapeDtypeStruct((2, rows, 6 * HEAD), bf16),),
        [],
        moving(8 * rows * 3 * HEAD * 2),
    )(places, cosine, sine, *heads)[0]


def deliver_kernel(columns, got, weight, gain, out, gain_grad):
    total = None
    for block, start, end, target in columns:
        value = got[block, :, start:end].astype(f32)
        span = slice(target, target + end - start)
        part = jnp.sum(value * weight[:, span].astype(f32), axis=1, keepdims=True)
        total = part if total is None else total + part
        out[:, span] = value * gain[...]
    gain_grad[...] = jnp.broadcast_to(total, gain_grad.shape)


def deliver(columns, got, weight, gain):
    rows, width = weight.shape
    return call(
        functools.partial(deliver_kernel, columns),
        0,
        3,
        (jax.ShapeDtypeStruct((rows, width), f32), jax.ShapeDtypeStruct((rows, 128), f32)),
        [],
        moving(8 * rows * width),
    )(got, weight, gain)


def attend(plan, info, real, own, other):
    blocks = len(plan.block_rel)
    tokens = plan.count * BLOCK
    work = blocks * BLOCK * min(plan.clip * plan.space * BLOCK, tokens) // 2
    shape = jax.ShapeDtypeStruct
    return call(
        functools.partial(attend_kernel, plan),
        2,
        2,
        (
            shape((blocks, BLOCK, HEAD), bf16),
            shape((blocks // plan.tile_blocks, HEAD, plan.tile_blocks * BLOCK), f32),
            shape((blocks // plan.tile_blocks, 1, plan.tile_blocks * BLOCK), f32),
            shape((tokens, HEAD), bf16),
            shape((tokens, HEAD), bf16),
        ),
        [pltpu.VMEM((plan.count, HEAD, BLOCK), bf16)],
        pl.CostEstimate(flops=8 * work * HEAD, bytes_accessed=8 << 20, transcendentals=work),
    )(info, real, own, other)


def attend_back(plan, info, real, own, keys, values, grads, out_t, lse):
    blocks = len(plan.block_rel)
    tokens = plan.count * BLOCK
    work = blocks * BLOCK * min(plan.clip * plan.space * BLOCK, tokens) // 2
    shape = jax.ShapeDtypeStruct
    return call(
        functools.partial(attend_back_kernel, plan),
        2,
        6,
        (
            shape((blocks, BLOCK, HEAD), bf16),
            shape((blocks, BLOCK, 2 * HEAD), bf16),
            shape((len(plan.part_rel) - 1, blocks, BLOCK, 2 * HEAD), bf16),
        ),
        [
            pltpu.VMEM((tokens, HEAD), f32),
            pltpu.VMEM((tokens, HEAD), f32),
            pltpu.VMEM((plan.count, HEAD, BLOCK), bf16),
        ],
        pl.CostEstimate(flops=20 * work * HEAD, bytes_accessed=8 << 20, transcendentals=work),
    )(info, real, own, keys, values, grads, out_t, lse)


def added(*values):
    return sum(v.astype(f32) for v in values).astype(bf16)


def quarters(value):
    return jnp.split(value, 4)


class Side:
    def __init__(self, plan, me, team, gather, groups, shard, width, rows, cut):
        self.plan, self.me, self.groups = plan, me, groups
        self.team_hi, self.team_lo = team
        self.gather, self.shard, self.cut = gather, shard, cut
        self.first, self.second = gather[:2]
        low = self.low = min(gather)
        self.chunk = low * shard
        self.n_chunks = width // self.chunk
        self.order = [
            (
                sum(b for j, b in enumerate(gather) if (i >> j) & 1)
                + (self.team_hi if hi else 0)
                + (self.team_lo if lo else 0)
            )
            // low
            for i in range(1 << len(gather))
            for hi in range(2)
            for lo in range(2 if self.team_lo > low else 1)
        ]
        self.inverse = [self.order.index(m) for m in range(self.n_chunks)]
        at = jnp.array(self.order, jnp.int32) ^ ((me & sum(gather)) // low)
        self.lanes = at * self.chunk

    def swap(self, value, bit):
        return self.plan.swap(value, bit)

    def flipped(self, pieces):
        for bit in self.gather:
            step = bit // self.low
            own = (self.me & bit) != 0
            pieces = [jnp.where(own, pieces[m ^ step], pieces[m]) for m in range(self.n_chunks)]
        return pieces

    def pieces(self, value):
        chunk = self.chunk
        return [value[:, m * chunk : (m + 1) * chunk] for m in range(self.n_chunks)]

    def to_rel(self, value, normed):
        if self.chunk % 128 == 0:
            return arrange(normed, self.chunk, self.lanes, value)
        value = layer_norm(value.astype(f32))[0] if normed else value
        pieces = self.flipped(self.pieces(value.astype(bf16)))
        return jnp.concatenate([pieces[m] for m in self.order], axis=1)

    def from_rel(self, value):
        pieces = self.pieces(value)
        return jnp.concatenate(self.flipped([pieces[m] for m in self.inverse]), axis=1)

    def gather_one(self, value):
        a, b = value[: self.cut], value[self.cut :]
        return a, b, self.swap(a, self.team_lo), self.swap(b, self.team_hi)

    def gather_two(self, a, b, a_lo, b_hi):
        return (
            self.swap(jnp.concatenate([a, a_lo]), self.team_hi),
            self.swap(jnp.concatenate([b, b_hi]), self.team_lo),
        )

    def scatter_one(self, parts):
        parts = parts.reshape(4, parts.shape[0] // 4, -1)
        a, b = parts[:, : self.cut], parts[:, self.cut :]
        a_got = self.swap(a[2:], self.team_hi)
        b_got = self.swap(jnp.stack([b[1], b[3]]), self.team_lo)
        return a[:2], jnp.stack([b[0], b[2]]), a_got, b_got

    def scatter_two(self, a, b, a_got, b_got):
        a_last = self.swap(added(a[1], a_got[1]), self.team_lo)
        b_last = self.swap(added(b[1], b_got[1]), self.team_hi)
        a_sum = a[0].astype(f32) + a_got[0].astype(f32) + a_last.astype(f32)
        b_sum = b[0].astype(f32) + b_got[0].astype(f32) + b_last.astype(f32)
        return jnp.concatenate([a_sum, b_sum])

    def octet(self, value):
        value = value.reshape(8, self.shard, -1)
        return lax.all_to_all(value, AXES, 0, 0, axis_index_groups=self.groups)

    def joined(self, *blocks):
        whole = jnp.concatenate(blocks)
        for bit in self.gather[2:]:
            whole = jnp.concatenate([whole, self.swap(whole, bit)])
        return whole

    def first_sum(self, mine, others_swapped):
        block = added(mine, others_swapped)
        for bit in reversed(self.gather[2:]):
            block = block.reshape(2, block.shape[0] // 2, -1)
            block = added(block[0], self.swap(block[1], bit))
        return block.reshape(4, 8 * self.shard, -1)


def on_device(
    plan, layer_input, frame_real, gain_attn, w_qkv, w_out, gain_mlp, w_up, w_down, cotangent
):
    rows = layer_input.shape[1]
    width = layer_input.shape[2]
    shard = w_up.shape[0]
    space = plan.space
    me = lax.axis_index("tm") * space + lax.axis_index("space")
    inputs = layer_input[0].astype(f32)
    grad_out = cotangent[0].astype(f32)
    swap = plan.swap
    attn = Side(plan, me, plan.team, plan.gather, plan.octets, shard, width, rows, rows * 3 // 8)
    feed = Side(
        plan, me, plan.feed_team, plan.feed_gather, plan.feed_octets, shard, width, rows, rows // 2
    )

    def has(bit):
        return (me & bit) != 0

    gain_one = gain_attn.astype(f32)[:, None]
    gain_two = gain_mlp.astype(f32)[:, None]
    qkv_scaled = (w_qkv.astype(f32) * gain_one).astype(bf16)
    up_scaled = (w_up.astype(f32) * gain_two).astype(bf16)
    n_ff = w_up.shape[1] // 8
    qkv_sent = (
        qkv_scaled.reshape(shard, 3, 2, 2, 2, 2, HEAD)
        .transpose(2, 5, 3, 0, 4, 1, 6)
        .reshape(8, shard, 6 * HEAD)
    )
    qkv_columns = [
        (
            4 * hi + 2 * lo + c,
            (3 * jj + i) * HEAD,
            (3 * jj + i + 1) * HEAD,
            (i * HEADS + 8 * hi + 4 * c + 2 * jj + lo) * HEAD,
        )
        for hi in range(2)
        for lo in range(2)
        for c in range(2)
        for jj in range(2)
        for i in range(3)
    ]
    ff_columns = [(b, 0, n_ff, b * n_ff) for b in range(8)]
    up_sent = up_scaled.reshape(shard, 8, n_ff).transpose(1, 0, 2)
    down_sent = w_down.reshape(shard, 8, n_ff).transpose(1, 0, 2)

    first_rel = attn.to_rel(layer_input[0], True)
    grad_rel = feed.to_rel(cotangent[0], False)
    qkv_block = attn.octet(qkv_sent).reshape(8 * shard, -1)
    qkv_block, first_rel, grad_rel, up_sent, down_sent = tied(
        qkv_block, first_rel, grad_rel, up_sent, down_sent
    )
    qkv_first = swap(qkv_block, attn.first)
    qkv_second = swap(qkv_block, attn.second)
    first_near = attn.gather_one(first_rel)
    qkv_first, qkv_second, first_near, up_sent = tied(qkv_first, qkv_second, first_near, up_sent)
    qkv_both = swap(qkv_first, attn.second)
    first_far = attn.gather_two(*first_near)
    up_block = feed.octet(up_sent).reshape(8 * shard, -1)
    qkv_both, first_far, up_block, down_sent, w_out = tied(
        qkv_both, first_far, up_block, down_sent, w_out
    )
    qkv_mine = attn.joined(qkv_block, qkv_first, qkv_second, qkv_both)
    qkv_other = swap(qkv_mine, 1)
    first_all = team_rows(*first_near, *first_far)
    up_rows = quarters(up_block)
    up_z = [swap(up_rows[i], feed.first) for i in (0, 1)]
    up_x = [swap(up_rows[i], feed.second) for i in (0, 1)]
    out_x = swap(w_out, attn.second)
    down_block = feed.octet(down_sent).reshape(8 * shard, -1)

    team_device = me ^ jnp.array(plan.team_rel, jnp.int32)
    row_index = jnp.arange(rows, dtype=jnp.int32)
    positions = (
        ((team_device // space) % plan.clip * (space * rows) + (team_device % space) * rows)[:, None]
        + row_index[None, :]
    ).reshape(4 * rows)
    half_dim = HEAD // 2
    inverse_freq = jnp.exp(-jnp.log(10000.0) * jnp.arange(half_dim, dtype=f32) * 2.0 / HEAD)
    angles = positions.astype(f32)[:, None] * inverse_freq[None, :]
    angles = jnp.concatenate([angles, angles], axis=-1)
    cosine, sine = jnp.cos(angles), jnp.sin(angles)

    def rotate(value):
        turned = jnp.concatenate([-value[:, half_dim:], value[:, :half_dim]], axis=-1)
        return value * cosine + turned * sine

    def rotate_back(value):
        scaled = value * sine
        turned = jnp.concatenate([scaled[:, half_dim:], -scaled[:, :half_dim]], axis=-1)
        return value * cosine + turned

    def head_triples(mixed):
        found = []
        for j in range(2):
            q, k, v = (
                mixed[:, (3 * j + i) * HEAD : (3 * j + i + 1) * HEAD] for i in range(3)
            )
            found.append(jnp.concatenate([rotate(q), rotate(k), v], axis=1).astype(bf16))
        return found

    mixed_mine = matmul(first_all, qkv_mine)
    mixed_other = matmul(first_all, qkv_other)
    stack = jnp.stack(head_triples(mixed_mine) + head_triples(mixed_other))
    my_head = jnp.where(has(plan.heads[0]), 2, 0) + jnp.where(has(plan.heads[1]), 1, 0)
    core_flip = jnp.where(has(1), 2, 0)
    pick = [(my_head ^ r) ^ core_flip for r in range(4)]
    sent = [lax.dynamic_index_in_dim(stack, pick[r], 0, keepdims=False) for r in range(4)]
    sent, up_z, up_x, out_x, down_block, up_rows = tied(
        sent, up_z, up_x, out_x, down_block, up_rows
    )
    got = [swap(sent[r], plan.head_rel[r]) for r in range(1, 4)]
    up_z += [swap(up_rows[i], feed.first) for i in (2, 3)]
    got, up_z, up_rows, down_block, grad_rel = tied(got, up_z, up_rows, down_block, grad_rel)
    down_rows = quarters(down_block)
    own = jnp.stack([sent[0]] + got).reshape(16, rows, 3 * HEAD)
    down_z = [swap(down_rows[i], feed.first) for i in (0, 1)]
    up_x += [swap(up_rows[i], feed.second) for i in (2, 3)]
    up_both = [swap(up_z[i], feed.second) for i in (0, 1)]
    grad_near = feed.gather_one(grad_rel)
    out_z = swap(jnp.stack([w_out, out_x]), attn.first)
    shared = own[:, :, HEAD:]
    other = jnp.stack([swap(shared, rel) for rel in plan.part_rel[1:]])

    block_rel = jnp.array(plan.block_rel, jnp.int32)
    tile_rel = jnp.array(plan.block_rel[:: plan.tile_blocks], jnp.int32)
    tile_slot = (me ^ tile_rel) // space
    no_more = jnp.zeros((16 - tile_slot.shape[0],), jnp.int32)
    info = jnp.concatenate(
        [
            jnp.stack([me, (me % space) * rows, ((me ^ plan.team[1]) % space) * rows]),
            jnp.zeros((5,), jnp.int32),
            block_rel,
            tile_slot,
            no_more,
            tile_slot // plan.clip * plan.clip,
            no_more,
        ]
    ).astype(jnp.int32)

    attended, attended_t, log_total, keys, values = attend(plan, info, frame_real, own, other)
    attended, down_z, up_x, up_both, grad_near, out_z, down_rows = tied(
        attended, down_z, up_x, up_both, grad_near, out_z, down_rows
    )
    attended = attended.reshape(4, 4 * rows, HEAD)
    heads_got = [swap(attended[r], plan.head_rel[r]) for r in range(1, 4)]
    down_z += [swap(down_rows[2], feed.first)]
    grad_far = feed.gather_two(*grad_near)
    w_team = jnp.stack([w_out, out_x, out_z[0], out_z[1]])
    for bit in reversed(plan.parts):
        w_got = swap(w_team, bit)
        w_team = jnp.where(
            has(bit),
            jnp.concatenate([w_got, w_team], axis=1),
            jnp.concatenate([w_team, w_got], axis=1),
        )
    w_team = w_team.reshape(4 * HEAD, width)
    heads_got, w_team, down_z, grad_far, up_z, down_rows = tied(
        heads_got, w_team, down_z, grad_far, up_z, down_rows
    )
    attended_team = jnp.concatenate([attended[0]] + heads_got, axis=1)
    branch = matmul(attended_team, w_team).astype(bf16)
    branch_near = attn.scatter_one(branch)
    up_both += [swap(up_z[i], feed.second) for i in (2, 3)]
    down_x = [swap(down_rows[i], feed.second) for i in (0, 1)]
    grad_all = team_rows(*grad_near, *grad_far)
    branch_near, up_both, down_x, grad_all, down_rows, down_z = tied(
        branch_near, up_both, down_x, grad_all, down_rows, down_z
    )
    middle = attn.scatter_two(*branch_near)
    down_x += [swap(down_rows[i], feed.second) for i in (2, 3)]
    up_mine = feed.joined(up_block, *up_z, *up_x, *up_both)
    middle, down_x, up_mine, down_rows, down_z = tied(middle, down_x, up_mine, down_rows, down_z)
    middle = inputs + middle
    second_near = feed.gather_one(feed.to_rel(middle, True))
    down_z += [swap(down_rows[3], feed.first)]
    down_both = [swap(down_z[0], feed.second)]
    up_other = swap(up_mine, 1)
    second_near, down_z, down_both, up_other = tied(second_near, down_z, down_both, up_other)
    second_far = feed.gather_two(*second_near)
    down_both += [swap(down_z[i], feed.second) for i in (1, 2, 3)]
    second_far, down_both = tied(second_far, down_both)
    second_all = team_rows(*second_near, *second_far)
    normed_two, scale_two = layer_norm(middle)
    down_mine = feed.joined(down_block, *down_z, *down_x, *down_both)
    down_other = swap(down_mine, 1)
    gelu = functools.partial(jax.nn.gelu, approximate=True)
    hidden_other = matmul(second_all, up_other)
    hidden_mine = matmul(second_all, up_mine)
    act_other = gelu(hidden_other).astype(bf16)
    act_mine = gelu(hidden_mine).astype(bf16)
    down_other_grad = matmul(grad_all, act_other, ((0,), (0,))).astype(bf16)
    down_other_grad, down_other, down_mine, act_mine, act_other = tied(
        down_other_grad, down_other, down_mine, act_mine, act_other
    )
    down_swapped = swap(down_other_grad, 1)
    down_mine_grad = matmul(grad_all, act_mine, ((0,), (0,))).astype(bf16)

    def back(hidden, down):
        return jax.vjp(gelu, hidden)[1](matmul(grad_all, down))[0].astype(bf16)

    hid_mine, hid_other = back(hidden_mine, down_mine), back(hidden_other, down_other)
    second_parts = matmul(hid_mine, up_mine, ((1,), (1,))) + matmul(hid_other, up_other, ((1,), (1,)))
    second_parts, hid_mine, hid_other, down_swapped, down_mine_grad = tied(
        second_parts.astype(bf16), hid_mine, hid_other, down_swapped, down_mine_grad
    )
    second_back = feed.scatter_one(second_parts)
    down_sum = feed.first_sum(down_mine_grad, down_swapped)
    down_sum = [quarters(part) for part in down_sum]
    down_x3 = [swap(down_sum[3][i], feed.second) for i in (0, 1)]
    second_back, down_x3, down_sum = tied(second_back, down_x3, down_sum)
    grad_second = feed.scatter_two(*second_back)
    down_x3 += [swap(down_sum[3][2], feed.second)]
    down_z1 = [swap(added(down_sum[1][0], down_x3[0]), feed.first)]
    grad_second, down_x3, down_z1, down_sum = tied(grad_second, down_x3, down_z1, down_sum)
    grad_second = feed.from_rel(grad_second)
    grad_middle = grad_out + layer_norm_back(grad_second, normed_two, scale_two)
    middle_near = attn.gather_one(grad_middle.astype(bf16))
    down_x3 += [swap(down_sum[3][3], feed.second)]
    down_x2 = [swap(down_sum[2][0], feed.second)]
    out_parts = (
        matmul(act_mine, down_mine, ((1,), (1,))) + matmul(act_other, down_other, ((1,), (1,)))
    ).astype(bf16)
    middle_near, down_x3, down_x2, down_sum, out_parts, hid_other, hid_mine = tied(
        middle_near, down_x3, down_x2, down_sum, out_parts, hid_other, hid_mine
    )
    middle_far = attn.gather_two(*middle_near)
    down_x2 += [swap(down_sum[2][i], feed.second) for i in (1, 2, 3)]
    up_other_grad = matmul(second_all, hid_other, ((0,), (0,))).astype(bf16)
    up_mine_grad = matmul(second_all, hid_mine, ((0,), (0,))).astype(bf16)
    middle_far, down_x2, up_other_grad, up_mine_grad, down_sum, down_x3 = tied(
        middle_far, down_x2, up_other_grad, up_mine_grad, down_sum, down_x3
    )
    middle_all = team_rows(*middle_near, *middle_far)
    grad_heads = matmul(middle_all, w_team, ((1,), (1,))).astype(bf16)
    grad_own = grad_heads[:, :HEAD]
    grad_got = [
        swap(grad_heads[:, r * HEAD : (r + 1) * HEAD], plan.head_rel[r]) for r in range(1, 4)
    ]
    up_swapped = swap(up_other_grad, 1)
    down_z1 += [swap(added(down_sum[1][1], down_x3[1]), feed.first)]
    out_grad = matmul(attended_team, middle_all, ((0,), (0,))).astype(bf16).reshape(4, HEAD, width)
    up_sum = feed.first_sum(up_mine_grad, up_swapped)
    up_sum = [quarters(part) for part in up_sum]
    grad_got, up_sum, down_z1, out_grad, down_sum, down_x3 = tied(
        grad_got, up_sum, down_z1, out_grad, down_sum, down_x3
    )
    up_x3 = [swap(up_sum[3][i], feed.second) for i in range(4)]
    down_z1 += [swap(added(down_sum[1][i], down_x3[i]), feed.first) for i in (2, 3)]
    out_near = feed.scatter_one(out_parts)
    for bit in plan.parts:
        lower, upper = jnp.split(out_grad, 2, axis=1)
        kept = jnp.where(has(bit), upper, lower)
        out_grad = added(kept, swap(jnp.where(has(bit), lower, upper), bit))
    dq, dkv_own, dkv_other = attend_back(
        plan,
        info,
        frame_real,
        own,
        keys,
        values,
        jnp.stack([grad_own] + grad_got).reshape(16, rows, HEAD),
        attended_t,
        log_total,
    )
    dq, dkv_own, dkv_other, up_x3, down_z1, out_near, out_grad = tied(
        dq, dkv_own, dkv_other, up_x3, down_z1, out_near, out_grad
    )
    dkv = dkv_own.astype(f32)
    for i, rel in enumerate(plan.part_rel[1:]):
        dkv = dkv + swap(dkv_other[i], rel).astype(f32)
    triple = jnp.concatenate([dq, dkv.astype(bf16)], axis=2).reshape(4, 4 * rows, 3 * HEAD)
    triple, up_sum, up_x3, down_z1 = tied(triple, up_sum, up_x3, down_z1)
    got = [swap(triple[r], plan.head_rel[r]) for r in range(1, 4)]
    up_z1 = [swap(added(up_sum[1][i], up_x3[i]), feed.first) for i in (0, 1)]
    down_done = jnp.concatenate(
        [added(down_sum[0][i], down_x2[i], down_z1[i]) for i in range(4)]
    )
    got, up_z1, down_done, up_sum, up_x3, out_near, out_grad = tied(
        got, up_z1, down_done, up_sum, up_x3, out_near, out_grad
    )
    places = (my_head ^ jnp.arange(4, dtype=jnp.int32)) ^ core_flip
    mixed_grad = turn_back(places, cosine, sine, [triple[0]] + got)
    mixed_grad_mine, mixed_grad_other = mixed_grad[0], mixed_grad[1]
    qkv_other_grad = matmul(first_all, mixed_grad_other, ((0,), (0,))).astype(bf16)
    up_x2 = [swap(up_sum[2][i], feed.second) for i in (0, 1)]
    up_z1 += [swap(added(up_sum[1][2], up_x3[2]), feed.first)]
    out_sum = feed.scatter_two(*out_near)
    out_grad = added(out_grad[:2], swap(out_grad[2:], attn.first))
    qkv_other_grad, mixed_grad_mine, up_x2, up_z1, out_sum, out_grad, up_sum, down_done = tied(
        qkv_other_grad, mixed_grad_mine, up_x2, up_z1, out_sum, out_grad, up_sum, down_done
    )
    qkv_swapped = swap(qkv_other_grad, 1)
    qkv_mine_grad = matmul(first_all, mixed_grad_mine, ((0,), (0,))).astype(bf16)
    first_parts = matmul(mixed_grad_mine, qkv_mine, ((1,), (1,))) + matmul(
        mixed_grad_other, qkv_other, ((1,), (1,))
    )
    up_x2 += [swap(up_sum[2][i], feed.second) for i in (2, 3)]
    up_z1 += [swap(added(up_sum[1][3], up_x3[3]), feed.first)]
    down_got = feed.octet(down_done)
    qkv_sum = attn.first_sum(qkv_mine_grad, qkv_swapped)
    qkv_sum, first_parts, up_x2, up_z1, down_got, up_sum = tied(
        qkv_sum, first_parts.astype(bf16), up_x2, up_z1, down_got, up_sum
    )
    qkv_x3 = swap(qkv_sum[3], attn.second)
    first_back = attn.scatter_one(first_parts)
    up_done = jnp.concatenate([added(up_sum[0][i], up_x2[i], up_z1[i]) for i in range(4)])
    up_got = feed.octet(up_done)
    output = (middle + feed.from_rel(out_sum)).astype(bf16)
    qkv_x3, first_back, up_got, qkv_sum, out_grad, output = tied(
        qkv_x3, first_back, up_got, qkv_sum, out_grad, output
    )
    qkv_z1 = swap(added(qkv_sum[1], qkv_x3), attn.first)
    qkv_x2 = swap(qkv_sum[2], attn.second)
    first_rows = attn.scatter_two(*first_back)
    grad_down = down_got.transpose(1, 0, 2).reshape(shard, 8 * n_ff).astype(f32)
    grad_up, grad_gain_two = deliver(ff_columns, up_got, w_up, gain_two)
    qkv_z1, qkv_x2, first_rows, grad_down, grad_up, out_grad = tied(
        qkv_z1, qkv_x2, first_rows, grad_down, grad_up, out_grad
    )
    qkv_got = attn.octet(added(qkv_sum[0], qkv_x2, qkv_z1))
    grad_first = attn.from_rel(first_rows)
    grad_inputs = grad_middle + layer_norm_back(grad_first, *layer_norm(inputs))
    out_grad = out_grad[0].astype(f32) + swap(out_grad[1], attn.second).astype(f32)
    grad_qkv, grad_gain_one = deliver(qkv_columns, qkv_got, w_qkv, gain_one)
    return (
        output[None],
        grad_inputs[None],
        grad_gain_one[:, 0],
        grad_qkv,
        out_grad,
        grad_gain_two[:, 0],
        grad_up,
        grad_down,
    )


def solution(mesh):
    plan = Plan(mesh.shape["tm"], mesh.shape["space"], BLOCK)
    tokens = P("tm", "space", None)
    line = P(("tm", "space"))
    table = P(("tm", "space"), None)
    return jax.shard_map(
        functools.partial(on_device, plan),
        mesh=mesh,
        in_specs=(tokens, P(), line, table, table, line, table, table, tokens),
        out_specs=(tokens, tokens, line, table, table, line, table, table),
        check_vma=False,
    )
```

```python
import functools

import jax
import jax.numpy as jnp
import numpy as np
from jax import lax
from jax.experimental import pallas as pl
from jax.experimental.pallas import tpu as pltpu
from jax.sharding import PartitionSpec as P

HEADS = 16
HEAD = 128
AXES = ("tm", "space")
BLOCK = 128

epsilon = 1e-05
masked_value = -1e30
inv_root = HEAD ** (-0.5)
to_log2 = inv_root * 1.4426950408889634
q_unscale = inv_root / to_log2

bf16 = jnp.bfloat16
f32 = jnp.float32


def matmul(left, right, dims=((1,), (0,))):
    return lax.dot_general(left, right, (dims, ((), ())), preferred_element_type=f32)


def tied(*values):
    return lax.optimization_barrier(values)


class Plan:
    def __init__(self, tm, space, frame_rows):
        self.count = tm * space
        self.space = space
        self.slots = tm
        self.clip = min(16, tm)
        count = self.count
        self.team = (count // 2, count // 16)
        self.heads = (count // 4, count // 8)
        self.feed_team = (count // 4, count // 16)
        bits = [1 << i for i in range(count.bit_length() - 1)]
        taken = set(self.team + self.heads)
        self.parts = [b for b in reversed(bits) if b not in taken]
        rest = [b for b in self.parts if b != 1]
        self.gather = [*self.heads, *rest]
        self.feed_gather = [count // 2, count // 8, *rest]
        self.team_rel = [0, self.team[1], self.team[0], self.team[0] | self.team[1]]
        self.head_rel = [0, self.heads[1], self.heads[0], self.heads[0] | self.heads[1]]
        self.block_rel = [h | t for h in self.head_rel for t in self.team_rel]
        self.part_rel = [
            sum(b for j, b in enumerate(self.parts) if (i >> j) & 1)
            for i in range(1 << len(self.parts))
        ]
        devices = range(count)
        self.octets = self.groups(sum(self.team) | 1)
        self.feed_octets = self.groups(sum(self.feed_team) | 1)
        self.tile_blocks = 2 if self.team[1] < space else 1
        self.devices = devices

    def groups(self, mask):
        held = {}
        for d in range(self.count):
            held.setdefault(d & ~mask, []).append(d)
        return list(held.values())

    def swap(self, value, mask):
        return lax.ppermute(value, AXES, [(d, d ^ mask) for d in self.devices])


def layer_norm(values):
    center = jnp.mean(values, axis=-1, keepdims=True)
    shifted = values - center
    spread = jnp.mean(shifted * shifted, axis=-1, keepdims=True)
    scale = lax.rsqrt(spread + epsilon)
    return shifted * scale, scale


def layer_norm_back(grads, normed, scale):
    inner = jnp.mean(grads * normed, axis=-1, keepdims=True)
    return (grads - jnp.mean(grads, axis=-1, keepdims=True) - normed * inner) * scale


def transposed(tile):
    return tile.astype(f32).T.astype(tile.dtype)


def attend_kernel(plan, info, real, own, other, out, out_t, lse, keys, values, values_t):
    me = info[0]
    n_blocks = len(plan.block_rel)
    for part, part_rel in enumerate(plan.part_rel):

        def place(b, _, part=part, part_rel=part_rel):
            home = me ^ part_rel ^ info[8 + b]
            if part == 0:
                key, value = own[b, :, HEAD : 2 * HEAD], own[b, :, 2 * HEAD :]
            else:
                key, value = other[part - 1, b, :, :HEAD], other[part - 1, b, :, HEAD:]
            rows = pl.ds(pl.multiple_of(home * BLOCK, BLOCK), BLOCK)
            keys[rows, :] = key
            values[rows, :] = value
            values_t[home] = transposed(value)
            return 0

        lax.fori_loop(0, n_blocks, place, 0, unroll=4)

    frame = plan.space * BLOCK
    per_tile = plan.tile_blocks
    two = per_tile * BLOCK
    lane = lax.broadcasted_iota(jnp.int32, (1, two), 1)
    q_place = jnp.where(lane < BLOCK, info[1] + lane, info[2] + lane - BLOCK)

    def tile(i, _):
        slot, first = info[24 + i], info[40 + i]
        q = jnp.concatenate([own[per_tile * i + j, :, :HEAD] for j in range(per_tile)], axis=0)

        def scores(g):
            key = keys[pl.ds(pl.multiple_of(g * frame, frame), frame), :]
            return matmul(key, q, ((1,), (1,)))

        def value_t(g):
            return jnp.concatenate(
                [values_t[g * plan.space + s] for s in range(plan.space)], axis=1
            )

        def fold(carry, s, g):
            top, total, acc = carry
            new = jnp.maximum(top, jnp.max(s, axis=0, keepdims=True))
            fade = jnp.exp2(top - new)
            p = jnp.exp2(s - new)
            total = total * fade + jnp.sum(p, axis=0, keepdims=True)
            acc = acc * fade + matmul(value_t(g), p.astype(bf16))
            return new, total, acc

        def step(g, carry):
            ahead = scores(g + 1)
            s = carry[3] + jnp.where(real[g] > 0, 0.0, masked_value)
            return (*fold(carry[:3], s, g), ahead)

        first = jnp.where(real[slot] > 0, first, slot)
        start = (
            jnp.full((1, two), masked_value, f32),
            jnp.zeros((1, two), f32),
            jnp.zeros((HEAD, two), f32),
            scores(first),
        )
        *carry, s = lax.fori_loop(first, slot, step, start)
        k_place = lax.broadcasted_iota(jnp.int32, (frame, two), 0)
        top, total, acc = fold(carry, jnp.where(k_place <= q_place, s, masked_value), slot)
        lse[i] = top + jnp.log2(total)
        acc = acc / total
        out_t[i] = acc
        back = acc.T.astype(bf16)
        for j in range(per_tile):
            out[per_tile * i + j] = back[j * BLOCK : (j + 1) * BLOCK]
        return 0

    lax.fori_loop(0, n_blocks // per_tile, tile, 0)


def attend_back_kernel(
    plan, info, real, own, keys, values, grads, out_t, lse, dq, dkv_own, dkv_other, dk, dv, keys_t
):
    me = info[0]
    n_blocks = len(plan.block_rel)

    def clear(b, _):
        rows = pl.ds(pl.multiple_of(b * BLOCK, BLOCK), BLOCK)
        dk[rows, :] = jnp.zeros((BLOCK, HEAD), f32)
        dv[rows, :] = jnp.zeros((BLOCK, HEAD), f32)
        keys_t[b] = transposed(keys[rows, :])
        return 0

    lax.fori_loop(0, plan.count, clear, 0, unroll=4)

    frame = plan.space * BLOCK
    per_tile = plan.tile_blocks
    two = per_tile * BLOCK
    lane = lax.broadcasted_iota(jnp.int32, (1, two), 1)
    q_place = jnp.where(lane < BLOCK, info[1] + lane, info[2] + lane - BLOCK)

    def tile(i, _):
        slot, first = info[24 + i], info[40 + i]
        q = jnp.concatenate([own[per_tile * i + j, :, :HEAD] for j in range(per_tile)], axis=0)
        do = jnp.concatenate([grads[per_tile * i + j] for j in range(per_tile)], axis=0)
        delta = jnp.sum(do.astype(f32).T * out_t[i], axis=0, keepdims=True)
        log_total = lse[i]

        def turn(g, mask):
            rows = pl.ds(pl.multiple_of(g * frame, frame), frame)
            key, value = keys[rows, :], values[rows, :]
            s = matmul(key, q, ((1,), (1,)))
            dp = matmul(value, do, ((1,), (1,)))
            if mask:
                p = jnp.exp2(s - log_total)
            else:
                p = jnp.exp2(s - jnp.where(real[g] > 0, log_total, -masked_value))
            if mask:
                k_place = lax.broadcasted_iota(jnp.int32, (frame, two), 0)
                p = jnp.where(k_place <= q_place, p, 0.0)
            ds = (p * (dp - delta)).astype(bf16)
            dv[rows, :] += matmul(p.astype(bf16), do)
            dk[rows, :] += matmul(ds, q)
            key_t = jnp.concatenate(
                [keys_t[g * plan.space + s] for s in range(plan.space)], axis=1
            )
            return matmul(key_t, ds)

        def step(g, dq_t):
            return dq_t + turn(g, False)

        first = jnp.where(real[slot] > 0, first, slot)
        dq_t = lax.fori_loop(first, slot, step, turn(slot, True))
        back = (dq_t * inv_root).T.astype(bf16)
        for j in range(per_tile):
            dq[per_tile * i + j] = back[j * BLOCK : (j + 1) * BLOCK]
        return 0

    lax.fori_loop(0, n_blocks // per_tile, tile, 0)

    for part, part_rel in enumerate(plan.part_rel):

        def hand_out(b, _, part=part, part_rel=part_rel):
            home = me ^ part_rel ^ info[8 + b]
            rows = pl.ds(pl.multiple_of(home * BLOCK, BLOCK), BLOCK)
            pair = jnp.concatenate([dk[rows, :] * q_unscale, dv[rows, :]], axis=1).astype(bf16)
            if part == 0:
                dkv_own[b] = pair
            else:
                dkv_other[part - 1, b] = pair
            return 0

        lax.fori_loop(0, n_blocks, hand_out, 0, unroll=4)


def call(kernel, n_scalar, n_in, outs, scratch, cost, room=16):
    return pl.pallas_call(
        kernel,
        out_shape=outs,
        in_specs=[pl.BlockSpec(memory_space=pltpu.SMEM)] * n_scalar
        + [pl.BlockSpec(memory_space=pltpu.VMEM)] * n_in,
        out_specs=tuple(pl.BlockSpec(memory_space=pltpu.VMEM) for _ in outs),
        scratch_shapes=scratch,
        cost_estimate=cost,
        compiler_params=pltpu.CompilerParams(vmem_limit_bytes=room << 20),
    )


def moving(n_bytes):
    return pl.CostEstimate(flops=n_bytes, bytes_accessed=n_bytes, transcendentals=0)


def arrange_kernel(normed, chunk, lanes, value, out, held):
    x = value[...].astype(f32)
    if normed:
        x = layer_norm(x)[0]
    held[...] = x.astype(bf16)
    for j in range(x.shape[1] // chunk):
        at = pl.multiple_of(lanes[j], chunk)
        out[:, j * chunk : (j + 1) * chunk] = held[:, pl.ds(at, chunk)]


def arrange(normed, chunk, lanes, value):
    shape = value.shape
    return call(
        functools.partial(arrange_kernel, normed, chunk),
        1,
        1,
        (jax.ShapeDtypeStruct(shape, bf16),),
        [pltpu.VMEM(shape, bf16)],
        moving(4 * value.size),
    )(lanes, value)[0]


def team_rows_kernel(a, b, a_lo, b_hi, a_far, b_far, out):
    one, two = a.shape[0], b.shape[0]
    pieces = (a[...], b[...], a_lo[...], b_far[:two], a_far[:one], b_hi[...], a_far[one:], b_far[two:])
    start = 0
    for piece in pieces:
        out[start : start + piece.shape[0]] = piece
        start += piece.shape[0]


def team_rows(*pieces):
    rows, width = pieces[0].shape[0] + pieces[1].shape[0], pieces[0].shape[1]
    return call(
        team_rows_kernel,
        0,
        6,
        (jax.ShapeDtypeStruct((4 * rows, width), bf16),),
        [],
        moving(16 * rows * width),
    )(*pieces)[0]


def turn_back_kernel(places, cosine, sine, *refs):
    heads, out = refs[:4], refs[4]
    half_dim = HEAD // 2
    cos, sin = cosine[...], sine[...]
    for r in range(4):
        found = []
        for i in range(2):
            t = heads[r][:, i * HEAD : (i + 1) * HEAD].astype(f32)
            scaled = t * sin
            turned = jnp.concatenate([scaled[:, half_dim:], -scaled[:, :half_dim]], axis=-1)
            found.append((t * cos + turned).astype(bf16))
        found.append(heads[r][:, 2 * HEAD :])
        whole = jnp.concatenate(found, axis=1)
        place = places[r]

        @pl.when(place % 2 == 0)
        def _():
            out[place // 2, :, : 3 * HEAD] = whole

        @pl.when(place % 2 == 1)
        def _():
            out[place // 2, :, 3 * HEAD :] = whole


def turn_back(places, cosine, sine, heads):
    rows = cosine.shape[0]
    return call(
        turn_back_kernel,
        1,
        6,
        (jax.ShapeDtypeStruct((2, rows, 6 * HEAD), bf16),),
        [],
        moving(8 * rows * 3 * HEAD * 2),
    )(places, cosine, sine, *heads)[0]


def deliver_kernel(columns, got, weight, gain, out, gain_grad):
    total = None
    for block, start, end, target in columns:
        value = got[block, :, start:end].astype(f32)
        span = slice(target, target + end - start)
        part = jnp.sum(value * weight[:, span].astype(f32), axis=1, keepdims=True)
        total = part if total is None else total + part
        out[:, span] = value * gain[...]
    gain_grad[...] = jnp.broadcast_to(total, gain_grad.shape)


def deliver(columns, got, weight, gain):
    rows, width = weight.shape
    return call(
        functools.partial(deliver_kernel, columns),
        0,
        3,
        (jax.ShapeDtypeStruct((rows, width), f32), jax.ShapeDtypeStruct((rows, 128), f32)),
        [],
        moving(8 * rows * width),
    )(got, weight, gain)


def attend(plan, info, real, own, other):
    blocks = len(plan.block_rel)
    tokens = plan.count * BLOCK
    work = blocks * BLOCK * min(plan.clip * plan.space * BLOCK, tokens) // 2
    shape = jax.ShapeDtypeStruct
    return call(
        functools.partial(attend_kernel, plan),
        2,
        2,
        (
            shape((blocks, BLOCK, HEAD), bf16),
            shape((blocks // plan.tile_blocks, HEAD, plan.tile_blocks * BLOCK), f32),
            shape((blocks // plan.tile_blocks, 1, plan.tile_blocks * BLOCK), f32),
            shape((tokens, HEAD), bf16),
            shape((tokens, HEAD), bf16),
        ),
        [pltpu.VMEM((plan.count, HEAD, BLOCK), bf16)],
        pl.CostEstimate(flops=8 * work * HEAD, bytes_accessed=8 << 20, transcendentals=work),
        min(56, 8 + plan.count * 3 // 4),
    )(info, real, own, other)


def attend_back(plan, info, real, own, keys, values, grads, out_t, lse):
    blocks = len(plan.block_rel)
    tokens = plan.count * BLOCK
    work = blocks * BLOCK * min(plan.clip * plan.space * BLOCK, tokens) // 2
    shape = jax.ShapeDtypeStruct
    return call(
        functools.partial(attend_back_kernel, plan),
        2,
        6,
        (
            shape((blocks, BLOCK, HEAD), bf16),
            shape((blocks, BLOCK, 2 * HEAD), bf16),
            shape((len(plan.part_rel) - 1, blocks, BLOCK, 2 * HEAD), bf16),
        ),
        [
            pltpu.VMEM((tokens, HEAD), f32),
            pltpu.VMEM((tokens, HEAD), f32),
            pltpu.VMEM((plan.count, HEAD, BLOCK), bf16),
        ],
        pl.CostEstimate(flops=20 * work * HEAD, bytes_accessed=8 << 20, transcendentals=work),
        min(56, 8 + plan.count * 3 // 4),
    )(info, real, own, keys, values, grads, out_t, lse)


def added(*values):
    return sum(v.astype(f32) for v in values).astype(bf16)


class Side:
    def __init__(self, plan, me, team, gather, groups, shard, width, rows, cut):
        self.plan, self.me, self.groups = plan, me, groups
        self.team_hi, self.team_lo = team
        self.gather, self.shard, self.cut = gather, shard, cut
        self.first, self.second = gather[:2]
        low = self.low = min(gather)
        self.chunk = low * shard
        self.n_chunks = width // self.chunk
        self.order = [
            (
                sum(b for j, b in enumerate(gather) if (i >> j) & 1)
                + (self.team_hi if hi else 0)
                + (self.team_lo if lo else 0)
            )
            // low
            for i in range(1 << len(gather))
            for hi in range(2)
            for lo in range(2 if self.team_lo > low else 1)
        ]
        self.inverse = [self.order.index(m) for m in range(self.n_chunks)]
        at = jnp.array(self.order, jnp.int32) ^ ((me & sum(gather)) // low)
        self.lanes = at * self.chunk

    def swap(self, value, bit):
        return self.plan.swap(value, bit)

    def flipped(self, pieces):
        for bit in self.gather:
            step = bit // self.low
            own = (self.me & bit) != 0
            pieces = [jnp.where(own, pieces[m ^ step], pieces[m]) for m in range(self.n_chunks)]
        return pieces

    def pieces(self, value):
        chunk = self.chunk
        return [value[:, m * chunk : (m + 1) * chunk] for m in range(self.n_chunks)]

    def to_rel(self, value, normed):
        if self.chunk % 128 == 0:
            return arrange(normed, self.chunk, self.lanes, value)
        value = layer_norm(value.astype(f32))[0] if normed else value
        pieces = self.flipped(self.pieces(value.astype(bf16)))
        return jnp.concatenate([pieces[m] for m in self.order], axis=1)

    def from_rel(self, value):
        pieces = self.pieces(value)
        return jnp.concatenate(self.flipped([pieces[m] for m in self.inverse]), axis=1)

    def gather_one(self, value):
        a, b = value[: self.cut], value[self.cut :]
        return a, b, self.swap(a, self.team_lo), self.swap(b, self.team_hi)

    def gather_two(self, a, b, a_lo, b_hi):
        return (
            self.swap(jnp.concatenate([a, a_lo]), self.team_hi),
            self.swap(jnp.concatenate([b, b_hi]), self.team_lo),
        )

    def scatter_one(self, parts):
        parts = parts.reshape(4, parts.shape[0] // 4, -1)
        a, b = parts[:, : self.cut], parts[:, self.cut :]
        a_got = self.swap(a[2:], self.team_hi)
        b_got = self.swap(jnp.stack([b[1], b[3]]), self.team_lo)
        return a[:2], jnp.stack([b[0], b[2]]), a_got, b_got

    def scatter_two(self, a, b, a_got, b_got):
        a_last = self.swap(added(a[1], a_got[1]), self.team_lo)
        b_last = self.swap(added(b[1], b_got[1]), self.team_hi)
        a_sum = a[0].astype(f32) + a_got[0].astype(f32) + a_last.astype(f32)
        b_sum = b[0].astype(f32) + b_got[0].astype(f32) + b_last.astype(f32)
        return jnp.concatenate([a_sum, b_sum])

    def octet(self, value):
        value = value.reshape(8, self.shard, -1)
        return lax.all_to_all(value, AXES, 0, 0, axis_index_groups=self.groups)

    def joined(self, *blocks):
        whole = jnp.concatenate(blocks)
        for bit in self.gather[2:]:
            whole = jnp.concatenate([whole, self.swap(whole, bit)])
        return whole

    def first_sum(self, mine, others_swapped):
        block = added(mine, others_swapped)
        for bit in reversed(self.gather[2:]):
            block = block.reshape(2, block.shape[0] // 2, -1)
            block = added(block[0], self.swap(block[1], bit))
        return block.reshape(4, 8 * self.shard, -1)


def on_device(
    plan, layer_input, frame_real, gain_attn, w_qkv, w_out, gain_mlp, w_up, w_down, cotangent
):
    rows = layer_input.shape[1]
    width = layer_input.shape[2]
    shard = w_up.shape[0]
    space = plan.space
    me = lax.axis_index("tm") * space + lax.axis_index("space")
    inputs = layer_input[0].astype(f32)
    grad_out = cotangent[0].astype(f32)
    swap = plan.swap
    attn = Side(plan, me, plan.team, plan.gather, plan.octets, shard, width, rows, rows * 3 // 8)
    feed = Side(
        plan, me, plan.feed_team, plan.feed_gather, plan.feed_octets, shard, width, rows, rows // 2
    )

    def has(bit):
        return (me & bit) != 0

    gain_one = gain_attn.astype(f32)[:, None]
    gain_two = gain_mlp.astype(f32)[:, None]
    qkv_scaled = (w_qkv.astype(f32) * gain_one).astype(bf16)
    up_scaled = (w_up.astype(f32) * gain_two).astype(bf16)
    n_ff = w_up.shape[1] // 8
    qkv_sent = (
        qkv_scaled.reshape(shard, 3, 2, 2, 2, 2, HEAD)
        .transpose(2, 5, 3, 0, 4, 1, 6)
        .reshape(8, shard, 6 * HEAD)
    )
    qkv_columns = [
        (
            4 * hi + 2 * lo + c,
            (3 * jj + i) * HEAD,
            (3 * jj + i + 1) * HEAD,
            (i * HEADS + 8 * hi + 4 * c + 2 * jj + lo) * HEAD,
        )
        for hi in range(2)
        for lo in range(2)
        for c in range(2)
        for jj in range(2)
        for i in range(3)
    ]
    ff_columns = [(b, 0, n_ff, b * n_ff) for b in range(8)]
    up_sent = up_scaled.reshape(shard, 8, n_ff).transpose(1, 0, 2)
    down_sent = w_down.reshape(shard, 8, n_ff).transpose(1, 0, 2)

    qkv_sent, tokens = tied(qkv_sent, layer_input[0])
    first_rel = attn.to_rel(tokens, True)
    grad_rel = feed.to_rel(cotangent[0], False)
    qkv_block = attn.octet(qkv_sent).reshape(8 * shard, -1)
    qkv_block, first_rel, grad_rel, up_sent, down_sent, w_out = tied(
        qkv_block, first_rel, grad_rel, up_sent, down_sent, w_out
    )
    first_near = attn.gather_one(first_rel)
    qkv_first = swap(qkv_block, attn.first)
    qkv_second = swap(qkv_block, attn.second)
    qkv_first, qkv_second, up_sent, first_near, w_out = tied(
        qkv_first, qkv_second, up_sent, first_near, w_out
    )
    qkv_both = swap(qkv_first, attn.second)
    first_far = attn.gather_two(*first_near)
    out_z = swap(w_out, attn.first)
    up_block = feed.octet(up_sent).reshape(8 * shard, -1)
    qkv_both, first_far, up_block, down_sent, out_z, w_out, grad_rel = tied(
        qkv_both, first_far, up_block, down_sent, out_z, w_out, grad_rel
    )
    qkv_mine = attn.joined(qkv_block, qkv_first, qkv_second, qkv_both)
    qkv_other = swap(qkv_mine, 1)
    first_all = team_rows(*first_near, *first_far)
    n_block = up_block.shape[0]
    half = n_block // 2
    up_za = swap(up_block[:half], feed.first)
    up_x = swap(up_block, feed.second)
    grad_near = feed.gather_one(grad_rel)
    down_block = feed.octet(down_sent).reshape(8 * shard, -1)

    team_device = me ^ jnp.array(plan.team_rel, jnp.int32)
    row_index = jnp.arange(rows, dtype=jnp.int32)
    positions = (
        ((team_device // space) % plan.clip * (space * rows) + (team_device % space) * rows)[:, None]
        + row_index[None, :]
    ).reshape(4 * rows)
    half_dim = HEAD // 2
    inverse_freq = jnp.exp(-jnp.log(10000.0) * jnp.arange(half_dim, dtype=f32) * 2.0 / HEAD)
    angles = positions.astype(f32)[:, None] * inverse_freq[None, :]
    angles = jnp.concatenate([angles, angles], axis=-1)
    cosine, sine = jnp.cos(angles), jnp.sin(angles)

    def rotate(value):
        turned = jnp.concatenate([-value[:, half_dim:], value[:, :half_dim]], axis=-1)
        return value * cosine + turned * sine

    def rotate_back(value):
        scaled = value * sine
        turned = jnp.concatenate([scaled[:, half_dim:], -scaled[:, :half_dim]], axis=-1)
        return value * cosine + turned

    def head_triples(mixed):
        found = []
        for j in range(2):
            q, k, v = (
                mixed[:, (3 * j + i) * HEAD : (3 * j + i + 1) * HEAD] for i in range(3)
            )
            found.append(
                jnp.concatenate([rotate(q) * to_log2, rotate(k), v], axis=1).astype(bf16)
            )
        return found

    mixed_mine = matmul(first_all, qkv_mine)
    mixed_other = matmul(first_all, qkv_other)
    stack = jnp.stack(head_triples(mixed_mine) + head_triples(mixed_other))
    my_head = jnp.where(has(plan.heads[0]), 2, 0) + jnp.where(has(plan.heads[1]), 1, 0)
    core_flip = jnp.where(has(1), 2, 0)
    pick = [(my_head ^ r) ^ core_flip for r in range(4)]
    sent = [lax.dynamic_index_in_dim(stack, pick[r], 0, keepdims=False) for r in range(4)]
    out_pair = jnp.stack([w_out, out_z])
    sent, up_za, up_x, grad_near, up_block, up_half, down_block, out_z, w_out, out_pair = tied(
        sent, up_za, up_x, grad_near, up_block, up_block[half:], down_block, out_z, w_out, out_pair
    )
    got = [swap(sent[r], plan.head_rel[r]) for r in range(1, 4)]
    up_zb = swap(up_half, feed.first)
    out_x = swap(out_pair, attn.second)
    cut_z = [0, n_block // 2, n_block * 3 // 4, n_block]
    got, up_za, up_zb, down_block, grad_near, out_x, down_first = tied(
        got, up_za, up_zb, down_block, grad_near, out_x, down_block[: cut_z[1]]
    )
    own = jnp.stack([sent[0]] + got).reshape(16, rows, 3 * HEAD)
    down_z = [swap(down_first, feed.first)]
    up_both = [swap(up_za, feed.second), swap(up_zb, feed.second)]
    grad_far = feed.gather_two(*grad_near)
    shared = own[:, :, HEAD:]
    other = jnp.stack([swap(shared, rel) for rel in plan.part_rel[1:]])

    block_rel = jnp.array(plan.block_rel, jnp.int32)
    tile_rel = jnp.array(plan.block_rel[:: plan.tile_blocks], jnp.int32)
    tile_slot = (me ^ tile_rel) // space
    no_more = jnp.zeros((16 - tile_slot.shape[0],), jnp.int32)
    info = jnp.concatenate(
        [
            jnp.stack([me, (me % space) * rows, ((me ^ plan.team[1]) % space) * rows]),
            jnp.zeros((5,), jnp.int32),
            block_rel,
            tile_slot,
            no_more,
            tile_slot // plan.clip * plan.clip,
            no_more,
        ]
    ).astype(jnp.int32)

    attended, attended_t, log_total, keys, values = attend(plan, info, frame_real, own, other)
    w_team = jnp.stack([w_out, out_x[0], out_z, out_x[1]])
    attended, down_z, up_both, grad_far, w_team, down_block, up_x, up_za, up_zb, up_block = tied(
        attended, down_z, up_both, grad_far, w_team, down_block, up_x, up_za, up_zb, up_block
    )
    w_got = swap(w_team, plan.parts[-1])
    attended = attended.reshape(4, 4 * rows, HEAD)
    heads_got = [swap(attended[r], plan.head_rel[r]) for r in range(1, 4)]
    down_z += [swap(down_block[cut_z[1] : cut_z[2]], feed.first)]
    up_mine = feed.joined(up_block, up_za, up_zb, up_x, *up_both)
    for bit in reversed(plan.parts):
        w_got = w_got if bit == plan.parts[-1] else swap(w_team, bit)
        w_team = jnp.where(
            has(bit),
            jnp.concatenate([w_got, w_team], axis=1),
            jnp.concatenate([w_team, w_got], axis=1),
        )
    w_team = w_team.reshape(4 * HEAD, width)
    heads_got, w_team, down_z, grad_far, down_block, up_mine = tied(
        heads_got, w_team, down_z, grad_far, down_block, up_mine
    )
    attended_team = jnp.concatenate([attended[0]] + heads_got, axis=1)
    branch = matmul(attended_team, w_team).astype(bf16)
    branch_near = attn.scatter_one(branch)
    cut_x = n_block * 5 // 8
    down_x = [swap(down_block[:cut_x], feed.second)]
    up_other = swap(up_mine, 1)
    grad_all = team_rows(*grad_near, *grad_far)
    branch_near, down_x, up_other, down_z, grad_all, down_block = tied(
        branch_near, down_x, up_other, down_z, grad_all, down_block
    )
    middle = attn.scatter_two(*branch_near)
    down_x += [swap(down_block[cut_x:], feed.second)]
    middle, down_x, down_z, down_block = tied(middle, down_x, down_z, down_block)
    middle = inputs + middle
    second_near = feed.gather_one(feed.to_rel(middle, True))
    down_z += [swap(down_block[cut_z[2] :], feed.first)]
    cut_both = n_block * 5 // 16
    down_both = [swap(down_z[0][:cut_both], feed.second)]
    second_near, down_both, down_z = tied(second_near, down_both, down_z)
    second_far = feed.gather_two(*second_near)
    down_z = jnp.concatenate(down_z)
    down_both += [swap(down_z[cut_both:], feed.second)]
    second_far, down_both, down_z = tied(second_far, down_both, down_z)
    down_mine = feed.joined(down_block, down_z, *down_x, *down_both)
    down_other = swap(down_mine, 1)
    second_all = team_rows(*second_near, *second_far)
    normed_two, scale_two = layer_norm(middle)
    gelu = functools.partial(jax.nn.gelu, approximate=True)
    hidden_other = matmul(second_all, up_other)
    hidden_mine = matmul(second_all, up_mine)
    act_other = gelu(hidden_other).astype(bf16)
    act_mine = gelu(hidden_mine).astype(bf16)
    down_other_grad = matmul(grad_all, act_other, ((0,), (0,))).astype(bf16)
    down_other_grad, down_other, down_mine, act_mine, act_other = tied(
        down_other_grad, down_other, down_mine, act_mine, act_other
    )
    down_swapped = swap(down_other_grad, 1)
    down_mine_grad = matmul(grad_all, act_mine, ((0,), (0,))).astype(bf16)

    def back(hidden, down):
        return jax.vjp(gelu, hidden)[1](matmul(grad_all, down))[0].astype(bf16)

    hid_mine, hid_other = back(hidden_mine, down_mine), back(hidden_other, down_other)
    second_parts = matmul(hid_mine, up_mine, ((1,), (1,))) + matmul(hid_other, up_other, ((1,), (1,)))
    second_parts, hid_mine, hid_other, down_swapped, down_mine_grad = tied(
        second_parts.astype(bf16), hid_mine, hid_other, down_swapped, down_mine_grad
    )
    second_back = feed.scatter_one(second_parts)
    down_sum = feed.first_sum(down_mine_grad, down_swapped)
    c1, c2, c3 = n_block * 3 // 8, n_block * 3 // 4, n_block * 3 // 8
    down_x3 = [swap(down_sum[3][:c1], feed.second)]
    second_back, down_x3, down_sum = tied(second_back, down_x3, down_sum)
    grad_second = feed.scatter_two(*second_back)
    z1, z2 = n_block * 3 // 16, n_block * 3 // 8
    down_z1 = [swap(added(down_sum[1][:z1], down_x3[0][:z1]), feed.first)]
    down_x3 += [swap(down_sum[3][c1:c2], feed.second)]
    grad_second, down_z1, down_x3, down_sum, act_mine, act_other = tied(
        grad_second, down_z1, down_x3, down_sum, act_mine, act_other
    )
    grad_second = feed.from_rel(grad_second)
    grad_middle = grad_out + layer_norm_back(grad_second, normed_two, scale_two)
    middle_near = attn.gather_one(grad_middle.astype(bf16))
    down_x32 = swap(jnp.concatenate([down_sum[3][c2:], down_sum[2][:c3]]), feed.second)
    out_parts = (
        matmul(act_mine, down_mine, ((1,), (1,))) + matmul(act_other, down_other, ((1,), (1,)))
    ).astype(bf16)
    middle_near, out_parts, hid_other, hid_mine, down_x32, down_sum, down_x3 = tied(
        middle_near, out_parts, hid_other, hid_mine, down_x32, down_sum, down_x3
    )
    middle_far = attn.gather_two(*middle_near)
    down_x3 = jnp.concatenate([*down_x3, down_x32[: n_block - c2]])
    down_x2 = [down_x32[n_block - c2 :], swap(down_sum[2][c3:], feed.second)]
    up_other_grad = matmul(second_all, hid_other, ((0,), (0,))).astype(bf16)
    up_swapped = swap(up_other_grad, 1)
    up_mine_grad = matmul(second_all, hid_mine, ((0,), (0,))).astype(bf16)
    down_z1b = added(down_sum[1][z1:z2], down_x3[z1:z2])
    middle_far, up_swapped, up_mine_grad, down_x2, down_x3, down_sum, down_z1b = tied(
        middle_far, up_swapped, up_mine_grad, down_x2, down_x3, down_sum, down_z1b
    )
    middle_all = team_rows(*middle_near, *middle_far)
    grad_heads = matmul(middle_all, w_team, ((1,), (1,))).astype(bf16)
    grad_own = grad_heads[:, :HEAD]
    grad_got = [
        swap(grad_heads[:, r * HEAD : (r + 1) * HEAD], plan.head_rel[r]) for r in range(1, 4)
    ]
    down_z1 += [swap(down_z1b, feed.first)]
    out_grad = matmul(attended_team, middle_all, ((0,), (0,))).astype(bf16).reshape(4, HEAD, width)
    up_sum = feed.first_sum(up_mine_grad, up_swapped)
    down_z1c = added(down_sum[1][z2:], down_x3[z2:])
    grad_got, up_sum, out_grad, down_z1, down_z1c, out_parts = tied(
        grad_got, up_sum, out_grad, down_z1, down_z1c, out_parts
    )
    up_x3 = swap(up_sum[3], feed.second)
    down_z1 += [swap(down_z1c, feed.first)]
    out_near = feed.scatter_one(out_parts)
    for bit in plan.parts:
        lower, upper = jnp.split(out_grad, 2, axis=1)
        kept = jnp.where(has(bit), upper, lower)
        out_grad = added(kept, swap(jnp.where(has(bit), lower, upper), bit))
    dq, dkv_own, dkv_other = attend_back(
        plan,
        info,
        frame_real,
        own,
        keys,
        values,
        jnp.stack([grad_own] + grad_got).reshape(16, rows, HEAD),
        attended_t,
        log_total,
    )
    dq, dkv_own, dkv_other, up_x3, down_z1, out_near, out_grad = tied(
        dq, dkv_own, dkv_other, up_x3, down_z1, out_near, out_grad
    )
    dkv = dkv_own.astype(f32)
    for i, rel in enumerate(plan.part_rel[1:]):
        dkv = dkv + swap(dkv_other[i], rel).astype(f32)
    triple = jnp.concatenate([dq, dkv.astype(bf16)], axis=2).reshape(4, 4 * rows, 3 * HEAD)
    up_z1 = added(up_sum[1], up_x3)
    triple, up_sum, up_z1, up_z1a, down_z1 = tied(triple, up_sum, up_z1, up_z1[:half], down_z1)
    got = [swap(triple[r], plan.head_rel[r]) for r in range(1, 4)]
    up_z1a = swap(up_z1a, feed.first)
    down_done = added(down_sum[0], jnp.concatenate(down_x2), jnp.concatenate(down_z1))
    got, up_z1a, up_z1, down_done, up_sum, out_grad, out_near = tied(
        got, up_z1a, up_z1, down_done, up_sum, out_grad, out_near
    )
    places = (my_head ^ jnp.arange(4, dtype=jnp.int32)) ^ core_flip
    mixed_grad = turn_back(places, cosine, sine, [triple[0]] + got)
    mixed_grad_mine, mixed_grad_other = mixed_grad[0], mixed_grad[1]
    qkv_other_grad = matmul(first_all, mixed_grad_other, ((0,), (0,))).astype(bf16)
    out_sum = feed.scatter_two(*out_near)
    kept, sent = out_grad.reshape(2, 2, -1, width)[:, 0], out_grad.reshape(2, 2, -1, width)[:, 1]
    out_grad = added(kept, swap(sent, attn.second))
    qkv_other_grad, mixed_grad_mine, up_sum, up_z1, down_done, out_sum, out_grad, up_z1b = tied(
        qkv_other_grad, mixed_grad_mine, up_sum, up_z1, down_done, out_sum, out_grad, up_z1[half:]
    )
    qkv_swapped = swap(qkv_other_grad, 1)
    up_x2 = swap(up_sum[2], feed.second)
    up_z1b = swap(up_z1b, feed.first)
    down_got = feed.octet(down_done)
    qkv_mine_grad = matmul(first_all, mixed_grad_mine, ((0,), (0,))).astype(bf16)
    first_parts = matmul(mixed_grad_mine, qkv_mine, ((1,), (1,))) + matmul(
        mixed_grad_other, qkv_other, ((1,), (1,))
    )
    qkv_sum = attn.first_sum(qkv_mine_grad, qkv_swapped)
    qkv_sum, first_parts, up_x2, up_sum, up_z1b, down_got, out_grad = tied(
        qkv_sum, first_parts.astype(bf16), up_x2, up_sum, up_z1b, down_got, out_grad
    )
    qkv_x3 = swap(qkv_sum[3], attn.second)
    first_back = attn.scatter_one(first_parts)
    up_done = added(up_sum[0], up_x2, jnp.concatenate([up_z1a, up_z1b]))
    grad_down = down_got.transpose(1, 0, 2).reshape(shard, 8 * n_ff).astype(f32)
    up_got = feed.octet(up_done)
    qkv_x3, first_back, up_got, qkv_sum, grad_down = tied(
        qkv_x3, first_back, up_got, qkv_sum, grad_down
    )
    qkv_z1 = swap(added(qkv_sum[1], qkv_x3), attn.first)
    qkv_x2 = swap(qkv_sum[2], attn.second)
    first_rows = attn.scatter_two(*first_back)
    output = (middle + feed.from_rel(out_sum)).astype(bf16)
    grad_up, grad_gain_two = deliver(ff_columns, up_got, w_up, gain_two)
    qkv_z1, qkv_x2, first_rows, out_grad, output, grad_up = tied(
        qkv_z1, qkv_x2, first_rows, out_grad, output, grad_up
    )
    qkv_got = attn.octet(added(qkv_sum[0], qkv_x2, qkv_z1))
    grad_first = attn.from_rel(first_rows)
    grad_inputs = grad_middle + layer_norm_back(grad_first, *layer_norm(inputs))
    out_grad = out_grad[0].astype(f32) + swap(out_grad[1], attn.first).astype(f32)
    grad_qkv, grad_gain_one = deliver(qkv_columns, qkv_got, w_qkv, gain_one)
    return (
        output[None],
        grad_inputs[None],
        grad_gain_one[:, 0],
        grad_qkv,
        out_grad,
        grad_gain_two[:, 0],
        grad_up,
        grad_down,
    )


def solution(mesh):
    plan = Plan(mesh.shape["tm"], mesh.shape["space"], BLOCK)
    tokens = P("tm", "space", None)
    line = P(("tm", "space"))
    table = P(("tm", "space"), None)
    return jax.shard_map(
        functools.partial(on_device, plan),
        mesh=mesh,
        in_specs=(tokens, P(), line, table, table, line, table, table, tokens),
        out_specs=(tokens, tokens, line, table, table, line, table, table),
        check_vma=False,
    )
```

```python
import functools

import jax
import jax.numpy as jnp
import numpy as np
from jax import lax
from jax.experimental import pallas as pl
from jax.experimental.pallas import tpu as pltpu
from jax.sharding import PartitionSpec as P

HEADS = 16
HEAD = 128
AXES = ("tm", "space")
BLOCK = 128

epsilon = 1e-05
masked_value = -1e30
inv_root = HEAD ** (-0.5)
to_log2 = inv_root * 1.4426950408889634
q_unscale = inv_root / to_log2

bf16 = jnp.bfloat16
f32 = jnp.float32


def matmul(left, right, dims=((1,), (0,))):
    return lax.dot_general(left, right, (dims, ((), ())), preferred_element_type=f32)


def tied(*values):
    return lax.optimization_barrier(values)


class Plan:
    def __init__(self, tm, space, frame_rows):
        self.count = tm * space
        self.space = space
        self.slots = tm
        self.clip = min(16, tm)
        count = self.count
        self.team = (count // 2, count // 16)
        self.heads = (count // 4, count // 8)
        self.feed_team = (count // 4, count // 16)
        bits = [1 << i for i in range(count.bit_length() - 1)]
        taken = set(self.team + self.heads)
        self.parts = [b for b in reversed(bits) if b not in taken]
        rest = [b for b in self.parts if b != 1]
        self.gather = [*self.heads, *rest]
        self.feed_gather = [count // 2, count // 8, *rest]
        self.team_rel = [0, self.team[1], self.team[0], self.team[0] | self.team[1]]
        self.head_rel = [0, self.heads[1], self.heads[0], self.heads[0] | self.heads[1]]
        self.block_rel = [h | t for h in self.head_rel for t in self.team_rel]
        self.part_rel = [
            sum(b for j, b in enumerate(self.parts) if (i >> j) & 1)
            for i in range(1 << len(self.parts))
        ]
        devices = range(count)
        self.octets = self.groups(sum(self.team) | 1)
        self.tile_blocks = 2 if self.team[1] < space else 1
        self.devices = devices

    def groups(self, mask):
        held = {}
        for d in range(self.count):
            held.setdefault(d & ~mask, []).append(d)
        return list(held.values())

    def swap(self, value, mask):
        return lax.ppermute(value, AXES, [(d, d ^ mask) for d in self.devices])


def layer_norm(values):
    center = jnp.mean(values, axis=-1, keepdims=True)
    shifted = values - center
    spread = jnp.mean(shifted * shifted, axis=-1, keepdims=True)
    scale = lax.rsqrt(spread + epsilon)
    return shifted * scale, scale


def layer_norm_back(grads, normed, scale):
    inner = jnp.mean(grads * normed, axis=-1, keepdims=True)
    return (grads - jnp.mean(grads, axis=-1, keepdims=True) - normed * inner) * scale


def transposed(tile):
    return tile.astype(f32).T.astype(tile.dtype)


def attend_kernel(plan, info, real, own, other, out, out_t, lse, keys, values, values_t):
    me = info[0]
    n_blocks = len(plan.block_rel)
    for part, part_rel in enumerate(plan.part_rel):

        def place(b, _, part=part, part_rel=part_rel):
            home = me ^ part_rel ^ info[8 + b]
            if part == 0:
                key, value = own[b, :, HEAD : 2 * HEAD], own[b, :, 2 * HEAD :]
            else:
                key, value = other[part - 1, b, :, :HEAD], other[part - 1, b, :, HEAD:]
            rows = pl.ds(pl.multiple_of(home * BLOCK, BLOCK), BLOCK)
            keys[rows, :] = key
            values[rows, :] = value
            values_t[home] = transposed(value)
            return 0

        lax.fori_loop(0, n_blocks, place, 0, unroll=4)

    frame = plan.space * BLOCK
    per_tile = plan.tile_blocks
    two = per_tile * BLOCK
    lane = lax.broadcasted_iota(jnp.int32, (1, two), 1)
    q_place = jnp.where(lane < BLOCK, info[1] + lane, info[2] + lane - BLOCK)

    def tile(i, _):
        slot, first = info[24 + i], info[40 + i]
        q = jnp.concatenate([own[per_tile * i + j, :, :HEAD] for j in range(per_tile)], axis=0)

        def scores(g):
            key = keys[pl.ds(pl.multiple_of(g * frame, frame), frame), :]
            return matmul(key, q, ((1,), (1,)))

        def value_t(g):
            return jnp.concatenate(
                [values_t[g * plan.space + s] for s in range(plan.space)], axis=1
            )

        def fold(carry, s, g):
            top, total, acc = carry
            new = jnp.maximum(top, jnp.max(s, axis=0, keepdims=True))
            fade = jnp.exp2(top - new)
            p = jnp.exp2(s - new)
            total = total * fade + jnp.sum(p, axis=0, keepdims=True)
            acc = acc * fade + matmul(value_t(g), p.astype(bf16))
            return new, total, acc

        def step(g, carry):
            ahead = scores(g + 1)
            s = carry[3] + jnp.where(real[g] > 0, 0.0, masked_value)
            return (*fold(carry[:3], s, g), ahead)

        first = jnp.where(real[slot] > 0, first, slot)
        start = (
            jnp.full((1, two), masked_value, f32),
            jnp.zeros((1, two), f32),
            jnp.zeros((HEAD, two), f32),
            scores(first),
        )
        *carry, s = lax.fori_loop(first, slot, step, start)
        k_place = lax.broadcasted_iota(jnp.int32, (frame, two), 0)
        top, total, acc = fold(carry, jnp.where(k_place <= q_place, s, masked_value), slot)
        lse[i] = top + jnp.log2(total)
        acc = acc / total
        out_t[i] = acc
        back = acc.T.astype(bf16)
        for j in range(per_tile):
            out[per_tile * i + j] = back[j * BLOCK : (j + 1) * BLOCK]
        return 0

    lax.fori_loop(0, n_blocks // per_tile, tile, 0)


def attend_back_kernel(
    plan, info, real, own, keys, values, grads, out_t, lse, dq, dkv_own, dkv_other, dk, dv, keys_t
):
    me = info[0]
    n_blocks = len(plan.block_rel)

    def clear(b, _):
        rows = pl.ds(pl.multiple_of(b * BLOCK, BLOCK), BLOCK)
        dk[rows, :] = jnp.zeros((BLOCK, HEAD), f32)
        dv[rows, :] = jnp.zeros((BLOCK, HEAD), f32)
        keys_t[b] = transposed(keys[rows, :])
        return 0

    lax.fori_loop(0, plan.count, clear, 0, unroll=4)

    frame = plan.space * BLOCK
    per_tile = plan.tile_blocks
    two = per_tile * BLOCK
    lane = lax.broadcasted_iota(jnp.int32, (1, two), 1)
    q_place = jnp.where(lane < BLOCK, info[1] + lane, info[2] + lane - BLOCK)

    def tile(i, _):
        slot, first = info[24 + i], info[40 + i]
        q = jnp.concatenate([own[per_tile * i + j, :, :HEAD] for j in range(per_tile)], axis=0)
        do = jnp.concatenate([grads[per_tile * i + j] for j in range(per_tile)], axis=0)
        delta = jnp.sum(do.astype(f32).T * out_t[i], axis=0, keepdims=True)
        log_total = lse[i]

        def turn(g, mask):
            rows = pl.ds(pl.multiple_of(g * frame, frame), frame)
            key, value = keys[rows, :], values[rows, :]
            s = matmul(key, q, ((1,), (1,)))
            dp = matmul(value, do, ((1,), (1,)))
            if mask:
                p = jnp.exp2(s - log_total)
            else:
                p = jnp.exp2(s - jnp.where(real[g] > 0, log_total, -masked_value))
            if mask:
                k_place = lax.broadcasted_iota(jnp.int32, (frame, two), 0)
                p = jnp.where(k_place <= q_place, p, 0.0)
            ds = (p * (dp - delta)).astype(bf16)
            dv[rows, :] += matmul(p.astype(bf16), do)
            dk[rows, :] += matmul(ds, q)
            key_t = jnp.concatenate(
                [keys_t[g * plan.space + s] for s in range(plan.space)], axis=1
            )
            return matmul(key_t, ds)

        def step(g, dq_t):
            return dq_t + turn(g, False)

        first = jnp.where(real[slot] > 0, first, slot)
        dq_t = lax.fori_loop(first, slot, step, turn(slot, True))
        back = (dq_t * inv_root).T.astype(bf16)
        for j in range(per_tile):
            dq[per_tile * i + j] = back[j * BLOCK : (j + 1) * BLOCK]
        return 0

    lax.fori_loop(0, n_blocks // per_tile, tile, 0)

    for part, part_rel in enumerate(plan.part_rel):

        def hand_out(b, _, part=part, part_rel=part_rel):
            home = me ^ part_rel ^ info[8 + b]
            rows = pl.ds(pl.multiple_of(home * BLOCK, BLOCK), BLOCK)
            pair = jnp.concatenate([dk[rows, :] * q_unscale, dv[rows, :]], axis=1).astype(bf16)
            if part == 0:
                dkv_own[b] = pair
            else:
                dkv_other[part - 1, b] = pair
            return 0

        lax.fori_loop(0, n_blocks, hand_out, 0, unroll=4)


def call(kernel, n_scalar, n_in, outs, scratch, cost, room=16):
    return pl.pallas_call(
        kernel,
        out_shape=outs,
        in_specs=[pl.BlockSpec(memory_space=pltpu.SMEM)] * n_scalar
        + [pl.BlockSpec(memory_space=pltpu.VMEM)] * n_in,
        out_specs=tuple(pl.BlockSpec(memory_space=pltpu.VMEM) for _ in outs),
        scratch_shapes=scratch,
        cost_estimate=cost,
        compiler_params=pltpu.CompilerParams(vmem_limit_bytes=room << 20),
    )


def moving(n_bytes):
    return pl.CostEstimate(flops=n_bytes, bytes_accessed=n_bytes, transcendentals=0)


def arrange_kernel(normed, chunk, lanes, value, out, held):
    x = value[...].astype(f32)
    if normed:
        x = layer_norm(x)[0]
    held[...] = x.astype(bf16)
    for j in range(x.shape[1] // chunk):
        at = pl.multiple_of(lanes[j], chunk)
        out[:, j * chunk : (j + 1) * chunk] = held[:, pl.ds(at, chunk)]


def arrange(normed, chunk, lanes, value):
    shape = value.shape
    return call(
        functools.partial(arrange_kernel, normed, chunk),
        1,
        1,
        (jax.ShapeDtypeStruct(shape, bf16),),
        [pltpu.VMEM(shape, bf16)],
        moving(4 * value.size),
    )(lanes, value)[0]


def team_rows_kernel(a, b, a_lo, b_hi, a_far, b_far, out):
    one, two = a.shape[0], b.shape[0]
    pieces = (a[...], b[...], a_lo[...], b_far[:two], a_far[:one], b_hi[...], a_far[one:], b_far[two:])
    start = 0
    for piece in pieces:
        out[start : start + piece.shape[0]] = piece
        start += piece.shape[0]


def team_rows(*pieces):
    rows, width = pieces[0].shape[0] + pieces[1].shape[0], pieces[0].shape[1]
    return call(
        team_rows_kernel,
        0,
        6,
        (jax.ShapeDtypeStruct((4 * rows, width), bf16),),
        [],
        moving(16 * rows * width),
    )(*pieces)[0]


def turn_back_kernel(places, cosine, sine, *refs):
    heads, out = refs[:4], refs[4]
    half_dim = HEAD // 2
    cos, sin = cosine[...], sine[...]
    for r in range(4):
        found = []
        for i in range(2):
            t = heads[r][:, i * HEAD : (i + 1) * HEAD].astype(f32)
            scaled = t * sin
            turned = jnp.concatenate([scaled[:, half_dim:], -scaled[:, :half_dim]], axis=-1)
            found.append((t * cos + turned).astype(bf16))
        found.append(heads[r][:, 2 * HEAD :])
        whole = jnp.concatenate(found, axis=1)
        place = places[r]

        @pl.when(place % 2 == 0)
        def _():
            out[place // 2, :, : 3 * HEAD] = whole

        @pl.when(place % 2 == 1)
        def _():
            out[place // 2, :, 3 * HEAD :] = whole


def turn_back(places, cosine, sine, heads):
    rows = cosine.shape[0]
    return call(
        turn_back_kernel,
        1,
        6,
        (jax.ShapeDtypeStruct((2, rows, 6 * HEAD), bf16),),
        [],
        moving(8 * rows * 3 * HEAD * 2),
    )(places, cosine, sine, *heads)[0]


def deliver_kernel(columns, got, weight, gain, out, gain_grad):
    total = None
    for block, start, end, target in columns:
        value = got[block, :, start:end].astype(f32)
        span = slice(target, target + end - start)
        part = jnp.sum(value * weight[:, span].astype(f32), axis=1, keepdims=True)
        total = part if total is None else total + part
        out[:, span] = value * gain[...]
    gain_grad[...] = jnp.broadcast_to(total, gain_grad.shape)


def deliver(columns, got, weight, gain):
    rows, width = weight.shape
    return call(
        functools.partial(deliver_kernel, columns),
        0,
        3,
        (jax.ShapeDtypeStruct((rows, width), f32), jax.ShapeDtypeStruct((rows, 128), f32)),
        [],
        moving(8 * rows * width),
    )(got, weight, gain)


def spread_kernel(places, up, down, gain, out):
    n = out.shape[2] // 2
    for i in range(8):
        at = pl.ds(pl.multiple_of(places[i] * n, n), n)
        out[i, :, :n] = (up[:, at].astype(f32) * gain[...]).astype(bf16)
        out[i, :, n:] = down[:, at]


def spread(places, up, down, gain):
    rows, width = up.shape
    return call(
        spread_kernel,
        1,
        3,
        (jax.ShapeDtypeStruct((8, rows, width // 4), bf16),),
        [],
        moving(8 * rows * width),
    )(places, up, down, gain)[0]


def settle_kernel(places, kept, got, out):
    rows = kept.shape[1]
    for i in range(8):
        at = pl.ds(pl.multiple_of(places[i] * rows, rows), rows)
        out[at, :] = kept[i] if i < 4 else got[i - 4]


def settle(places, kept, got):
    _, rows, n = kept.shape
    return call(
        settle_kernel,
        1,
        2,
        (jax.ShapeDtypeStruct((8 * rows, n), bf16),),
        [],
        moving(32 * rows * n),
    )(places, kept, got)[0]


def unsettle_kernel(places, block, kept, sent):
    rows = kept.shape[1]
    for i in range(8):
        value = block[pl.ds(pl.multiple_of(places[i] * rows, rows), rows), :]
        if i < 4:
            kept[i] = value
        else:
            sent[i - 4] = value


def unsettle(places, block):
    rows, n = block.shape[0] // 8, block.shape[1]
    half = jax.ShapeDtypeStruct((4, rows, n), bf16)
    return call(unsettle_kernel, 1, 1, (half, half), [], moving(32 * rows * n))(places, block)


def restore_kernel(with_gain, places, got, weight, gain, out, gain_grad):
    n = got.shape[2]
    total = None
    for i in range(8):
        at = pl.ds(pl.multiple_of(places[i] * n, n), n)
        value = got[i].astype(f32)
        if with_gain:
            part = jnp.sum(value * weight[:, at].astype(f32), axis=1, keepdims=True)
            total = part if total is None else total + part
            value = value * gain[...]
        out[:, at] = value
    if with_gain:
        gain_grad[...] = jnp.broadcast_to(total, gain_grad.shape)
    else:
        gain_grad[...] = jnp.zeros(gain_grad.shape, f32)


def restore(with_gain, places, got, weight, gain):
    rows, width = weight.shape
    return call(
        functools.partial(restore_kernel, with_gain),
        1,
        3,
        (jax.ShapeDtypeStruct((rows, width), f32), jax.ShapeDtypeStruct((rows, 128), f32)),
        [],
        moving(8 * rows * width),
    )(places, got, weight, gain)


def attend(plan, info, real, own, other):
    blocks = len(plan.block_rel)
    tokens = plan.count * BLOCK
    work = blocks * BLOCK * min(plan.clip * plan.space * BLOCK, tokens) // 2
    shape = jax.ShapeDtypeStruct
    return call(
        functools.partial(attend_kernel, plan),
        2,
        2,
        (
            shape((blocks, BLOCK, HEAD), bf16),
            shape((blocks // plan.tile_blocks, HEAD, plan.tile_blocks * BLOCK), f32),
            shape((blocks // plan.tile_blocks, 1, plan.tile_blocks * BLOCK), f32),
            shape((tokens, HEAD), bf16),
            shape((tokens, HEAD), bf16),
        ),
        [pltpu.VMEM((plan.count, HEAD, BLOCK), bf16)],
        pl.CostEstimate(flops=8 * work * HEAD, bytes_accessed=8 << 20, transcendentals=work),
        min(56, 8 + plan.count * 3 // 4),
    )(info, real, own, other)


def attend_back(plan, info, real, own, keys, values, grads, out_t, lse):
    blocks = len(plan.block_rel)
    tokens = plan.count * BLOCK
    work = blocks * BLOCK * min(plan.clip * plan.space * BLOCK, tokens) // 2
    shape = jax.ShapeDtypeStruct
    return call(
        functools.partial(attend_back_kernel, plan),
        2,
        6,
        (
            shape((blocks, BLOCK, HEAD), bf16),
            shape((blocks, BLOCK, 2 * HEAD), bf16),
            shape((len(plan.part_rel) - 1, blocks, BLOCK, 2 * HEAD), bf16),
        ),
        [
            pltpu.VMEM((tokens, HEAD), f32),
            pltpu.VMEM((tokens, HEAD), f32),
            pltpu.VMEM((plan.count, HEAD, BLOCK), bf16),
        ],
        pl.CostEstimate(flops=20 * work * HEAD, bytes_accessed=8 << 20, transcendentals=work),
        min(56, 8 + plan.count * 3 // 4),
    )(info, real, own, keys, values, grads, out_t, lse)


def added(*values):
    return sum(v.astype(f32) for v in values).astype(bf16)


class Side:
    def __init__(self, plan, me, team, gather, groups, shard, width, rows, cut):
        self.plan, self.me, self.groups = plan, me, groups
        self.team_hi, self.team_lo = team
        self.gather, self.shard, self.cut = gather, shard, cut
        self.first, self.second = gather[:2]
        low = self.low = min(gather)
        self.chunk = low * shard
        self.n_chunks = width // self.chunk
        self.order = [
            (
                sum(b for j, b in enumerate(gather) if (i >> j) & 1)
                + (self.team_hi if hi else 0)
                + (self.team_lo if lo else 0)
            )
            // low
            for i in range(1 << len(gather))
            for hi in range(2)
            for lo in range(2 if self.team_lo > low else 1)
        ]
        self.inverse = [self.order.index(m) for m in range(self.n_chunks)]
        at = jnp.array(self.order, jnp.int32) ^ ((me & sum(gather)) // low)
        self.lanes = at * self.chunk

    def swap(self, value, bit):
        return self.plan.swap(value, bit)

    def flipped(self, pieces):
        for bit in self.gather:
            step = bit // self.low
            own = (self.me & bit) != 0
            pieces = [jnp.where(own, pieces[m ^ step], pieces[m]) for m in range(self.n_chunks)]
        return pieces

    def pieces(self, value):
        chunk = self.chunk
        return [value[:, m * chunk : (m + 1) * chunk] for m in range(self.n_chunks)]

    def to_rel(self, value, normed):
        if self.chunk % 128 == 0:
            return arrange(normed, self.chunk, self.lanes, value)
        value = layer_norm(value.astype(f32))[0] if normed else value
        pieces = self.flipped(self.pieces(value.astype(bf16)))
        return jnp.concatenate([pieces[m] for m in self.order], axis=1)

    def from_rel(self, value):
        pieces = self.pieces(value)
        return jnp.concatenate(self.flipped([pieces[m] for m in self.inverse]), axis=1)

    def gather_one(self, value):
        a, b = value[: self.cut], value[self.cut :]
        return a, b, self.swap(a, self.team_lo), self.swap(b, self.team_hi)

    def gather_two(self, a, b, a_lo, b_hi):
        return (
            self.swap(jnp.concatenate([a, a_lo]), self.team_hi),
            self.swap(jnp.concatenate([b, b_hi]), self.team_lo),
        )

    def scatter_one(self, parts):
        parts = parts.reshape(4, parts.shape[0] // 4, -1)
        a, b = parts[:, : self.cut], parts[:, self.cut :]
        a_got = self.swap(a[2:], self.team_hi)
        b_got = self.swap(jnp.stack([b[1], b[3]]), self.team_lo)
        return a[:2], jnp.stack([b[0], b[2]]), a_got, b_got

    def scatter_two(self, a, b, a_got, b_got):
        a_last = self.swap(added(a[1], a_got[1]), self.team_lo)
        b_last = self.swap(added(b[1], b_got[1]), self.team_hi)
        a_sum = a[0].astype(f32) + a_got[0].astype(f32) + a_last.astype(f32)
        b_sum = b[0].astype(f32) + b_got[0].astype(f32) + b_last.astype(f32)
        return jnp.concatenate([a_sum, b_sum])

    def octet(self, value):
        value = value.reshape(8, self.shard, -1)
        return lax.all_to_all(value, AXES, 0, 0, axis_index_groups=self.groups)

    def joined(self, *blocks):
        whole = jnp.concatenate(blocks)
        for bit in self.gather[2:]:
            whole = jnp.concatenate([whole, self.swap(whole, bit)])
        return whole

    def first_sum(self, mine, others_swapped):
        block = added(mine, others_swapped)
        for bit in reversed(self.gather[2:]):
            block = block.reshape(2, block.shape[0] // 2, -1)
            block = added(block[0], self.swap(block[1], bit))
        return block.reshape(4, 8 * self.shard, -1)


def on_device(
    plan, layer_input, frame_real, gain_attn, w_qkv, w_out, gain_mlp, w_up, w_down, cotangent
):
    rows = layer_input.shape[1]
    width = layer_input.shape[2]
    shard = w_up.shape[0]
    space = plan.space
    me = lax.axis_index("tm") * space + lax.axis_index("space")
    inputs = layer_input[0].astype(f32)
    grad_out = cotangent[0].astype(f32)
    swap = plan.swap
    attn = Side(plan, me, plan.team, plan.gather, plan.octets, shard, width, rows, rows * 3 // 8)
    feed = Side(
        plan, me, plan.feed_team, plan.feed_gather, None, shard, width, rows, rows // 2
    )

    def has(bit):
        return (me & bit) != 0

    gain_one = gain_attn.astype(f32)[:, None]
    gain_two = gain_mlp.astype(f32)[:, None]
    qkv_scaled = (w_qkv.astype(f32) * gain_one).astype(bf16)
    n_ff = w_up.shape[1] // 8
    qkv_sent = (
        qkv_scaled.reshape(shard, 3, 2, 2, 2, 2, HEAD)
        .transpose(2, 5, 3, 0, 4, 1, 6)
        .reshape(8, shard, 6 * HEAD)
    )
    qkv_columns = [
        (
            4 * hi + 2 * lo + c,
            (3 * jj + i) * HEAD,
            (3 * jj + i + 1) * HEAD,
            (i * HEADS + 8 * hi + 4 * c + 2 * jj + lo) * HEAD,
        )
        for hi in range(2)
        for lo in range(2)
        for c in range(2)
        for jj in range(2)
        for i in range(3)
    ]
    mine = jnp.where(has(feed.team_hi), 4, 0) + jnp.where(has(feed.team_lo), 2, 0)
    mine = mine + jnp.where(has(1), 1, 0)
    codes = [(4 * hi, 2 * lo, c) for hi in range(2) for lo in range(2) for c in range(2)]

    def placed(*axes):
        ranked = sorted(codes, key=lambda code: [code[i] for i in axes])
        return jnp.array([sum(code) for code in ranked], jnp.int32) ^ mine

    by_lo_core_hi, by_hi_core_lo, by_core_lo_hi = placed(1, 2, 0), placed(0, 2, 1), placed(2, 1, 0)
    by_hi_lo_core = placed(0, 1, 2)
    feed_sent = spread(by_lo_core_hi, w_up, w_down, gain_two)

    qkv_sent, tokens = tied(qkv_sent, layer_input[0])
    first_rel = attn.to_rel(tokens, True)
    grad_rel = feed.to_rel(cotangent[0], False)
    qkv_block = attn.octet(qkv_sent).reshape(8 * shard, -1)
    feed_lo = swap(feed_sent[4:], feed.team_lo)
    qkv_block, first_rel, grad_rel, feed_sent, feed_lo, w_out = tied(
        qkv_block, first_rel, grad_rel, feed_sent, feed_lo, w_out
    )
    first_near = attn.gather_one(first_rel)
    qkv_first = swap(qkv_block, attn.first)
    qkv_second = swap(qkv_block, attn.second)
    feed_core = swap(jnp.stack([feed_sent[2:4], feed_lo[2:]]), 1)
    feed_kept = jnp.stack([jnp.stack([feed_sent[:2], feed_lo[:2]]), feed_core])
    up_send = feed_kept[:, :, 1, :, :n_ff].reshape(4, shard, n_ff)
    qkv_first, qkv_second, feed_kept, up_send, first_near, w_out = tied(
        qkv_first, qkv_second, feed_kept, up_send, first_near, w_out
    )
    qkv_both = swap(qkv_first, attn.second)
    first_far = attn.gather_two(*first_near)
    out_z = swap(w_out, attn.first)
    up_got = swap(up_send, feed.team_hi)
    down_send = feed_kept[:, :, 1, :, n_ff:].reshape(4, shard, n_ff)
    up_kept = feed_kept[:, :, 0, :, :n_ff].reshape(4, shard, n_ff)
    qkv_both, first_far, up_got, up_kept, down_send, feed_kept, out_z, w_out, grad_rel = tied(
        qkv_both, first_far, up_got, up_kept, down_send, feed_kept, out_z, w_out, grad_rel
    )
    down_got = swap(down_send, feed.team_hi)
    qkv_mine = attn.joined(qkv_block, qkv_first, qkv_second, qkv_both)
    qkv_other = swap(qkv_mine, 1)
    first_all = team_rows(*first_near, *first_far)
    up_block = settle(by_hi_core_lo, up_kept, up_got)
    n_block = up_block.shape[0]
    half = n_block // 2
    up_za = swap(up_block[:half], feed.first)
    up_x = swap(up_block, feed.second)

    team_device = me ^ jnp.array(plan.team_rel, jnp.int32)
    row_index = jnp.arange(rows, dtype=jnp.int32)
    positions = (
        ((team_device // space) % plan.clip * (space * rows) + (team_device % space) * rows)[:, None]
        + row_index[None, :]
    ).reshape(4 * rows)
    half_dim = HEAD // 2
    inverse_freq = jnp.exp(-jnp.log(10000.0) * jnp.arange(half_dim, dtype=f32) * 2.0 / HEAD)
    angles = positions.astype(f32)[:, None] * inverse_freq[None, :]
    angles = jnp.concatenate([angles, angles], axis=-1)
    cosine, sine = jnp.cos(angles), jnp.sin(angles)

    def rotate(value):
        turned = jnp.concatenate([-value[:, half_dim:], value[:, :half_dim]], axis=-1)
        return value * cosine + turned * sine

    def rotate_back(value):
        scaled = value * sine
        turned = jnp.concatenate([scaled[:, half_dim:], -scaled[:, :half_dim]], axis=-1)
        return value * cosine + turned

    def head_triples(mixed):
        found = []
        for j in range(2):
            q, k, v = (
                mixed[:, (3 * j + i) * HEAD : (3 * j + i + 1) * HEAD] for i in range(3)
            )
            found.append(
                jnp.concatenate([rotate(q) * to_log2, rotate(k), v], axis=1).astype(bf16)
            )
        return found

    mixed_mine = matmul(first_all, qkv_mine)
    mixed_other = matmul(first_all, qkv_other)
    stack = jnp.stack(head_triples(mixed_mine) + head_triples(mixed_other))
    my_head = jnp.where(has(plan.heads[0]), 2, 0) + jnp.where(has(plan.heads[1]), 1, 0)
    core_flip = jnp.where(has(1), 2, 0)
    pick = [(my_head ^ r) ^ core_flip for r in range(4)]
    sent = [lax.dynamic_index_in_dim(stack, pick[r], 0, keepdims=False) for r in range(4)]
    out_pair = jnp.stack([w_out, out_z])
    sent, up_za, up_x, grad_rel, up_block, up_half, down_got, out_z, w_out, out_pair = tied(
        sent, up_za, up_x, grad_rel, up_block, up_block[half:], down_got, out_z, w_out, out_pair
    )
    got = [swap(sent[r], plan.head_rel[r]) for r in range(1, 4)]
    up_zb = swap(up_half, feed.first)
    out_x = swap(out_pair, attn.second)
    cut_z = [0, n_block // 2, n_block * 3 // 4, n_block]
    down_kept = feed_kept[:, :, 0, :, n_ff:].reshape(4, shard, n_ff)
    down_block = settle(by_hi_core_lo, down_kept, down_got)
    got, up_za, up_zb, down_block, grad_rel, out_x, down_first = tied(
        got, up_za, up_zb, down_block, grad_rel, out_x, down_block[: cut_z[1]]
    )
    own = jnp.stack([sent[0]] + got).reshape(16, rows, 3 * HEAD)
    down_z = [swap(down_first, feed.first)]
    up_both = [swap(up_za, feed.second), swap(up_zb, feed.second)]
    grad_near = feed.gather_one(grad_rel)
    shared = own[:, :, HEAD:]
    other = jnp.stack([swap(shared, rel) for rel in plan.part_rel[1:]])

    block_rel = jnp.array(plan.block_rel, jnp.int32)
    tile_rel = jnp.array(plan.block_rel[:: plan.tile_blocks], jnp.int32)
    tile_slot = (me ^ tile_rel) // space
    no_more = jnp.zeros((16 - tile_slot.shape[0],), jnp.int32)
    info = jnp.concatenate(
        [
            jnp.stack([me, (me % space) * rows, ((me ^ plan.team[1]) % space) * rows]),
            jnp.zeros((5,), jnp.int32),
            block_rel,
            tile_slot,
            no_more,
            tile_slot // plan.clip * plan.clip,
            no_more,
        ]
    ).astype(jnp.int32)

    attended, attended_t, log_total, keys, values = attend(plan, info, frame_real, own, other)
    w_team = jnp.stack([w_out, out_x[0], out_z, out_x[1]])
    attended, down_z, up_both, grad_near, w_team, down_block, up_x, up_za, up_zb, up_block = tied(
        attended, down_z, up_both, grad_near, w_team, down_block, up_x, up_za, up_zb, up_block
    )
    w_got = swap(w_team, plan.parts[-1])
    attended = attended.reshape(4, 4 * rows, HEAD)
    heads_got = [swap(attended[r], plan.head_rel[r]) for r in range(1, 4)]
    down_z += [swap(down_block[cut_z[1] : cut_z[2]], feed.first)]
    up_mine = feed.joined(up_block, up_za, up_zb, up_x, *up_both)
    for bit in reversed(plan.parts):
        w_got = w_got if bit == plan.parts[-1] else swap(w_team, bit)
        w_team = jnp.where(
            has(bit),
            jnp.concatenate([w_got, w_team], axis=1),
            jnp.concatenate([w_team, w_got], axis=1),
        )
    w_team = w_team.reshape(4 * HEAD, width)
    heads_got, w_team, down_z, grad_near, down_block, up_mine = tied(
        heads_got, w_team, down_z, grad_near, down_block, up_mine
    )
    attended_team = jnp.concatenate([attended[0]] + heads_got, axis=1)
    branch = matmul(attended_team, w_team).astype(bf16)
    branch_near = attn.scatter_one(branch)
    cut_x = n_block * 5 // 8
    down_x = [swap(down_block[:cut_x], feed.second)]
    grad_far = feed.gather_two(*grad_near)
    branch_near, down_x, up_mine, down_z, grad_far, down_block = tied(
        branch_near, down_x, up_mine, down_z, grad_far, down_block
    )
    middle = attn.scatter_two(*branch_near)
    down_x += [swap(down_block[cut_x:], feed.second)]
    up_other = swap(up_mine, 1)
    grad_all = team_rows(*grad_near, *grad_far)
    middle, down_x, down_z, down_block, up_other, grad_all = tied(
        middle, down_x, down_z, down_block, up_other, grad_all
    )
    middle = inputs + middle
    second_near = feed.gather_one(feed.to_rel(middle, True))
    down_z += [swap(down_block[cut_z[2] :], feed.first)]
    cut_both = n_block * 5 // 16
    down_both = [swap(down_z[0][:cut_both], feed.second)]
    second_near, down_both, down_z = tied(second_near, down_both, down_z)
    second_far = feed.gather_two(*second_near)
    down_z = jnp.concatenate(down_z)
    down_both += [swap(down_z[cut_both:], feed.second)]
    second_far, down_both, down_z = tied(second_far, down_both, down_z)
    down_mine = feed.joined(down_block, down_z, *down_x, *down_both)
    down_other = swap(down_mine, 1)
    second_all = team_rows(*second_near, *second_far)
    normed_two, scale_two = layer_norm(middle)
    gelu = functools.partial(jax.nn.gelu, approximate=True)
    hidden_other = matmul(second_all, up_other)
    hidden_mine = matmul(second_all, up_mine)
    act_other = gelu(hidden_other).astype(bf16)
    act_mine = gelu(hidden_mine).astype(bf16)
    down_other_grad = matmul(grad_all, act_other, ((0,), (0,))).astype(bf16)
    down_other_grad, down_other, down_mine, act_mine, act_other = tied(
        down_other_grad, down_other, down_mine, act_mine, act_other
    )
    down_swapped = swap(down_other_grad, 1)
    down_mine_grad = matmul(grad_all, act_mine, ((0,), (0,))).astype(bf16)

    def back(hidden, down):
        return jax.vjp(gelu, hidden)[1](matmul(grad_all, down))[0].astype(bf16)

    hid_mine, hid_other = back(hidden_mine, down_mine), back(hidden_other, down_other)
    second_parts = matmul(hid_mine, up_mine, ((1,), (1,))) + matmul(hid_other, up_other, ((1,), (1,)))
    second_parts, hid_mine, hid_other, down_swapped, down_mine_grad = tied(
        second_parts.astype(bf16), hid_mine, hid_other, down_swapped, down_mine_grad
    )
    second_back = feed.scatter_one(second_parts)
    down_sum = feed.first_sum(down_mine_grad, down_swapped)
    c1, c2, c3 = n_block * 3 // 8, n_block * 3 // 4, n_block * 3 // 8
    down_x3 = [swap(down_sum[3][:c1], feed.second)]
    out_parts = (
        matmul(act_mine, down_mine, ((1,), (1,))) + matmul(act_other, down_other, ((1,), (1,)))
    ).astype(bf16)
    second_back, down_x3, down_sum, out_parts, hid_other = tied(
        second_back, down_x3, down_sum, out_parts, hid_other
    )
    grad_second = feed.scatter_two(*second_back)
    z1, z2 = n_block * 3 // 16, n_block * 3 // 8
    down_z1 = [swap(added(down_sum[1][:z1], down_x3[0][:z1]), feed.first)]
    down_x3 += [swap(down_sum[3][c1:c2], feed.second)]
    up_other_grad = matmul(second_all, hid_other, ((0,), (0,))).astype(bf16)
    down_x32 = jnp.concatenate([down_sum[3][c2:], down_sum[2][:c3]])
    grad_second, down_z1, down_x3, down_sum, up_other_grad, down_x32, hid_mine = tied(
        grad_second, down_z1, down_x3, down_sum, up_other_grad, down_x32, hid_mine
    )
    grad_second = feed.from_rel(grad_second)
    grad_middle = grad_out + layer_norm_back(grad_second, normed_two, scale_two)
    middle_near = attn.gather_one(grad_middle.astype(bf16))
    down_x32 = swap(down_x32, feed.second)
    up_swapped = swap(up_other_grad, 1)
    middle_near, down_x32, up_swapped, hid_mine, down_sum, down_x3, down_x2 = tied(
        middle_near, down_x32, up_swapped, hid_mine, down_sum, down_x3, down_sum[2][c3:]
    )
    middle_far = attn.gather_two(*middle_near)
    down_x3 = jnp.concatenate([*down_x3, down_x32[: n_block - c2]])
    down_x2 = [down_x32[n_block - c2 :], swap(down_x2, feed.second)]
    up_mine_grad = matmul(second_all, hid_mine, ((0,), (0,))).astype(bf16)
    down_z1b = added(down_sum[1][z1:z2], down_x3[z1:z2])
    middle_far, up_swapped, up_mine_grad, down_x2, down_x3, down_sum, down_z1b = tied(
        middle_far, up_swapped, up_mine_grad, down_x2, down_x3, down_sum, down_z1b
    )
    middle_all = team_rows(*middle_near, *middle_far)
    grad_heads = matmul(middle_all, w_team, ((1,), (1,))).astype(bf16)
    grad_own = grad_heads[:, :HEAD]
    grad_got = [
        swap(grad_heads[:, r * HEAD : (r + 1) * HEAD], plan.head_rel[r]) for r in range(1, 4)
    ]
    down_z1 += [swap(down_z1b, feed.first)]
    out_grad = matmul(attended_team, middle_all, ((0,), (0,))).astype(bf16).reshape(4, HEAD, width)
    up_sum = feed.first_sum(up_mine_grad, up_swapped)
    down_z1c = added(down_sum[1][z2:], down_x3[z2:])
    grad_got, up_sum, out_grad, down_z1, down_z1c, out_parts = tied(
        grad_got, up_sum, out_grad, down_z1, down_z1c, out_parts
    )
    up_x3 = swap(up_sum[3], feed.second)
    down_z1 += [swap(down_z1c, feed.first)]
    out_near = feed.scatter_one(out_parts)
    for bit in plan.parts:
        lower, upper = jnp.split(out_grad, 2, axis=1)
        kept = jnp.where(has(bit), upper, lower)
        out_grad = added(kept, swap(jnp.where(has(bit), lower, upper), bit))
    dq, dkv_own, dkv_other = attend_back(
        plan,
        info,
        frame_real,
        own,
        keys,
        values,
        jnp.stack([grad_own] + grad_got).reshape(16, rows, HEAD),
        attended_t,
        log_total,
    )
    dq, dkv_own, dkv_other, up_x3, down_z1, out_near, out_grad = tied(
        dq, dkv_own, dkv_other, up_x3, down_z1, out_near, out_grad
    )
    dkv = dkv_own.astype(f32)
    for i, rel in enumerate(plan.part_rel[1:]):
        dkv = dkv + swap(dkv_other[i], rel).astype(f32)
    triple = jnp.concatenate([dq, dkv.astype(bf16)], axis=2).reshape(4, 4 * rows, 3 * HEAD)
    up_z1 = added(up_sum[1], up_x3)
    triple, up_sum, up_z1, up_z1a, down_z1 = tied(triple, up_sum, up_z1, up_z1[:half], down_z1)
    got = [swap(triple[r], plan.head_rel[r]) for r in range(1, 4)]
    up_z1a = swap(up_z1a, feed.first)
    down_done = added(down_sum[0], jnp.concatenate(down_x2), jnp.concatenate(down_z1))
    down_rows, down_rows_hi = unsettle(by_hi_lo_core, down_done)
    got, up_z1a, up_z1, down_rows, down_rows_hi, up_sum, out_grad, out_near = tied(
        got, up_z1a, up_z1, down_rows, down_rows_hi, up_sum, out_grad, out_near
    )
    places = (my_head ^ jnp.arange(4, dtype=jnp.int32)) ^ core_flip
    mixed_grad = turn_back(places, cosine, sine, [triple[0]] + got)
    mixed_grad_mine, mixed_grad_other = mixed_grad[0], mixed_grad[1]
    qkv_other_grad = matmul(first_all, mixed_grad_other, ((0,), (0,))).astype(bf16)
    out_sum = feed.scatter_two(*out_near)
    kept, sent = out_grad.reshape(2, 2, -1, width)[:, 0], out_grad.reshape(2, 2, -1, width)[:, 1]
    out_grad = added(kept, swap(sent, attn.second))
    down_rows = jnp.stack([down_rows, swap(down_rows_hi, feed.team_hi)]).reshape(2, 2, 2, shard, n_ff)
    qkv_other_grad, mixed_grad_mine, up_sum, down_rows, out_sum, out_grad, up_z1b = tied(
        qkv_other_grad, mixed_grad_mine, up_sum, down_rows, out_sum, out_grad, up_z1[half:]
    )
    qkv_swapped = swap(qkv_other_grad, 1)
    up_x2 = swap(up_sum[2], feed.second)
    up_z1b = swap(up_z1b, feed.first)
    down_rows_lo = swap(down_rows[:, 1], feed.team_lo)
    qkv_mine_grad = matmul(first_all, mixed_grad_mine, ((0,), (0,))).astype(bf16)
    first_parts = matmul(mixed_grad_mine, qkv_mine, ((1,), (1,))) + matmul(
        mixed_grad_other, qkv_other, ((1,), (1,))
    )
    qkv_sum = attn.first_sum(qkv_mine_grad, qkv_swapped)
    qkv_sum, first_parts, up_x2, up_sum, up_z1b, down_rows, out_grad = tied(
        qkv_sum,
        first_parts.astype(bf16),
        up_x2,
        up_sum,
        up_z1b,
        jnp.stack([down_rows[:, 0], down_rows_lo]),
        out_grad,
    )
    qkv_x3 = swap(qkv_sum[3], attn.second)
    first_back = attn.scatter_one(first_parts)
    up_done = added(up_sum[0], up_x2, jnp.concatenate([up_z1a, up_z1b]))
    down_rows = jnp.stack([down_rows[:, :, 0], swap(down_rows[:, :, 1], 1)])
    up_rows, up_rows_hi = unsettle(by_hi_lo_core, up_done)
    up_rows = jnp.stack([up_rows, swap(up_rows_hi, feed.team_hi)]).reshape(2, 2, 2, shard, n_ff)
    qkv_x3, first_back, up_rows, qkv_sum, down_rows, up_send = tied(
        qkv_x3, first_back, up_rows, qkv_sum, down_rows, up_rows[:, 1]
    )
    qkv_z1 = swap(added(qkv_sum[1], qkv_x3), attn.first)
    qkv_x2 = swap(qkv_sum[2], attn.second)
    first_rows = attn.scatter_two(*first_back)
    output = (middle + feed.from_rel(out_sum)).astype(bf16)
    grad_down, _ = restore(False, by_core_lo_hi, down_rows.reshape(8, shard, n_ff), w_down, gain_two)
    up_rows = jnp.stack([up_rows[:, 0], swap(up_send, feed.team_lo)])
    qkv_z1, qkv_x2, first_rows, out_grad, output, up_rows, grad_down = tied(
        qkv_z1, qkv_x2, first_rows, out_grad, output, up_rows, grad_down
    )
    up_rows = jnp.stack([up_rows[:, :, 0], swap(up_rows[:, :, 1], 1)])
    grad_up, grad_gain_two = restore(
        True, by_core_lo_hi, up_rows.reshape(8, shard, n_ff), w_up, gain_two
    )
    qkv_got = attn.octet(added(qkv_sum[0], qkv_x2, qkv_z1))
    grad_first = attn.from_rel(first_rows)
    grad_inputs = grad_middle + layer_norm_back(grad_first, *layer_norm(inputs))
    out_grad = out_grad[0].astype(f32) + swap(out_grad[1], attn.first).astype(f32)
    grad_qkv, grad_gain_one = deliver(qkv_columns, qkv_got, w_qkv, gain_one)
    return (
        output[None],
        grad_inputs[None],
        grad_gain_one[:, 0],
        grad_qkv,
        out_grad,
        grad_gain_two[:, 0],
        grad_up,
        grad_down,
    )


def solution(mesh):
    plan = Plan(mesh.shape["tm"], mesh.shape["space"], BLOCK)
    tokens = P("tm", "space", None)
    line = P(("tm", "space"))
    table = P(("tm", "space"), None)
    return jax.shard_map(
        functools.partial(on_device, plan),
        mesh=mesh,
        in_specs=(tokens, P(), line, table, table, line, table, table, tokens),
        out_specs=(tokens, tokens, line, table, table, line, table, table),
        check_vma=False,
    )
```

```python
import functools

import jax
import jax.numpy as jnp
import numpy as np
from jax import lax
from jax.experimental import pallas as pl
from jax.experimental.pallas import tpu as pltpu
from jax.sharding import PartitionSpec as P

HEADS = 16
HEAD = 128
AXES = ("tm", "space")
BLOCK = 128

epsilon = 1e-05
masked_value = -1e30
inv_root = HEAD ** (-0.5)
to_log2 = inv_root * 1.4426950408889634
q_unscale = inv_root / to_log2

bf16 = jnp.bfloat16
f32 = jnp.float32


def matmul(left, right, dims=((1,), (0,))):
    return lax.dot_general(left, right, (dims, ((), ())), preferred_element_type=f32)


def tied(*values):
    return lax.optimization_barrier(values)


class Plan:
    def __init__(self, tm, space, frame_rows):
        self.count = tm * space
        self.space = space
        self.slots = tm
        self.clip = min(16, tm)
        count = self.count
        self.team = (count // 2, count // 16)
        self.heads = (count // 4, count // 8)
        self.feed_team = (count // 4, count // 16)
        bits = [1 << i for i in range(count.bit_length() - 1)]
        taken = set(self.team + self.heads)
        self.parts = [b for b in reversed(bits) if b not in taken]
        rest = [b for b in self.parts if b != 1]
        self.gather = [*self.heads, *rest]
        self.feed_gather = [count // 2, count // 8, *rest]
        self.team_rel = [0, self.team[1], self.team[0], self.team[0] | self.team[1]]
        self.head_rel = [0, self.heads[1], self.heads[0], self.heads[0] | self.heads[1]]
        self.block_rel = [h | t for h in self.head_rel for t in self.team_rel]
        self.part_rel = [
            sum(b for j, b in enumerate(self.parts) if (i >> j) & 1)
            for i in range(1 << len(self.parts))
        ]
        devices = range(count)
        self.octets = self.groups(sum(self.team) | 1)
        self.tile_blocks = 2 if self.team[1] < space else 1
        self.devices = devices

    def groups(self, mask):
        held = {}
        for d in range(self.count):
            held.setdefault(d & ~mask, []).append(d)
        return list(held.values())

    def swap(self, value, mask):
        return lax.ppermute(value, AXES, [(d, d ^ mask) for d in self.devices])


def layer_norm(values):
    center = jnp.mean(values, axis=-1, keepdims=True)
    shifted = values - center
    spread = jnp.mean(shifted * shifted, axis=-1, keepdims=True)
    scale = lax.rsqrt(spread + epsilon)
    return shifted * scale, scale


def layer_norm_back(grads, normed, scale):
    inner = jnp.mean(grads * normed, axis=-1, keepdims=True)
    return (grads - jnp.mean(grads, axis=-1, keepdims=True) - normed * inner) * scale


def transposed(tile):
    return tile.astype(f32).T.astype(tile.dtype)


def attend_kernel(plan, info, real, own, other, out, out_t, lse, keys, values, values_t):
    me = info[0]
    n_blocks = len(plan.block_rel)
    for part, part_rel in enumerate(plan.part_rel):

        def place(b, _, part=part, part_rel=part_rel):
            home = me ^ part_rel ^ info[8 + b]
            if part == 0:
                key, value = own[b, :, HEAD : 2 * HEAD], own[b, :, 2 * HEAD :]
            else:
                key, value = other[part - 1, b, :, :HEAD], other[part - 1, b, :, HEAD:]
            rows = pl.ds(pl.multiple_of(home * BLOCK, BLOCK), BLOCK)
            keys[rows, :] = key
            values[rows, :] = value
            values_t[home] = transposed(value)
            return 0

        lax.fori_loop(0, n_blocks, place, 0, unroll=4)

    frame = plan.space * BLOCK
    per_tile = plan.tile_blocks
    two = per_tile * BLOCK
    lane = lax.broadcasted_iota(jnp.int32, (1, two), 1)
    q_place = jnp.where(lane < BLOCK, info[1] + lane, info[2] + lane - BLOCK)

    def tile(i, _):
        slot, first = info[24 + i], info[40 + i]
        q = jnp.concatenate([own[per_tile * i + j, :, :HEAD] for j in range(per_tile)], axis=0)

        def scores(g):
            key = keys[pl.ds(pl.multiple_of(g * frame, frame), frame), :]
            return matmul(key, q, ((1,), (1,)))

        def value_t(g):
            return jnp.concatenate(
                [values_t[g * plan.space + s] for s in range(plan.space)], axis=1
            )

        def fold(carry, s, g):
            top, total, acc = carry
            new = jnp.maximum(top, jnp.max(s, axis=0, keepdims=True))
            fade = jnp.exp2(top - new)
            p = jnp.exp2(s - new)
            total = total * fade + jnp.sum(p, axis=0, keepdims=True)
            acc = acc * fade + matmul(value_t(g), p.astype(bf16))
            return new, total, acc

        def step(g, carry):
            ahead = scores(g + 1)
            s = carry[3] + jnp.where(real[g] > 0, 0.0, masked_value)
            return (*fold(carry[:3], s, g), ahead)

        first = jnp.where(real[slot] > 0, first, slot)
        start = (
            jnp.full((1, two), masked_value, f32),
            jnp.zeros((1, two), f32),
            jnp.zeros((HEAD, two), f32),
            scores(first),
        )
        *carry, s = lax.fori_loop(first, slot, step, start)
        k_place = lax.broadcasted_iota(jnp.int32, (frame, two), 0)
        top, total, acc = fold(carry, jnp.where(k_place <= q_place, s, masked_value), slot)
        lse[i] = top + jnp.log2(total)
        acc = acc / total
        out_t[i] = acc
        back = acc.T.astype(bf16)
        for j in range(per_tile):
            out[per_tile * i + j] = back[j * BLOCK : (j + 1) * BLOCK]
        return 0

    lax.fori_loop(0, n_blocks // per_tile, tile, 0)


def attend_back_kernel(
    plan, info, real, own, keys, values, grads, out_t, lse, dq, dkv_own, dkv_other, dk, dv, keys_t
):
    me = info[0]
    n_blocks = len(plan.block_rel)

    def clear(b, _):
        rows = pl.ds(pl.multiple_of(b * BLOCK, BLOCK), BLOCK)
        dk[rows, :] = jnp.zeros((BLOCK, HEAD), f32)
        dv[rows, :] = jnp.zeros((BLOCK, HEAD), f32)
        keys_t[b] = transposed(keys[rows, :])
        return 0

    lax.fori_loop(0, plan.count, clear, 0, unroll=4)

    frame = plan.space * BLOCK
    per_tile = plan.tile_blocks
    two = per_tile * BLOCK
    lane = lax.broadcasted_iota(jnp.int32, (1, two), 1)
    q_place = jnp.where(lane < BLOCK, info[1] + lane, info[2] + lane - BLOCK)

    def tile(i, _):
        slot, first = info[24 + i], info[40 + i]
        q = jnp.concatenate([own[per_tile * i + j, :, :HEAD] for j in range(per_tile)], axis=0)
        do = jnp.concatenate([grads[per_tile * i + j] for j in range(per_tile)], axis=0)
        delta = jnp.sum(do.astype(f32).T * out_t[i], axis=0, keepdims=True)
        log_total = lse[i]

        def turn(g, mask):
            rows = pl.ds(pl.multiple_of(g * frame, frame), frame)
            key, value = keys[rows, :], values[rows, :]
            s = matmul(key, q, ((1,), (1,)))
            dp = matmul(value, do, ((1,), (1,)))
            if mask:
                p = jnp.exp2(s - log_total)
            else:
                p = jnp.exp2(s - jnp.where(real[g] > 0, log_total, -masked_value))
            if mask:
                k_place = lax.broadcasted_iota(jnp.int32, (frame, two), 0)
                p = jnp.where(k_place <= q_place, p, 0.0)
            ds = (p * (dp - delta)).astype(bf16)
            dv[rows, :] += matmul(p.astype(bf16), do)
            dk[rows, :] += matmul(ds, q)
            key_t = jnp.concatenate(
                [keys_t[g * plan.space + s] for s in range(plan.space)], axis=1
            )
            return matmul(key_t, ds)

        def step(g, dq_t):
            return dq_t + turn(g, False)

        first = jnp.where(real[slot] > 0, first, slot)
        dq_t = lax.fori_loop(first, slot, step, turn(slot, True))
        back = (dq_t * inv_root).T.astype(bf16)
        for j in range(per_tile):
            dq[per_tile * i + j] = back[j * BLOCK : (j + 1) * BLOCK]
        return 0

    lax.fori_loop(0, n_blocks // per_tile, tile, 0)

    for part, part_rel in enumerate(plan.part_rel):

        def hand_out(b, _, part=part, part_rel=part_rel):
            home = me ^ part_rel ^ info[8 + b]
            rows = pl.ds(pl.multiple_of(home * BLOCK, BLOCK), BLOCK)
            pair = jnp.concatenate([dk[rows, :] * q_unscale, dv[rows, :]], axis=1).astype(bf16)
            if part == 0:
                dkv_own[b] = pair
            else:
                dkv_other[part - 1, b] = pair
            return 0

        lax.fori_loop(0, n_blocks, hand_out, 0, unroll=4)


def call(kernel, n_scalar, n_in, outs, scratch, cost, room=16):
    return pl.pallas_call(
        kernel,
        out_shape=outs,
        in_specs=[pl.BlockSpec(memory_space=pltpu.SMEM)] * n_scalar
        + [pl.BlockSpec(memory_space=pltpu.VMEM)] * n_in,
        out_specs=tuple(pl.BlockSpec(memory_space=pltpu.VMEM) for _ in outs),
        scratch_shapes=scratch,
        cost_estimate=cost,
        compiler_params=pltpu.CompilerParams(vmem_limit_bytes=room << 20),
    )


def moving(n_bytes):
    return pl.CostEstimate(flops=n_bytes, bytes_accessed=n_bytes, transcendentals=0)


def arrange_kernel(normed, chunk, lanes, value, out, held):
    x = value[...].astype(f32)
    if normed:
        x = layer_norm(x)[0]
    held[...] = x.astype(bf16)
    for j in range(x.shape[1] // chunk):
        at = pl.multiple_of(lanes[j], chunk)
        out[:, j * chunk : (j + 1) * chunk] = held[:, pl.ds(at, chunk)]


def arrange(normed, chunk, lanes, value):
    shape = value.shape
    return call(
        functools.partial(arrange_kernel, normed, chunk),
        1,
        1,
        (jax.ShapeDtypeStruct(shape, bf16),),
        [pltpu.VMEM(shape, bf16)],
        moving(4 * value.size),
    )(lanes, value)[0]


def team_rows_kernel(a, b, a_lo, b_hi, a_far, b_far, out):
    one, two = a.shape[0], b.shape[0]
    pieces = (a[...], b[...], a_lo[...], b_far[:two], a_far[:one], b_hi[...], a_far[one:], b_far[two:])
    start = 0
    for piece in pieces:
        out[start : start + piece.shape[0]] = piece
        start += piece.shape[0]


def team_rows(*pieces):
    rows, width = pieces[0].shape[0] + pieces[1].shape[0], pieces[0].shape[1]
    return call(
        team_rows_kernel,
        0,
        6,
        (jax.ShapeDtypeStruct((4 * rows, width), bf16),),
        [],
        moving(16 * rows * width),
    )(*pieces)[0]


def turn_back_kernel(places, cosine, sine, *refs):
    heads, out = refs[:4], refs[4]
    half_dim = HEAD // 2
    cos, sin = cosine[...], sine[...]
    for r in range(4):
        found = []
        for i in range(2):
            t = heads[r][:, i * HEAD : (i + 1) * HEAD].astype(f32)
            scaled = t * sin
            turned = jnp.concatenate([scaled[:, half_dim:], -scaled[:, :half_dim]], axis=-1)
            found.append((t * cos + turned).astype(bf16))
        found.append(heads[r][:, 2 * HEAD :])
        whole = jnp.concatenate(found, axis=1)
        place = places[r]

        @pl.when(place % 2 == 0)
        def _():
            out[place // 2, :, : 3 * HEAD] = whole

        @pl.when(place % 2 == 1)
        def _():
            out[place // 2, :, 3 * HEAD :] = whole


def turn_back(places, cosine, sine, heads):
    rows = cosine.shape[0]
    return call(
        turn_back_kernel,
        1,
        6,
        (jax.ShapeDtypeStruct((2, rows, 6 * HEAD), bf16),),
        [],
        moving(8 * rows * 3 * HEAD * 2),
    )(places, cosine, sine, *heads)[0]


def deal_kernel(columns, weight, gain, out):
    for block, start, end, target in columns:
        value = weight[:, target : target + end - start].astype(f32) * gain[...]
        out[block, :, start:end] = value.astype(bf16)


def deal(columns, weight, gain):
    rows, width = weight.shape
    return call(
        functools.partial(deal_kernel, columns),
        0,
        2,
        (jax.ShapeDtypeStruct((8, rows, width // 8), bf16),),
        [],
        moving(4 * rows * width),
    )(weight, gain)[0]


def deliver_kernel(columns, got, weight, gain, out, gain_grad):
    total = None
    for block, start, end, target in columns:
        value = got[block, :, start:end].astype(f32)
        span = slice(target, target + end - start)
        part = jnp.sum(value * weight[:, span].astype(f32), axis=1, keepdims=True)
        total = part if total is None else total + part
        out[:, span] = value * gain[...]
    gain_grad[...] = jnp.broadcast_to(total, gain_grad.shape)


def deliver(columns, got, weight, gain):
    rows, width = weight.shape
    return call(
        functools.partial(deliver_kernel, columns),
        0,
        3,
        (jax.ShapeDtypeStruct((rows, width), f32), jax.ShapeDtypeStruct((rows, 128), f32)),
        [],
        moving(8 * rows * width),
    )(got, weight, gain)


def spread_kernel(places, up, down, gain, out):
    n = out.shape[2] // 2
    for i in range(8):
        at = pl.ds(pl.multiple_of(places[i] * n, n), n)
        out[i, :, :n] = (up[:, at].astype(f32) * gain[...]).astype(bf16)
        out[i, :, n:] = down[:, at]


def spread(places, up, down, gain):
    rows, width = up.shape
    return call(
        spread_kernel,
        1,
        3,
        (jax.ShapeDtypeStruct((8, rows, width // 4), bf16),),
        [],
        moving(8 * rows * width),
    )(places, up, down, gain)[0]


def settle_kernel(places, kept, got, out):
    rows = kept.shape[1]
    for i in range(8):
        at = pl.ds(pl.multiple_of(places[i] * rows, rows), rows)
        out[at, :] = kept[i] if i < 4 else got[i - 4]


def settle(places, kept, got):
    _, rows, n = kept.shape
    return call(
        settle_kernel,
        1,
        2,
        (jax.ShapeDtypeStruct((8 * rows, n), bf16),),
        [],
        moving(32 * rows * n),
    )(places, kept, got)[0]


def unsettle_kernel(places, block, kept, sent):
    rows = kept.shape[1]
    for i in range(8):
        value = block[pl.ds(pl.multiple_of(places[i] * rows, rows), rows), :]
        if i < 4:
            kept[i] = value
        else:
            sent[i - 4] = value


def unsettle(places, block):
    rows, n = block.shape[0] // 8, block.shape[1]
    half = jax.ShapeDtypeStruct((4, rows, n), bf16)
    return call(unsettle_kernel, 1, 1, (half, half), [], moving(32 * rows * n))(places, block)


def restore_kernel(with_gain, places, got, weight, gain, out, gain_grad):
    n = got.shape[2]
    total = None
    for i in range(8):
        at = pl.ds(pl.multiple_of(places[i] * n, n), n)
        value = got[i].astype(f32)
        if with_gain:
            part = jnp.sum(value * weight[:, at].astype(f32), axis=1, keepdims=True)
            total = part if total is None else total + part
            value = value * gain[...]
        out[:, at] = value
    if with_gain:
        gain_grad[...] = jnp.broadcast_to(total, gain_grad.shape)
    else:
        gain_grad[...] = jnp.zeros(gain_grad.shape, f32)


def restore(with_gain, places, got, weight, gain):
    rows, width = weight.shape
    return call(
        functools.partial(restore_kernel, with_gain),
        1,
        3,
        (jax.ShapeDtypeStruct((rows, width), f32), jax.ShapeDtypeStruct((rows, 128), f32)),
        [],
        moving(8 * rows * width),
    )(places, got, weight, gain)


def attend(plan, info, real, own, other):
    blocks = len(plan.block_rel)
    tokens = plan.count * BLOCK
    work = blocks * BLOCK * min(plan.clip * plan.space * BLOCK, tokens) // 2
    shape = jax.ShapeDtypeStruct
    return call(
        functools.partial(attend_kernel, plan),
        2,
        2,
        (
            shape((blocks, BLOCK, HEAD), bf16),
            shape((blocks // plan.tile_blocks, HEAD, plan.tile_blocks * BLOCK), f32),
            shape((blocks // plan.tile_blocks, 1, plan.tile_blocks * BLOCK), f32),
            shape((tokens, HEAD), bf16),
            shape((tokens, HEAD), bf16),
        ),
        [pltpu.VMEM((plan.count, HEAD, BLOCK), bf16)],
        pl.CostEstimate(flops=8 * work * HEAD, bytes_accessed=8 << 20, transcendentals=work),
        min(56, 8 + plan.count * 3 // 4),
    )(info, real, own, other)


def attend_back(plan, info, real, own, keys, values, grads, out_t, lse):
    blocks = len(plan.block_rel)
    tokens = plan.count * BLOCK
    work = blocks * BLOCK * min(plan.clip * plan.space * BLOCK, tokens) // 2
    shape = jax.ShapeDtypeStruct
    return call(
        functools.partial(attend_back_kernel, plan),
        2,
        6,
        (
            shape((blocks, BLOCK, HEAD), bf16),
            shape((blocks, BLOCK, 2 * HEAD), bf16),
            shape((len(plan.part_rel) - 1, blocks, BLOCK, 2 * HEAD), bf16),
        ),
        [
            pltpu.VMEM((tokens, HEAD), f32),
            pltpu.VMEM((tokens, HEAD), f32),
            pltpu.VMEM((plan.count, HEAD, BLOCK), bf16),
        ],
        pl.CostEstimate(flops=20 * work * HEAD, bytes_accessed=8 << 20, transcendentals=work),
        min(56, 8 + plan.count * 3 // 4),
    )(info, real, own, keys, values, grads, out_t, lse)


def added(*values):
    return sum(v.astype(f32) for v in values).astype(bf16)


class Side:
    def __init__(self, plan, me, team, gather, groups, shard, width, rows, cut):
        self.plan, self.me, self.groups = plan, me, groups
        self.team_hi, self.team_lo = team
        self.gather, self.shard, self.cut = gather, shard, cut
        self.first, self.second = gather[:2]
        low = self.low = min(gather)
        self.chunk = low * shard
        self.n_chunks = width // self.chunk
        self.order = [
            (
                sum(b for j, b in enumerate(gather) if (i >> j) & 1)
                + (self.team_hi if hi else 0)
                + (self.team_lo if lo else 0)
            )
            // low
            for i in range(1 << len(gather))
            for hi in range(2)
            for lo in range(2 if self.team_lo > low else 1)
        ]
        self.inverse = [self.order.index(m) for m in range(self.n_chunks)]
        at = jnp.array(self.order, jnp.int32) ^ ((me & sum(gather)) // low)
        self.lanes = at * self.chunk

    def swap(self, value, bit):
        return self.plan.swap(value, bit)

    def flipped(self, pieces):
        for bit in self.gather:
            step = bit // self.low
            own = (self.me & bit) != 0
            pieces = [jnp.where(own, pieces[m ^ step], pieces[m]) for m in range(self.n_chunks)]
        return pieces

    def pieces(self, value):
        chunk = self.chunk
        return [value[:, m * chunk : (m + 1) * chunk] for m in range(self.n_chunks)]

    def to_rel(self, value, normed):
        if self.chunk % 128 == 0:
            return arrange(normed, self.chunk, self.lanes, value)
        value = layer_norm(value.astype(f32))[0] if normed else value
        pieces = self.flipped(self.pieces(value.astype(bf16)))
        return jnp.concatenate([pieces[m] for m in self.order], axis=1)

    def from_rel(self, value):
        pieces = self.pieces(value)
        return jnp.concatenate(self.flipped([pieces[m] for m in self.inverse]), axis=1)

    def gather_one(self, value):
        a, b = value[: self.cut], value[self.cut :]
        return a, b, self.swap(a, self.team_lo), self.swap(b, self.team_hi)

    def gather_two(self, a, b, a_lo, b_hi):
        return (
            self.swap(jnp.concatenate([a, a_lo]), self.team_hi),
            self.swap(jnp.concatenate([b, b_hi]), self.team_lo),
        )

    def scatter_one(self, parts):
        parts = parts.reshape(4, parts.shape[0] // 4, -1)
        a, b = parts[:, : self.cut], parts[:, self.cut :]
        a_got = self.swap(a[2:], self.team_hi)
        b_got = self.swap(jnp.stack([b[1], b[3]]), self.team_lo)
        return a[:2], jnp.stack([b[0], b[2]]), a_got, b_got

    def scatter_two(self, a, b, a_got, b_got):
        a_last = self.swap(added(a[1], a_got[1]), self.team_lo)
        b_last = self.swap(added(b[1], b_got[1]), self.team_hi)
        a_sum = a[0].astype(f32) + a_got[0].astype(f32) + a_last.astype(f32)
        b_sum = b[0].astype(f32) + b_got[0].astype(f32) + b_last.astype(f32)
        return jnp.concatenate([a_sum, b_sum])

    def octet(self, value):
        value = value.reshape(8, self.shard, -1)
        return lax.all_to_all(value, AXES, 0, 0, axis_index_groups=self.groups)

    def joined(self, *blocks):
        whole = jnp.concatenate(blocks)
        for bit in self.gather[2:]:
            whole = jnp.concatenate([whole, self.swap(whole, bit)])
        return whole

    def first_sum(self, mine, others_swapped):
        block = added(mine, others_swapped)
        for bit in reversed(self.gather[2:]):
            block = block.reshape(2, block.shape[0] // 2, -1)
            block = added(block[0], self.swap(block[1], bit))
        return block.reshape(4, 8 * self.shard, -1)


def on_device(
    plan, layer_input, frame_real, gain_attn, w_qkv, w_out, gain_mlp, w_up, w_down, cotangent
):
    rows = layer_input.shape[1]
    width = layer_input.shape[2]
    shard = w_up.shape[0]
    space = plan.space
    me = lax.axis_index("tm") * space + lax.axis_index("space")
    inputs = layer_input[0].astype(f32)
    grad_out = cotangent[0].astype(f32)
    swap = plan.swap
    attn = Side(plan, me, plan.team, plan.gather, plan.octets, shard, width, rows, rows * 3 // 8)
    feed = Side(
        plan, me, plan.feed_team, plan.feed_gather, None, shard, width, rows, rows // 2
    )

    def has(bit):
        return (me & bit) != 0

    gain_one = gain_attn.astype(f32)[:, None]
    gain_two = gain_mlp.astype(f32)[:, None]
    n_ff = w_up.shape[1] // 8
    qkv_columns = [
        (
            4 * hi + 2 * lo + c,
            (3 * jj + i) * HEAD,
            (3 * jj + i + 1) * HEAD,
            (i * HEADS + 8 * hi + 4 * c + 2 * jj + lo) * HEAD,
        )
        for hi in range(2)
        for lo in range(2)
        for c in range(2)
        for jj in range(2)
        for i in range(3)
    ]
    qkv_sent = deal(qkv_columns, w_qkv, gain_one)
    mine = jnp.where(has(feed.team_hi), 4, 0) + jnp.where(has(feed.team_lo), 2, 0)
    mine = mine + jnp.where(has(1), 1, 0)
    codes = [(4 * hi, 2 * lo, c) for hi in range(2) for lo in range(2) for c in range(2)]

    def placed(*axes):
        ranked = sorted(codes, key=lambda code: [code[i] for i in axes])
        return jnp.array([sum(code) for code in ranked], jnp.int32) ^ mine

    by_lo_core_hi, by_hi_core_lo, by_core_lo_hi = placed(1, 2, 0), placed(0, 2, 1), placed(2, 1, 0)
    by_hi_lo_core = placed(0, 1, 2)

    qkv_sent, tokens, up_in, down_in = tied(qkv_sent, layer_input[0], w_up, w_down)
    feed_sent = spread(by_lo_core_hi, up_in, down_in, gain_two)
    first_rel = attn.to_rel(tokens, True)
    grad_rel = feed.to_rel(cotangent[0], False)
    qkv_block = attn.octet(qkv_sent).reshape(8 * shard, -1)
    out_z = swap(w_out, attn.first)
    qkv_block, first_rel, grad_rel, feed_sent, feed_send, out_z, w_out = tied(
        qkv_block, first_rel, grad_rel, feed_sent, feed_sent[4:], out_z, w_out
    )
    first_near = attn.gather_one(first_rel)
    qkv_first = swap(qkv_block, attn.first)
    qkv_second = swap(qkv_block, attn.second)
    feed_lo = swap(feed_send, feed.team_lo)
    qkv_first, qkv_second, first_near, feed_sent, feed_lo = tied(
        qkv_first, qkv_second, first_near, feed_sent, feed_lo
    )
    qkv_both = swap(qkv_first, attn.second)
    first_far = attn.gather_two(*first_near)
    feed_core = swap(jnp.stack([feed_sent[2:4], feed_lo[2:]]), 1)
    feed_kept = jnp.stack([jnp.stack([feed_sent[:2], feed_lo[:2]]), feed_core])
    (up_kept, down_kept), (up_send, down_send) = (
        [feed_kept[:, :, h, :, part].reshape(4, shard, n_ff) for part in (slice(n_ff), slice(n_ff, None))]
        for h in range(2)
    )
    up_got = swap(up_send, feed.team_hi)
    qkv_both, first_far, up_got, up_kept, down_kept, down_send, grad_rel = tied(
        qkv_both, first_far, up_got, up_kept, down_kept, down_send, grad_rel
    )
    down_got = swap(down_send, feed.team_hi)
    up_block = settle(by_hi_core_lo, up_kept, up_got)
    n_block = up_block.shape[0]
    cut_up = n_block // 2
    qkv_mine = attn.joined(qkv_block, qkv_first, qkv_second, qkv_both)
    qkv_other = swap(qkv_mine, 1)
    first_all = team_rows(*first_near, *first_far)
    half = n_block // 2
    up_z = [swap(up_block[:cut_up], feed.first)]
    up_x = swap(up_block, feed.second)

    team_device = me ^ jnp.array(plan.team_rel, jnp.int32)
    row_index = jnp.arange(rows, dtype=jnp.int32)
    positions = (
        ((team_device // space) % plan.clip * (space * rows) + (team_device % space) * rows)[:, None]
        + row_index[None, :]
    ).reshape(4 * rows)
    half_dim = HEAD // 2
    inverse_freq = jnp.exp(-jnp.log(10000.0) * jnp.arange(half_dim, dtype=f32) * 2.0 / HEAD)
    angles = positions.astype(f32)[:, None] * inverse_freq[None, :]
    angles = jnp.concatenate([angles, angles], axis=-1)
    cosine, sine = jnp.cos(angles), jnp.sin(angles)

    def rotate(value):
        turned = jnp.concatenate([-value[:, half_dim:], value[:, :half_dim]], axis=-1)
        return value * cosine + turned * sine

    def rotate_back(value):
        scaled = value * sine
        turned = jnp.concatenate([scaled[:, half_dim:], -scaled[:, :half_dim]], axis=-1)
        return value * cosine + turned

    def head_triples(mixed):
        found = []
        for j in range(2):
            q, k, v = (
                mixed[:, (3 * j + i) * HEAD : (3 * j + i + 1) * HEAD] for i in range(3)
            )
            found.append(
                jnp.concatenate([rotate(q) * to_log2, rotate(k), v], axis=1).astype(bf16)
            )
        return found

    mixed_mine = matmul(first_all, qkv_mine)
    mixed_other = matmul(first_all, qkv_other)
    stack = jnp.stack(head_triples(mixed_mine) + head_triples(mixed_other))
    my_head = jnp.where(has(plan.heads[0]), 2, 0) + jnp.where(has(plan.heads[1]), 1, 0)
    core_flip = jnp.where(has(1), 2, 0)
    pick = [(my_head ^ r) ^ core_flip for r in range(4)]
    sent = [lax.dynamic_index_in_dim(stack, pick[r], 0, keepdims=False) for r in range(4)]
    out_pair = jnp.stack([w_out, out_z])
    sent, up_z, up_x, grad_rel, up_block, up_part, down_got, down_kept, out_pair = tied(
        sent, up_z, up_x, grad_rel, up_block, up_block[cut_up:], down_got, down_kept, out_pair
    )
    got = [swap(sent[r], plan.head_rel[r]) for r in range(1, 4)]
    up_z += [swap(up_part, feed.first)]
    out_x = swap(out_pair, attn.second)
    cut_z = [0, n_block // 2, n_block * 3 // 4, n_block]
    down_block = settle(by_hi_core_lo, down_kept, down_got)
    got, up_z, down_block, grad_rel, out_x, down_first = tied(
        got, up_z, down_block, grad_rel, out_x, down_block[: cut_z[1]]
    )
    up_za, up_zb = up_z
    own = jnp.stack([sent[0]] + got).reshape(16, rows, 3 * HEAD)
    down_z = [swap(down_first, feed.first)]
    up_both = [swap(up_za, feed.second), swap(up_zb, feed.second)]
    grad_near = feed.gather_one(grad_rel)
    shared = own[:, :, HEAD:]
    other = jnp.stack([swap(shared, rel) for rel in plan.part_rel[1:]])

    block_rel = jnp.array(plan.block_rel, jnp.int32)
    tile_rel = jnp.array(plan.block_rel[:: plan.tile_blocks], jnp.int32)
    tile_slot = (me ^ tile_rel) // space
    no_more = jnp.zeros((16 - tile_slot.shape[0],), jnp.int32)
    info = jnp.concatenate(
        [
            jnp.stack([me, (me % space) * rows, ((me ^ plan.team[1]) % space) * rows]),
            jnp.zeros((5,), jnp.int32),
            block_rel,
            tile_slot,
            no_more,
            tile_slot // plan.clip * plan.clip,
            no_more,
        ]
    ).astype(jnp.int32)

    attended, attended_t, log_total, keys, values = attend(plan, info, frame_real, own, other)
    w_team = jnp.stack([w_out, out_x[0], out_z, out_x[1]])
    attended, down_z, up_both, grad_near, w_team, down_block, up_x, up_za, up_zb, up_block = tied(
        attended, down_z, up_both, grad_near, w_team, down_block, up_x, up_za, up_zb, up_block
    )
    w_got = swap(w_team, plan.parts[-1])
    attended = attended.reshape(4, 4 * rows, HEAD)
    heads_got = [swap(attended[r], plan.head_rel[r]) for r in range(1, 4)]
    down_z += [swap(down_block[cut_z[1] : cut_z[2]], feed.first)]
    up_mine = feed.joined(up_block, up_za, up_zb, up_x, *up_both)
    for bit in reversed(plan.parts):
        w_got = w_got if bit == plan.parts[-1] else swap(w_team, bit)
        w_team = jnp.where(
            has(bit),
            jnp.concatenate([w_got, w_team], axis=1),
            jnp.concatenate([w_team, w_got], axis=1),
        )
    w_team = w_team.reshape(4 * HEAD, width)
    heads_got, w_team, down_z, grad_near, down_block, up_mine = tied(
        heads_got, w_team, down_z, grad_near, down_block, up_mine
    )
    attended_team = jnp.concatenate([attended[0]] + heads_got, axis=1)
    branch = matmul(attended_team, w_team).astype(bf16)
    branch_near = attn.scatter_one(branch)
    cut_x = n_block * 5 // 8
    down_x = [swap(down_block[:cut_x], feed.second)]
    grad_far = feed.gather_two(*grad_near)
    branch_near, down_x, up_mine, down_z, grad_far, down_block = tied(
        branch_near, down_x, up_mine, down_z, grad_far, down_block
    )
    middle = attn.scatter_two(*branch_near)
    down_x += [swap(down_block[cut_x:], feed.second)]
    up_other = swap(up_mine, 1)
    grad_all = team_rows(*grad_near, *grad_far)
    middle, down_x, down_z, down_block, up_other, grad_all = tied(
        middle, down_x, down_z, down_block, up_other, grad_all
    )
    middle = inputs + middle
    second_near = feed.gather_one(feed.to_rel(middle, True))
    down_z += [swap(down_block[cut_z[2] :], feed.first)]
    cut_both = n_block * 5 // 16
    down_both = [swap(down_z[0][:cut_both], feed.second)]
    second_near, down_both, down_z = tied(second_near, down_both, down_z)
    second_far = feed.gather_two(*second_near)
    down_z = jnp.concatenate(down_z)
    down_both += [swap(down_z[cut_both:], feed.second)]
    second_far, down_both, down_z = tied(second_far, down_both, down_z)
    down_mine = feed.joined(down_block, down_z, *down_x, *down_both)
    down_other = swap(down_mine, 1)
    second_all = team_rows(*second_near, *second_far)
    normed_two, scale_two = layer_norm(middle)
    gelu = functools.partial(jax.nn.gelu, approximate=True)
    hidden_other = matmul(second_all, up_other)
    hidden_mine = matmul(second_all, up_mine)
    act_other = gelu(hidden_other).astype(bf16)
    act_mine = gelu(hidden_mine).astype(bf16)
    down_other_grad = matmul(grad_all, act_other, ((0,), (0,))).astype(bf16)
    down_other_grad, down_other, down_mine, act_mine, act_other = tied(
        down_other_grad, down_other, down_mine, act_mine, act_other
    )
    down_swapped = swap(down_other_grad, 1)

    def back(hidden, down):
        return jax.vjp(gelu, hidden)[1](matmul(grad_all, down))[0].astype(bf16)

    hid_mine, hid_other = back(hidden_mine, down_mine), back(hidden_other, down_other)
    second_parts = matmul(hid_mine, up_mine, ((1,), (1,))) + matmul(hid_other, up_other, ((1,), (1,)))
    second_parts, hid_mine, hid_other, down_swapped, act_mine, act_other = tied(
        second_parts.astype(bf16), hid_mine, hid_other, down_swapped, act_mine, act_other
    )
    second_back = feed.scatter_one(second_parts)
    down_mine_grad = matmul(grad_all, act_mine, ((0,), (0,))).astype(bf16)
    down_sum = feed.first_sum(down_mine_grad, down_swapped)
    c1, c2, c3 = n_block * 3 // 8, n_block * 3 // 4, n_block * 3 // 8
    down_x3 = [swap(down_sum[3][:c1], feed.second)]
    out_parts = (
        matmul(act_mine, down_mine, ((1,), (1,))) + matmul(act_other, down_other, ((1,), (1,)))
    ).astype(bf16)
    second_back, down_x3, down_sum, out_parts, hid_other = tied(
        second_back, down_x3, down_sum, out_parts, hid_other
    )
    grad_second = feed.scatter_two(*second_back)
    z1, z2 = n_block * 3 // 16, n_block * 3 // 8
    down_z1 = [swap(added(down_sum[1][:z1], down_x3[0][:z1]), feed.first)]
    down_x3 += [swap(down_sum[3][c1:c2], feed.second)]
    up_other_grad = matmul(second_all, hid_other, ((0,), (0,))).astype(bf16)
    down_x32 = jnp.concatenate([down_sum[3][c2:], down_sum[2][:c3]])
    grad_second, down_z1, down_x3, down_sum, up_other_grad, down_x32, hid_mine = tied(
        grad_second, down_z1, down_x3, down_sum, up_other_grad, down_x32, hid_mine
    )
    grad_second = feed.from_rel(grad_second)
    grad_middle = grad_out + layer_norm_back(grad_second, normed_two, scale_two)
    middle_near = attn.gather_one(grad_middle.astype(bf16))
    down_x32 = swap(down_x32, feed.second)
    up_swapped = swap(up_other_grad, 1)
    middle_near, down_x32, up_swapped, hid_mine, down_sum, down_x3, down_x2 = tied(
        middle_near, down_x32, up_swapped, hid_mine, down_sum, down_x3, down_sum[2][c3:]
    )
    middle_far = attn.gather_two(*middle_near)
    down_x3 = jnp.concatenate([*down_x3, down_x32[: n_block - c2]])
    down_x2 = [down_x32[n_block - c2 :], swap(down_x2, feed.second)]
    up_mine_grad = matmul(second_all, hid_mine, ((0,), (0,))).astype(bf16)
    down_z1b = added(down_sum[1][z1:z2], down_x3[z1:z2])
    middle_far, up_swapped, up_mine_grad, down_x2, down_x3, down_sum, down_z1b = tied(
        middle_far, up_swapped, up_mine_grad, down_x2, down_x3, down_sum, down_z1b
    )
    middle_all = team_rows(*middle_near, *middle_far)
    grad_heads = matmul(middle_all, w_team, ((1,), (1,))).astype(bf16)
    grad_own = grad_heads[:, :HEAD]
    grad_got = [
        swap(grad_heads[:, r * HEAD : (r + 1) * HEAD], plan.head_rel[r]) for r in range(1, 4)
    ]
    down_z1 += [swap(down_z1b, feed.first)]
    out_grad = matmul(attended_team, middle_all, ((0,), (0,))).astype(bf16).reshape(4, HEAD, width)
    up_sum = feed.first_sum(up_mine_grad, up_swapped)
    down_z1c = added(down_sum[1][z2:], down_x3[z2:])
    grad_got, up_sum, out_grad, down_z1, down_z1c, out_parts = tied(
        grad_got, up_sum, out_grad, down_z1, down_z1c, out_parts
    )
    up_x3 = swap(up_sum[3], feed.second)
    down_z1 += [swap(down_z1c, feed.first)]
    out_near = feed.scatter_one(out_parts)
    for bit in plan.parts:
        lower, upper = jnp.split(out_grad, 2, axis=1)
        kept = jnp.where(has(bit), upper, lower)
        out_grad = added(kept, swap(jnp.where(has(bit), lower, upper), bit))
    dq, dkv_own, dkv_other = attend_back(
        plan,
        info,
        frame_real,
        own,
        keys,
        values,
        jnp.stack([grad_own] + grad_got).reshape(16, rows, HEAD),
        attended_t,
        log_total,
    )
    dq, dkv_own, dkv_other, up_x3, down_z1, out_near, out_grad = tied(
        dq, dkv_own, dkv_other, up_x3, down_z1, out_near, out_grad
    )
    dkv = dkv_own.astype(f32)
    for i, rel in enumerate(plan.part_rel[1:]):
        dkv = dkv + swap(dkv_other[i], rel).astype(f32)
    triple = jnp.concatenate([dq, dkv.astype(bf16)], axis=2).reshape(4, 4 * rows, 3 * HEAD)
    up_z1 = added(up_sum[1], up_x3)
    za, zb = n_block * 3 // 8, n_block * 11 // 16
    out_grad = out_grad.reshape(2, 2, HEAD // len(plan.part_rel), width)
    triple, up_sum, up_z1, up_z1a, down_z1, out_grad, out_sent = tied(
        triple, up_sum, up_z1, up_z1[:za], down_z1, out_grad, out_grad[:, 1]
    )
    got = [swap(triple[r], plan.head_rel[r]) for r in range(1, 4)]
    up_z1a = swap(up_z1a, feed.first)
    out_grad = added(out_grad[:, 0], swap(out_sent, attn.second))
    down_done = added(down_sum[0], jnp.concatenate(down_x2), jnp.concatenate(down_z1))
    down_rows, down_rows_hi = unsettle(by_hi_lo_core, down_done)
    got, up_z1a, up_z1b, up_z1c, down_rows, down_rows_hi, up_sum, out_grad, out_near = tied(
        got, up_z1a, up_z1[za:zb], up_z1[zb:], down_rows, down_rows_hi, up_sum, out_grad, out_near
    )
    places = (my_head ^ jnp.arange(4, dtype=jnp.int32)) ^ core_flip
    mixed_grad = turn_back(places, cosine, sine, [triple[0]] + got)
    mixed_grad_mine, mixed_grad_other = mixed_grad[0], mixed_grad[1]
    qkv_other_grad = matmul(first_all, mixed_grad_other, ((0,), (0,))).astype(bf16)
    out_sum = feed.scatter_two(*out_near)
    up_x2a = swap(up_sum[2][:half], feed.second)
    up_z1b = swap(up_z1b, feed.first)
    (
        qkv_other_grad,
        mixed_grad_mine,
        mixed_grad_other,
        up_x2a,
        up_z1b,
        up_z1c,
        up_x2b,
        up_sum,
        down_rows,
        down_rows_hi,
        out_sum,
    ) = tied(
        qkv_other_grad,
        mixed_grad_mine,
        mixed_grad_other,
        up_x2a,
        up_z1b,
        up_z1c,
        up_sum[2][half:],
        up_sum,
        down_rows,
        down_rows_hi,
        out_sum,
    )
    qkv_swapped = swap(qkv_other_grad, 1)
    up_x2b = swap(up_x2b, feed.second)
    up_z1c = swap(up_z1c, feed.first)
    down_rows = jnp.stack([down_rows, swap(down_rows_hi, feed.team_hi)]).reshape(2, 2, 2, shard, n_ff)
    qkv_mine_grad = matmul(first_all, mixed_grad_mine, ((0,), (0,))).astype(bf16)
    first_parts = matmul(mixed_grad_mine, qkv_mine, ((1,), (1,))) + matmul(
        mixed_grad_other, qkv_other, ((1,), (1,))
    )
    qkv_sum = attn.first_sum(qkv_mine_grad, qkv_swapped)
    qkv_sum, first_parts, up_x2b, up_sum, up_z1c, down_rows, down_send, out_grad = tied(
        qkv_sum,
        first_parts.astype(bf16),
        up_x2b,
        up_sum,
        up_z1c,
        down_rows,
        down_rows[:, 1],
        out_grad,
    )
    qkv_x3 = swap(qkv_sum[3], attn.second)
    first_back = attn.scatter_one(first_parts)
    up_done = added(
        up_sum[0],
        jnp.concatenate([up_x2a, up_x2b]),
        jnp.concatenate([up_z1a, up_z1b, up_z1c]),
    )
    down_rows = jnp.stack([down_rows[:, 0], swap(down_send, feed.team_lo)])
    up_rows, up_rows_hi = unsettle(by_hi_lo_core, up_done)
    up_rows = jnp.stack([up_rows, swap(up_rows_hi, feed.team_hi)]).reshape(2, 2, 2, shard, n_ff)
    qkv_x3, first_back, up_rows, qkv_sum, down_rows, up_send = tied(
        qkv_x3, first_back, up_rows, qkv_sum, down_rows, up_rows[:, 1]
    )
    qkv_z1 = swap(added(qkv_sum[1], qkv_x3), attn.first)
    qkv_x2 = swap(qkv_sum[2], attn.second)
    first_rows = attn.scatter_two(*first_back)
    output = (middle + feed.from_rel(out_sum)).astype(bf16)
    up_rows = jnp.stack([up_rows[:, 0], swap(up_send, feed.team_lo)])
    qkv_z1, qkv_x2, first_rows, out_grad, output, up_rows, down_rows = tied(
        qkv_z1, qkv_x2, first_rows, out_grad, output, up_rows, down_rows
    )
    down_rows = jnp.stack([down_rows[:, :, 0], swap(down_rows[:, :, 1], 1)])
    grad_down, _ = restore(False, by_core_lo_hi, down_rows.reshape(8, shard, n_ff), w_down, gain_two)
    up_rows = jnp.stack([up_rows[:, :, 0], swap(up_rows[:, :, 1], 1)])
    grad_up, grad_gain_two = restore(
        True, by_core_lo_hi, up_rows.reshape(8, shard, n_ff), w_up, gain_two
    )
    qkv_got = attn.octet(added(qkv_sum[0], qkv_x2, qkv_z1))
    grad_first = attn.from_rel(first_rows)
    grad_inputs = grad_middle + layer_norm_back(grad_first, *layer_norm(inputs))
    out_grad = out_grad[0].astype(f32) + swap(out_grad[1], attn.first).astype(f32)
    grad_qkv, grad_gain_one = deliver(qkv_columns, qkv_got, w_qkv, gain_one)
    return (
        output[None],
        grad_inputs[None],
        grad_gain_one[:, 0],
        grad_qkv,
        out_grad,
        grad_gain_two[:, 0],
        grad_up,
        grad_down,
    )


def solution(mesh):
    plan = Plan(mesh.shape["tm"], mesh.shape["space"], BLOCK)
    tokens = P("tm", "space", None)
    line = P(("tm", "space"))
    table = P(("tm", "space"), None)
    return jax.shard_map(
        functools.partial(on_device, plan),
        mesh=mesh,
        in_specs=(tokens, P(), line, table, table, line, table, table, tokens),
        out_specs=(tokens, tokens, line, table, table, line, table, table),
        check_vma=False,
    )
```

```python
import functools

import jax
import jax.numpy as jnp
import numpy as np
from jax import lax
from jax.experimental import pallas as pl
from jax.experimental.pallas import tpu as pltpu
from jax.sharding import PartitionSpec as P

HEADS = 16
HEAD = 128
AXES = ("tm", "space")
BLOCK = 128

epsilon = 1e-05
masked_value = -1e30
inv_root = HEAD ** (-0.5)
to_log2 = inv_root * 1.4426950408889634
q_unscale = inv_root / to_log2

bf16 = jnp.bfloat16
f32 = jnp.float32


def matmul(left, right, dims=((1,), (0,))):
    return lax.dot_general(left, right, (dims, ((), ())), preferred_element_type=f32)


def tied(*values):
    return lax.optimization_barrier(values)


class Plan:
    def __init__(self, tm, space, frame_rows):
        self.count = tm * space
        self.space = space
        self.slots = tm
        self.clip = min(16, tm)
        count = self.count
        self.team = (count // 2, count // 16)
        self.heads = (count // 4, count // 8)
        self.feed_team = (count // 4, count // 16)
        bits = [1 << i for i in range(count.bit_length() - 1)]
        taken = set(self.team + self.heads)
        self.parts = [b for b in reversed(bits) if b not in taken]
        rest = [b for b in self.parts if b != 1]
        self.gather = [*self.heads, *rest]
        self.feed_gather = [count // 2, count // 8, *rest]
        self.team_rel = [0, self.team[1], self.team[0], self.team[0] | self.team[1]]
        self.head_rel = [0, self.heads[1], self.heads[0], self.heads[0] | self.heads[1]]
        self.block_rel = [h | t for h in self.head_rel for t in self.team_rel]
        self.part_rel = [
            sum(b for j, b in enumerate(self.parts) if (i >> j) & 1)
            for i in range(1 << len(self.parts))
        ]
        devices = range(count)
        self.octets = self.groups(sum(self.team) | 1)
        self.tile_blocks = 2 if self.team[1] < space else 1
        self.devices = devices

    def groups(self, mask):
        held = {}
        for d in range(self.count):
            held.setdefault(d & ~mask, []).append(d)
        return list(held.values())

    def swap(self, value, mask):
        return lax.ppermute(value, AXES, [(d, d ^ mask) for d in self.devices])


def layer_norm(values):
    center = jnp.mean(values, axis=-1, keepdims=True)
    shifted = values - center
    spread = jnp.mean(shifted * shifted, axis=-1, keepdims=True)
    scale = lax.rsqrt(spread + epsilon)
    return shifted * scale, scale


def layer_norm_back(grads, normed, scale):
    inner = jnp.mean(grads * normed, axis=-1, keepdims=True)
    return (grads - jnp.mean(grads, axis=-1, keepdims=True) - normed * inner) * scale


def transposed(tile):
    return tile.astype(f32).T.astype(tile.dtype)


def attend_kernel(plan, info, real, own, other, out, out_t, lse, keys, values, values_t):
    me = info[0]
    n_blocks = len(plan.block_rel)
    for part, part_rel in enumerate(plan.part_rel):

        def place(b, _, part=part, part_rel=part_rel):
            home = me ^ part_rel ^ info[8 + b]
            if part == 0:
                key, value = own[b, :, HEAD : 2 * HEAD], own[b, :, 2 * HEAD :]
            else:
                key, value = other[part - 1, b, :, :HEAD], other[part - 1, b, :, HEAD:]
            rows = pl.ds(pl.multiple_of(home * BLOCK, BLOCK), BLOCK)
            keys[rows, :] = key
            values[rows, :] = value
            values_t[home] = transposed(value)
            return 0

        lax.fori_loop(0, n_blocks, place, 0, unroll=4)

    frame = plan.space * BLOCK
    per_tile = plan.tile_blocks
    two = per_tile * BLOCK
    lane = lax.broadcasted_iota(jnp.int32, (1, two), 1)
    q_place = jnp.where(lane < BLOCK, info[1] + lane, info[2] + lane - BLOCK)

    def tile(i, _):
        slot, first = info[24 + i], info[40 + i]
        q = jnp.concatenate([own[per_tile * i + j, :, :HEAD] for j in range(per_tile)], axis=0)

        def scores(g):
            key = keys[pl.ds(pl.multiple_of(g * frame, frame), frame), :]
            return matmul(key, q, ((1,), (1,)))

        def value_t(g):
            return jnp.concatenate(
                [values_t[g * plan.space + s] for s in range(plan.space)], axis=1
            )

        def fold(carry, s, g):
            top, total, acc = carry
            new = jnp.maximum(top, jnp.max(s, axis=0, keepdims=True))
            fade = jnp.exp2(top - new)
            p = jnp.exp2(s - new)
            total = total * fade + jnp.sum(p, axis=0, keepdims=True)
            acc = acc * fade + matmul(value_t(g), p.astype(bf16))
            return new, total, acc

        def step(g, carry):
            ahead = scores(g + 1)
            s = carry[3] + jnp.where(real[g] > 0, 0.0, masked_value)
            return (*fold(carry[:3], s, g), ahead)

        first = jnp.where(real[slot] > 0, first, slot)
        start = (
            jnp.full((1, two), masked_value, f32),
            jnp.zeros((1, two), f32),
            jnp.zeros((HEAD, two), f32),
            scores(first),
        )
        *carry, s = lax.fori_loop(first, slot, step, start)
        k_place = lax.broadcasted_iota(jnp.int32, (frame, two), 0)
        top, total, acc = fold(carry, jnp.where(k_place <= q_place, s, masked_value), slot)
        lse[i] = top + jnp.log2(total)
        acc = acc / total
        out_t[i] = acc
        back = acc.T.astype(bf16)
        for j in range(per_tile):
            out[per_tile * i + j] = back[j * BLOCK : (j + 1) * BLOCK]
        return 0

    lax.fori_loop(0, n_blocks // per_tile, tile, 0)


def attend_back_kernel(
    plan, info, real, own, keys, values, grads, out_t, lse, dq, dkv_own, dkv_other, dk, dv, keys_t
):
    me = info[0]
    n_blocks = len(plan.block_rel)

    def clear(b, _):
        rows = pl.ds(pl.multiple_of(b * BLOCK, BLOCK), BLOCK)
        dk[rows, :] = jnp.zeros((BLOCK, HEAD), f32)
        dv[rows, :] = jnp.zeros((BLOCK, HEAD), f32)
        keys_t[b] = transposed(keys[rows, :])
        return 0

    lax.fori_loop(0, plan.count, clear, 0, unroll=4)

    frame = plan.space * BLOCK
    per_tile = plan.tile_blocks
    two = per_tile * BLOCK
    lane = lax.broadcasted_iota(jnp.int32, (1, two), 1)
    q_place = jnp.where(lane < BLOCK, info[1] + lane, info[2] + lane - BLOCK)

    def tile(i, _):
        slot, first = info[24 + i], info[40 + i]
        q = jnp.concatenate([own[per_tile * i + j, :, :HEAD] for j in range(per_tile)], axis=0)
        do = jnp.concatenate([grads[per_tile * i + j] for j in range(per_tile)], axis=0)
        delta = jnp.sum(do.astype(f32).T * out_t[i], axis=0, keepdims=True)
        log_total = lse[i]

        def turn(g, mask):
            rows = pl.ds(pl.multiple_of(g * frame, frame), frame)
            key, value = keys[rows, :], values[rows, :]
            s = matmul(key, q, ((1,), (1,)))
            dp = matmul(value, do, ((1,), (1,)))
            if mask:
                p = jnp.exp2(s - log_total)
            else:
                p = jnp.exp2(s - jnp.where(real[g] > 0, log_total, -masked_value))
            if mask:
                k_place = lax.broadcasted_iota(jnp.int32, (frame, two), 0)
                p = jnp.where(k_place <= q_place, p, 0.0)
            ds = (p * (dp - delta)).astype(bf16)
            dv[rows, :] += matmul(p.astype(bf16), do)
            dk[rows, :] += matmul(ds, q)
            key_t = jnp.concatenate(
                [keys_t[g * plan.space + s] for s in range(plan.space)], axis=1
            )
            return matmul(key_t, ds)

        def step(g, dq_t):
            return dq_t + turn(g, False)

        first = jnp.where(real[slot] > 0, first, slot)
        dq_t = lax.fori_loop(first, slot, step, turn(slot, True))
        back = (dq_t * inv_root).T.astype(bf16)
        for j in range(per_tile):
            dq[per_tile * i + j] = back[j * BLOCK : (j + 1) * BLOCK]
        return 0

    lax.fori_loop(0, n_blocks // per_tile, tile, 0)

    for part, part_rel in enumerate(plan.part_rel):

        def hand_out(b, _, part=part, part_rel=part_rel):
            home = me ^ part_rel ^ info[8 + b]
            rows = pl.ds(pl.multiple_of(home * BLOCK, BLOCK), BLOCK)
            pair = jnp.concatenate([dk[rows, :] * q_unscale, dv[rows, :]], axis=1).astype(bf16)
            if part == 0:
                dkv_own[b] = pair
            else:
                dkv_other[part - 1, b] = pair
            return 0

        lax.fori_loop(0, n_blocks, hand_out, 0, unroll=4)


def call(kernel, n_scalar, n_in, outs, scratch, cost, room=16):
    return pl.pallas_call(
        kernel,
        out_shape=outs,
        in_specs=[pl.BlockSpec(memory_space=pltpu.SMEM)] * n_scalar
        + [pl.BlockSpec(memory_space=pltpu.VMEM)] * n_in,
        out_specs=tuple(pl.BlockSpec(memory_space=pltpu.VMEM) for _ in outs),
        scratch_shapes=scratch,
        cost_estimate=cost,
        compiler_params=pltpu.CompilerParams(vmem_limit_bytes=room << 20),
    )


def moving(n_bytes):
    return pl.CostEstimate(flops=n_bytes, bytes_accessed=n_bytes, transcendentals=0)


def arrange_kernel(normed, chunk, lanes, value, out, held):
    x = value[...].astype(f32)
    if normed:
        x = layer_norm(x)[0]
    held[...] = x.astype(bf16)
    for j in range(x.shape[1] // chunk):
        at = pl.multiple_of(lanes[j], chunk)
        out[:, j * chunk : (j + 1) * chunk] = held[:, pl.ds(at, chunk)]


def arrange(normed, chunk, lanes, value):
    shape = value.shape
    return call(
        functools.partial(arrange_kernel, normed, chunk),
        1,
        1,
        (jax.ShapeDtypeStruct(shape, bf16),),
        [pltpu.VMEM(shape, bf16)],
        moving(4 * value.size),
    )(lanes, value)[0]


def team_rows_kernel(a, b, a_lo, b_hi, a_far, b_far, out):
    one, two = a.shape[0], b.shape[0]
    pieces = (a[...], b[...], a_lo[...], b_far[:two], a_far[:one], b_hi[...], a_far[one:], b_far[two:])
    start = 0
    for piece in pieces:
        out[start : start + piece.shape[0]] = piece
        start += piece.shape[0]


def team_rows(*pieces):
    rows, width = pieces[0].shape[0] + pieces[1].shape[0], pieces[0].shape[1]
    return call(
        team_rows_kernel,
        0,
        6,
        (jax.ShapeDtypeStruct((4 * rows, width), bf16),),
        [],
        moving(16 * rows * width),
    )(*pieces)[0]


def turn_back_kernel(places, cosine, sine, *refs):
    heads, out = refs[:4], refs[4]
    half_dim = HEAD // 2
    cos, sin = cosine[...], sine[...]
    for r in range(4):
        found = []
        for i in range(2):
            t = heads[r][:, i * HEAD : (i + 1) * HEAD].astype(f32)
            scaled = t * sin
            turned = jnp.concatenate([scaled[:, half_dim:], -scaled[:, :half_dim]], axis=-1)
            found.append((t * cos + turned).astype(bf16))
        found.append(heads[r][:, 2 * HEAD :])
        whole = jnp.concatenate(found, axis=1)
        place = places[r]

        @pl.when(place % 2 == 0)
        def _():
            out[place // 2, :, : 3 * HEAD] = whole

        @pl.when(place % 2 == 1)
        def _():
            out[place // 2, :, 3 * HEAD :] = whole


def turn_back(places, cosine, sine, heads):
    rows = cosine.shape[0]
    return call(
        turn_back_kernel,
        1,
        6,
        (jax.ShapeDtypeStruct((2, rows, 6 * HEAD), bf16),),
        [],
        moving(8 * rows * 3 * HEAD * 2),
    )(places, cosine, sine, *heads)[0]


def deal_kernel(columns, weight, gain, out):
    for block, start, end, target in columns:
        value = weight[:, target : target + end - start].astype(f32) * gain[...]
        out[block, :, start:end] = value.astype(bf16)


def deal(columns, weight, gain):
    rows, width = weight.shape
    return call(
        functools.partial(deal_kernel, columns),
        0,
        2,
        (jax.ShapeDtypeStruct((8, rows, width // 8), bf16),),
        [],
        moving(4 * rows * width),
    )(weight, gain)[0]


def deliver_kernel(columns, got, weight, gain, out, gain_grad):
    total = None
    for block, start, end, target in columns:
        value = got[block, :, start:end].astype(f32)
        span = slice(target, target + end - start)
        part = jnp.sum(value * weight[:, span].astype(f32), axis=1, keepdims=True)
        total = part if total is None else total + part
        out[:, span] = value * gain[...]
    gain_grad[...] = jnp.broadcast_to(total, gain_grad.shape)


def deliver(columns, got, weight, gain):
    rows, width = weight.shape
    return call(
        functools.partial(deliver_kernel, columns),
        0,
        3,
        (jax.ShapeDtypeStruct((rows, width), f32), jax.ShapeDtypeStruct((rows, 128), f32)),
        [],
        moving(8 * rows * width),
    )(got, weight, gain)


def spread_kernel(places, up, down, gain, out):
    n = out.shape[2] // 2
    for i in range(8):
        at = pl.ds(pl.multiple_of(places[i] * n, n), n)
        out[i, :, :n] = (up[:, at].astype(f32) * gain[...]).astype(bf16)
        out[i, :, n:] = down[:, at]


def spread(places, up, down, gain):
    rows, width = up.shape
    return call(
        spread_kernel,
        1,
        3,
        (jax.ShapeDtypeStruct((8, rows, width // 4), bf16),),
        [],
        moving(8 * rows * width),
    )(places, up, down, gain)[0]


def settle_kernel(places, kept, got, out):
    rows = kept.shape[1]
    for i in range(8):
        at = pl.ds(pl.multiple_of(places[i] * rows, rows), rows)
        out[at, :] = kept[i] if i < 4 else got[i - 4]


def settle(places, kept, got):
    _, rows, n = kept.shape
    return call(
        settle_kernel,
        1,
        2,
        (jax.ShapeDtypeStruct((8 * rows, n), bf16),),
        [],
        moving(32 * rows * n),
    )(places, kept, got)[0]


def unsettle_kernel(places, block, kept, sent):
    rows = kept.shape[1]
    for i in range(8):
        value = block[pl.ds(pl.multiple_of(places[i] * rows, rows), rows), :]
        if i < 4:
            kept[i] = value
        else:
            sent[i - 4] = value


def unsettle(places, block):
    rows, n = block.shape[0] // 8, block.shape[1]
    half = jax.ShapeDtypeStruct((4, rows, n), bf16)
    return call(unsettle_kernel, 1, 1, (half, half), [], moving(32 * rows * n))(places, block)


def restore_kernel(with_gain, places, got, weight, gain, out, gain_grad):
    n = got.shape[2]
    total = None
    for i in range(8):
        at = pl.ds(pl.multiple_of(places[i] * n, n), n)
        value = got[i].astype(f32)
        if with_gain:
            part = jnp.sum(value * weight[:, at].astype(f32), axis=1, keepdims=True)
            total = part if total is None else total + part
            value = value * gain[...]
        out[:, at] = value
    if with_gain:
        gain_grad[...] = jnp.broadcast_to(total, gain_grad.shape)
    else:
        gain_grad[...] = jnp.zeros(gain_grad.shape, f32)


def restore(with_gain, places, got, weight, gain):
    rows, width = weight.shape
    return call(
        functools.partial(restore_kernel, with_gain),
        1,
        3,
        (jax.ShapeDtypeStruct((rows, width), f32), jax.ShapeDtypeStruct((rows, 128), f32)),
        [],
        moving(8 * rows * width),
    )(places, got, weight, gain)


def attend(plan, info, real, own, other):
    blocks = len(plan.block_rel)
    tokens = plan.count * BLOCK
    work = blocks * BLOCK * min(plan.clip * plan.space * BLOCK, tokens) // 2
    shape = jax.ShapeDtypeStruct
    return call(
        functools.partial(attend_kernel, plan),
        2,
        2,
        (
            shape((blocks, BLOCK, HEAD), bf16),
            shape((blocks // plan.tile_blocks, HEAD, plan.tile_blocks * BLOCK), f32),
            shape((blocks // plan.tile_blocks, 1, plan.tile_blocks * BLOCK), f32),
            shape((tokens, HEAD), bf16),
            shape((tokens, HEAD), bf16),
        ),
        [pltpu.VMEM((plan.count, HEAD, BLOCK), bf16)],
        pl.CostEstimate(flops=8 * work * HEAD, bytes_accessed=8 << 20, transcendentals=work),
        min(56, 8 + plan.count * 3 // 4),
    )(info, real, own, other)


def attend_back(plan, info, real, own, keys, values, grads, out_t, lse):
    blocks = len(plan.block_rel)
    tokens = plan.count * BLOCK
    work = blocks * BLOCK * min(plan.clip * plan.space * BLOCK, tokens) // 2
    shape = jax.ShapeDtypeStruct
    return call(
        functools.partial(attend_back_kernel, plan),
        2,
        6,
        (
            shape((blocks, BLOCK, HEAD), bf16),
            shape((blocks, BLOCK, 2 * HEAD), bf16),
            shape((len(plan.part_rel) - 1, blocks, BLOCK, 2 * HEAD), bf16),
        ),
        [
            pltpu.VMEM((tokens, HEAD), f32),
            pltpu.VMEM((tokens, HEAD), f32),
            pltpu.VMEM((plan.count, HEAD, BLOCK), bf16),
        ],
        pl.CostEstimate(flops=20 * work * HEAD, bytes_accessed=8 << 20, transcendentals=work),
        min(56, 8 + plan.count * 3 // 4),
    )(info, real, own, keys, values, grads, out_t, lse)


def added(*values):
    return sum(v.astype(f32) for v in values).astype(bf16)


class Side:
    def __init__(self, plan, me, team, gather, groups, shard, width, rows, cut):
        self.plan, self.me, self.groups = plan, me, groups
        self.team_hi, self.team_lo = team
        self.gather, self.shard, self.cut = gather, shard, cut
        self.first, self.second = gather[:2]
        low = self.low = min(gather)
        self.chunk = low * shard
        self.n_chunks = width // self.chunk
        self.order = [
            (
                sum(b for j, b in enumerate(gather) if (i >> j) & 1)
                + (self.team_hi if hi else 0)
                + (self.team_lo if lo else 0)
            )
            // low
            for i in range(1 << len(gather))
            for hi in range(2)
            for lo in range(2 if self.team_lo > low else 1)
        ]
        self.inverse = [self.order.index(m) for m in range(self.n_chunks)]
        at = jnp.array(self.order, jnp.int32) ^ ((me & sum(gather)) // low)
        self.lanes = at * self.chunk

    def swap(self, value, bit):
        return self.plan.swap(value, bit)

    def flipped(self, pieces):
        for bit in self.gather:
            step = bit // self.low
            own = (self.me & bit) != 0
            pieces = [jnp.where(own, pieces[m ^ step], pieces[m]) for m in range(self.n_chunks)]
        return pieces

    def pieces(self, value):
        chunk = self.chunk
        return [value[:, m * chunk : (m + 1) * chunk] for m in range(self.n_chunks)]

    def to_rel(self, value, normed):
        if self.chunk % 128 == 0:
            return arrange(normed, self.chunk, self.lanes, value)
        value = layer_norm(value.astype(f32))[0] if normed else value
        pieces = self.flipped(self.pieces(value.astype(bf16)))
        return jnp.concatenate([pieces[m] for m in self.order], axis=1)

    def from_rel(self, value):
        pieces = self.pieces(value)
        return jnp.concatenate(self.flipped([pieces[m] for m in self.inverse]), axis=1)

    def gather_one(self, value):
        a, b = value[: self.cut], value[self.cut :]
        return a, b, self.swap(a, self.team_lo), self.swap(b, self.team_hi)

    def gather_two(self, a, b, a_lo, b_hi):
        return (
            self.swap(jnp.concatenate([a, a_lo]), self.team_hi),
            self.swap(jnp.concatenate([b, b_hi]), self.team_lo),
        )

    def scatter_one(self, parts):
        parts = parts.reshape(4, parts.shape[0] // 4, -1)
        a, b = parts[:, : self.cut], parts[:, self.cut :]
        a_got = self.swap(a[2:], self.team_hi)
        b_got = self.swap(jnp.stack([b[1], b[3]]), self.team_lo)
        return a[:2], jnp.stack([b[0], b[2]]), a_got, b_got

    def scatter_two(self, a, b, a_got, b_got):
        a_last = self.swap(added(a[1], a_got[1]), self.team_lo)
        b_last = self.swap(added(b[1], b_got[1]), self.team_hi)
        a_sum = a[0].astype(f32) + a_got[0].astype(f32) + a_last.astype(f32)
        b_sum = b[0].astype(f32) + b_got[0].astype(f32) + b_last.astype(f32)
        return jnp.concatenate([a_sum, b_sum])

    def octet(self, value):
        value = value.reshape(8, self.shard, -1)
        return lax.all_to_all(value, AXES, 0, 0, axis_index_groups=self.groups)

    def joined(self, *blocks):
        whole = jnp.concatenate(blocks)
        for bit in self.gather[2:]:
            whole = jnp.concatenate([whole, self.swap(whole, bit)])
        return whole

    def first_sum(self, mine, others_swapped):
        block = added(mine, others_swapped)
        for bit in reversed(self.gather[2:]):
            block = block.reshape(2, block.shape[0] // 2, -1)
            block = added(block[0], self.swap(block[1], bit))
        return block.reshape(4, 8 * self.shard, -1)


def on_device(
    plan, layer_input, frame_real, gain_attn, w_qkv, w_out, gain_mlp, w_up, w_down, cotangent
):
    rows = layer_input.shape[1]
    width = layer_input.shape[2]
    shard = w_up.shape[0]
    space = plan.space
    me = lax.axis_index("tm") * space + lax.axis_index("space")
    inputs = layer_input[0].astype(f32)
    grad_out = cotangent[0].astype(f32)
    swap = plan.swap
    attn = Side(plan, me, plan.team, plan.gather, plan.octets, shard, width, rows, rows * 3 // 8)
    feed = Side(
        plan, me, plan.feed_team, plan.feed_gather, None, shard, width, rows, rows // 2
    )

    def has(bit):
        return (me & bit) != 0

    gain_one = gain_attn.astype(f32)[:, None]
    gain_two = gain_mlp.astype(f32)[:, None]
    n_ff = w_up.shape[1] // 8
    qkv_columns = [
        (
            4 * hi + 2 * lo + c,
            (3 * jj + i) * HEAD,
            (3 * jj + i + 1) * HEAD,
            (i * HEADS + 8 * hi + 4 * c + 2 * jj + lo) * HEAD,
        )
        for hi in range(2)
        for lo in range(2)
        for c in range(2)
        for jj in range(2)
        for i in range(3)
    ]
    qkv_sent = deal(qkv_columns, w_qkv, gain_one)
    mine = jnp.where(has(feed.team_hi), 4, 0) + jnp.where(has(feed.team_lo), 2, 0)
    mine = mine + jnp.where(has(1), 1, 0)
    codes = [(4 * hi, 2 * lo, c) for hi in range(2) for lo in range(2) for c in range(2)]

    def placed(*axes):
        ranked = sorted(codes, key=lambda code: [code[i] for i in axes])
        return jnp.array([sum(code) for code in ranked], jnp.int32) ^ mine

    by_lo_core_hi, by_hi_core_lo, by_core_lo_hi = placed(1, 2, 0), placed(0, 2, 1), placed(2, 1, 0)
    by_hi_lo_core = placed(0, 1, 2)

    qkv_sent, tokens, up_in, down_in = tied(qkv_sent, layer_input[0], w_up, w_down)
    feed_sent = spread(by_lo_core_hi, up_in, down_in, gain_two)
    first_rel = attn.to_rel(tokens, True)
    grad_rel = feed.to_rel(cotangent[0], False)
    qkv_block = attn.octet(qkv_sent).reshape(8 * shard, -1)
    out_z = swap(w_out, attn.first)
    grad_near = feed.gather_one(grad_rel)
    qkv_block, first_rel, grad_near, feed_sent, feed_send, out_z, w_out = tied(
        qkv_block, first_rel, grad_near, feed_sent, feed_sent[4:], out_z, w_out
    )
    first_near = attn.gather_one(first_rel)
    qkv_first = swap(qkv_block, attn.first)
    qkv_second = swap(qkv_block, attn.second)
    feed_lo = swap(feed_send, feed.team_lo)
    qkv_first, qkv_second, first_near, feed_sent, feed_lo = tied(
        qkv_first, qkv_second, first_near, feed_sent, feed_lo
    )
    qkv_both = swap(qkv_first, attn.second)
    first_far = attn.gather_two(*first_near)
    feed_core = swap(jnp.stack([feed_sent[2:4], feed_lo[2:]]), 1)
    feed_kept = jnp.stack([jnp.stack([feed_sent[:2], feed_lo[:2]]), feed_core])
    (up_kept, down_kept), (up_send, down_send) = (
        [feed_kept[:, :, h, :, part].reshape(4, shard, n_ff) for part in (slice(n_ff), slice(n_ff, None))]
        for h in range(2)
    )
    up_got = swap(up_send, feed.team_hi)
    qkv_both, first_far, up_got, up_kept, down_kept, down_send, grad_near = tied(
        qkv_both, first_far, up_got, up_kept, down_kept, down_send, grad_near
    )
    down_got = swap(down_send, feed.team_hi)
    up_block = settle(by_hi_core_lo, up_kept, up_got)
    n_block = up_block.shape[0]
    cut_up = n_block // 2
    qkv_mine = attn.joined(qkv_block, qkv_first, qkv_second, qkv_both)
    qkv_other = swap(qkv_mine, 1)
    first_all = team_rows(*first_near, *first_far)
    half = n_block // 2
    up_z = [swap(up_block[:cut_up], feed.first)]
    up_x = swap(up_block, feed.second)

    team_device = me ^ jnp.array(plan.team_rel, jnp.int32)
    row_index = jnp.arange(rows, dtype=jnp.int32)
    positions = (
        ((team_device // space) % plan.clip * (space * rows) + (team_device % space) * rows)[:, None]
        + row_index[None, :]
    ).reshape(4 * rows)
    half_dim = HEAD // 2
    inverse_freq = jnp.exp(-jnp.log(10000.0) * jnp.arange(half_dim, dtype=f32) * 2.0 / HEAD)
    angles = positions.astype(f32)[:, None] * inverse_freq[None, :]
    angles = jnp.concatenate([angles, angles], axis=-1)
    cosine, sine = jnp.cos(angles), jnp.sin(angles)

    def rotate(value):
        turned = jnp.concatenate([-value[:, half_dim:], value[:, :half_dim]], axis=-1)
        return value * cosine + turned * sine

    def rotate_back(value):
        scaled = value * sine
        turned = jnp.concatenate([scaled[:, half_dim:], -scaled[:, :half_dim]], axis=-1)
        return value * cosine + turned

    def head_triples(mixed):
        found = []
        for j in range(2):
            q, k, v = (
                mixed[:, (3 * j + i) * HEAD : (3 * j + i + 1) * HEAD] for i in range(3)
            )
            found.append(
                jnp.concatenate([rotate(q) * to_log2, rotate(k), v], axis=1).astype(bf16)
            )
        return found

    mixed_mine = matmul(first_all, qkv_mine)
    mixed_other = matmul(first_all, qkv_other)
    stack = jnp.stack(head_triples(mixed_mine) + head_triples(mixed_other))
    my_head = jnp.where(has(plan.heads[0]), 2, 0) + jnp.where(has(plan.heads[1]), 1, 0)
    core_flip = jnp.where(has(1), 2, 0)
    pick = [(my_head ^ r) ^ core_flip for r in range(4)]
    sent = [lax.dynamic_index_in_dim(stack, pick[r], 0, keepdims=False) for r in range(4)]
    out_pair = jnp.stack([w_out, out_z])
    sent, up_z, up_x, grad_near, up_block, up_part, down_got, down_kept, out_pair = tied(
        sent, up_z, up_x, grad_near, up_block, up_block[cut_up:], down_got, down_kept, out_pair
    )
    got = [swap(sent[r], plan.head_rel[r]) for r in range(1, 4)]
    up_z += [swap(up_part, feed.first)]
    out_x = swap(out_pair, attn.second)
    cut_z = [0, n_block // 2, n_block * 3 // 4, n_block * 15 // 16, n_block]
    down_block = settle(by_hi_core_lo, down_kept, down_got)
    got, up_z, down_block, grad_near, out_x, down_first = tied(
        got, up_z, down_block, grad_near, out_x, down_block[: cut_z[1]]
    )
    up_za, up_zb = up_z
    own = jnp.stack([sent[0]] + got).reshape(16, rows, 3 * HEAD)
    down_z = [swap(down_first, feed.first)]
    up_both = [swap(up_za, feed.second), swap(up_zb, feed.second)]
    grad_far = feed.gather_two(*grad_near)
    shared = own[:, :, HEAD:]
    other = jnp.stack([swap(shared, rel) for rel in plan.part_rel[1:]])

    block_rel = jnp.array(plan.block_rel, jnp.int32)
    tile_rel = jnp.array(plan.block_rel[:: plan.tile_blocks], jnp.int32)
    tile_slot = (me ^ tile_rel) // space
    no_more = jnp.zeros((16 - tile_slot.shape[0],), jnp.int32)
    info = jnp.concatenate(
        [
            jnp.stack([me, (me % space) * rows, ((me ^ plan.team[1]) % space) * rows]),
            jnp.zeros((5,), jnp.int32),
            block_rel,
            tile_slot,
            no_more,
            tile_slot // plan.clip * plan.clip,
            no_more,
        ]
    ).astype(jnp.int32)

    attended, attended_t, log_total, keys, values = attend(plan, info, frame_real, own, other)
    w_team = jnp.stack([w_out, out_x[0], out_z, out_x[1]])
    attended, down_z, up_both, grad_far, w_team, down_block, up_x, up_za, up_zb, up_block = tied(
        attended, down_z, up_both, grad_far, w_team, down_block, up_x, up_za, up_zb, up_block
    )
    w_got = swap(w_team, plan.parts[-1])
    attended = attended.reshape(4, 4 * rows, HEAD)
    heads_got = [swap(attended[r], plan.head_rel[r]) for r in range(1, 4)]
    down_z += [swap(down_block[cut_z[1] : cut_z[2]], feed.first)]
    for bit in reversed(plan.parts):
        w_got = w_got if bit == plan.parts[-1] else swap(w_team, bit)
        w_team = jnp.where(
            has(bit),
            jnp.concatenate([w_got, w_team], axis=1),
            jnp.concatenate([w_team, w_got], axis=1),
        )
    w_team = w_team.reshape(4 * HEAD, width)
    cut_x = n_block * 5 // 8
    heads_got, w_team, down_z, grad_far, down_block, down_part, up_both, up_block = tied(
        heads_got, w_team, down_z, grad_far, down_block, down_block[:cut_x], up_both, up_block
    )
    attended_team = jnp.concatenate([attended[0]] + heads_got, axis=1)
    branch = matmul(attended_team, w_team).astype(bf16)
    branch_near = attn.scatter_one(branch)
    down_x = [swap(down_part, feed.second)]
    up_mine = feed.joined(up_block, up_za, up_zb, up_x, *up_both)
    cuts = [0, n_block * 5 // 16, n_block * 9 // 16, n_block * 15 // 16, n_block]
    branch_near, down_x, up_mine, down_z, grad_far, down_block, down_part, both_part = tied(
        branch_near,
        down_x,
        up_mine,
        down_z,
        grad_far,
        down_block,
        down_block[cut_x:],
        down_z[0][: cuts[1]],
    )
    middle = attn.scatter_two(*branch_near)
    down_x += [swap(down_part, feed.second)]
    down_both = [swap(both_part, feed.second)]
    up_other = swap(up_mine, 1)
    grad_all = team_rows(*grad_near, *grad_far)
    both_part = jnp.concatenate(down_z)[cuts[1] : cuts[2]]
    middle, down_x, down_z, down_block, up_other, grad_all, down_both, both_part, down_part = tied(
        middle,
        down_x,
        down_z,
        down_block,
        up_other,
        grad_all,
        down_both,
        both_part,
        down_block[cut_z[2] : cut_z[3]],
    )
    middle = inputs + middle
    second_near = feed.gather_one(feed.to_rel(middle, True))
    down_z += [swap(down_part, feed.first)]
    down_both += [swap(both_part, feed.second)]
    second_near, down_both, down_z, down_part = tied(
        second_near, down_both, down_z, down_block[cut_z[3] :]
    )
    second_far = feed.gather_two(*second_near)
    both_part = jnp.concatenate(down_z)[cuts[2] : cuts[3]]
    down_z += [swap(down_part, feed.first)]
    down_both += [swap(both_part, feed.second), swap(down_z[-1], feed.second)]
    down_z = jnp.concatenate(down_z)
    second_far, down_both, down_z = tied(second_far, down_both, down_z)
    down_mine = feed.joined(down_block, down_z, *down_x, *down_both)
    down_other = swap(down_mine, 1)
    second_all = team_rows(*second_near, *second_far)
    normed_two, scale_two = layer_norm(middle)
    gelu = functools.partial(jax.nn.gelu, approximate=True)
    hidden_other = matmul(second_all, up_other)
    hidden_mine = matmul(second_all, up_mine)
    act_other = gelu(hidden_other).astype(bf16)
    act_mine = gelu(hidden_mine).astype(bf16)
    down_other_grad = matmul(grad_all, act_other, ((0,), (0,))).astype(bf16)
    down_other_grad, down_other, down_mine, act_mine, act_other = tied(
        down_other_grad, down_other, down_mine, act_mine, act_other
    )
    down_swapped = swap(down_other_grad, 1)

    def back(hidden, down):
        return jax.vjp(gelu, hidden)[1](matmul(grad_all, down))[0].astype(bf16)

    hid_mine, hid_other = back(hidden_mine, down_mine), back(hidden_other, down_other)
    second_parts = matmul(hid_mine, up_mine, ((1,), (1,))) + matmul(hid_other, up_other, ((1,), (1,)))
    second_parts, hid_mine, hid_other, down_swapped, act_mine, act_other = tied(
        second_parts.astype(bf16), hid_mine, hid_other, down_swapped, act_mine, act_other
    )
    second_back = feed.scatter_one(second_parts)
    down_mine_grad = matmul(grad_all, act_mine, ((0,), (0,))).astype(bf16)
    down_sum = feed.first_sum(down_mine_grad, down_swapped)
    c1, c2, c3 = n_block // 4, n_block * 5 // 8, n_block // 4
    down_x3 = [swap(down_sum[3][:c1], feed.second)]
    second_back, down_x3, down_sum, hid_other = tied(second_back, down_x3, down_sum, hid_other)
    grad_second = feed.scatter_two(*second_back)
    z1, z2 = n_block // 4, n_block * 3 // 8
    down_z1 = [swap(added(down_sum[1][:z1], down_x3[0][:z1]), feed.first)]
    down_x3 += [swap(down_sum[3][c1:c2], feed.second)]
    up_other_grad = matmul(second_all, hid_other, ((0,), (0,))).astype(bf16)
    down_x32 = jnp.concatenate([down_sum[3][c2:], down_sum[2][:c3]])
    grad_second, down_z1, down_x3, down_sum, up_other_grad, down_x32, hid_mine = tied(
        grad_second, down_z1, down_x3, down_sum, up_other_grad, down_x32, hid_mine
    )
    grad_second = feed.from_rel(grad_second)
    grad_middle = grad_out + layer_norm_back(grad_second, normed_two, scale_two)
    middle_near = attn.gather_one(grad_middle.astype(bf16))
    down_x32 = swap(down_x32, feed.second)
    up_swapped = swap(up_other_grad, 1)
    (
        middle_near,
        down_x32,
        up_swapped,
        hid_mine,
        down_sum,
        down_x3,
        down_x2,
        act_mine,
        act_other,
        down_mine,
        down_other,
    ) = tied(
        middle_near,
        down_x32,
        up_swapped,
        hid_mine,
        down_sum,
        down_x3,
        down_sum[2][c3:],
        act_mine,
        act_other,
        down_mine,
        down_other,
    )
    middle_far = attn.gather_two(*middle_near)
    down_x3 = jnp.concatenate([*down_x3, down_x32[: n_block - c2]])
    down_x2 = [down_x32[n_block - c2 :], swap(down_x2, feed.second)]
    up_mine_grad = matmul(second_all, hid_mine, ((0,), (0,))).astype(bf16)
    down_z1b = added(down_sum[1][z1:z2], down_x3[z1:z2])
    out_parts = (
        matmul(act_mine, down_mine, ((1,), (1,))) + matmul(act_other, down_other, ((1,), (1,)))
    ).astype(bf16)
    middle_far, up_swapped, up_mine_grad, down_x2, down_x3, down_sum, down_z1b, out_parts = tied(
        middle_far, up_swapped, up_mine_grad, down_x2, down_x3, down_sum, down_z1b, out_parts
    )
    middle_all = team_rows(*middle_near, *middle_far)
    grad_heads = matmul(middle_all, w_team, ((1,), (1,))).astype(bf16)
    grad_own = grad_heads[:, :HEAD]
    grad_got = [
        swap(grad_heads[:, r * HEAD : (r + 1) * HEAD], plan.head_rel[r]) for r in range(1, 4)
    ]
    down_z1 += [swap(down_z1b, feed.first)]
    out_grad = matmul(attended_team, middle_all, ((0,), (0,))).astype(bf16).reshape(4, HEAD, width)
    up_sum = feed.first_sum(up_mine_grad, up_swapped)
    down_z1c = added(down_sum[1][z2:], down_x3[z2:])
    grad_got, up_sum, out_grad, down_z1, down_z1c, out_parts = tied(
        grad_got, up_sum, out_grad, down_z1, down_z1c, out_parts
    )
    up_x3 = swap(up_sum[3], feed.second)
    down_z1 += [swap(down_z1c, feed.first)]
    out_near = feed.scatter_one(out_parts)
    for bit in plan.parts:
        lower, upper = jnp.split(out_grad, 2, axis=1)
        kept = jnp.where(has(bit), upper, lower)
        out_grad = added(kept, swap(jnp.where(has(bit), lower, upper), bit))
    dq, dkv_own, dkv_other = attend_back(
        plan,
        info,
        frame_real,
        own,
        keys,
        values,
        jnp.stack([grad_own] + grad_got).reshape(16, rows, HEAD),
        attended_t,
        log_total,
    )
    dq, dkv_own, dkv_other, up_x3, down_z1, out_near, out_grad = tied(
        dq, dkv_own, dkv_other, up_x3, down_z1, out_near, out_grad
    )
    dkv = dkv_own.astype(f32)
    for i, rel in enumerate(plan.part_rel[1:]):
        dkv = dkv + swap(dkv_other[i], rel).astype(f32)
    triple = jnp.concatenate([dq, dkv.astype(bf16)], axis=2).reshape(4, 4 * rows, 3 * HEAD)
    up_z1 = added(up_sum[1], up_x3)
    za, zb = n_block // 2, n_block * 11 // 16
    out_grad = out_grad.reshape(2, 2, HEAD // len(plan.part_rel), width)
    triple, up_sum, up_z1, up_z1a, down_z1, out_grad, out_sent = tied(
        triple, up_sum, up_z1, up_z1[:za], down_z1, out_grad, out_grad[:, 1]
    )
    got = [swap(triple[r], plan.head_rel[r]) for r in range(1, 4)]
    up_z1a = swap(up_z1a, feed.first)
    down_done = added(down_sum[0], jnp.concatenate(down_x2), jnp.concatenate(down_z1))
    down_rows, down_rows_hi = unsettle(by_hi_lo_core, down_done)
    got, up_z1a, up_z1b, up_z1c, down_rows, down_rows_hi, up_sum, out_grad, out_near = tied(
        got, up_z1a, up_z1[za:zb], up_z1[zb:], down_rows, down_rows_hi, up_sum, out_grad, out_near
    )
    places = (my_head ^ jnp.arange(4, dtype=jnp.int32)) ^ core_flip
    mixed_grad = turn_back(places, cosine, sine, [triple[0]] + got)
    mixed_grad_mine, mixed_grad_other = mixed_grad[0], mixed_grad[1]
    qkv_other_grad = matmul(first_all, mixed_grad_other, ((0,), (0,))).astype(bf16)
    out_sum = feed.scatter_two(*out_near)
    up_x2a = swap(up_sum[2][:half], feed.second)
    up_z1b = swap(up_z1b, feed.first)
    (
        qkv_other_grad,
        mixed_grad_mine,
        mixed_grad_other,
        up_x2a,
        up_z1b,
        up_z1c,
        up_x2b,
        up_sum,
        down_rows,
        down_rows_hi,
        out_sum,
    ) = tied(
        qkv_other_grad,
        mixed_grad_mine,
        mixed_grad_other,
        up_x2a,
        up_z1b,
        up_z1c,
        up_sum[2][half:],
        up_sum,
        down_rows,
        down_rows_hi,
        out_sum,
    )
    qkv_swapped = swap(qkv_other_grad, 1)
    up_x2b = swap(up_x2b, feed.second)
    up_z1c = swap(up_z1c, feed.first)
    down_rows = jnp.stack([down_rows, swap(down_rows_hi, feed.team_hi)]).reshape(2, 2, 2, shard, n_ff)
    qkv_mine_grad = matmul(first_all, mixed_grad_mine, ((0,), (0,))).astype(bf16)
    first_parts = matmul(mixed_grad_mine, qkv_mine, ((1,), (1,))) + matmul(
        mixed_grad_other, qkv_other, ((1,), (1,))
    )
    qkv_sum = attn.first_sum(qkv_mine_grad, qkv_swapped)
    qkv_sum, first_parts, up_x2b, up_sum, up_z1c, down_rows, down_send, out_grad = tied(
        qkv_sum,
        first_parts.astype(bf16),
        up_x2b,
        up_sum,
        up_z1c,
        down_rows,
        down_rows[:, 1],
        out_grad,
    )
    qkv_x3 = swap(qkv_sum[3], attn.second)
    first_back = attn.scatter_one(first_parts)
    up_done = added(
        up_sum[0],
        jnp.concatenate([up_x2a, up_x2b]),
        jnp.concatenate([up_z1a, up_z1b, up_z1c]),
    )
    down_rows = jnp.stack([down_rows[:, 0], swap(down_send, feed.team_lo)])
    up_rows, up_rows_hi = unsettle(by_hi_lo_core, up_done)
    up_rows = jnp.stack([up_rows, swap(up_rows_hi, feed.team_hi)]).reshape(2, 2, 2, shard, n_ff)
    qkv_x3, first_back, up_rows, qkv_sum, down_rows, up_send = tied(
        qkv_x3, first_back, up_rows, qkv_sum, down_rows, up_rows[:, 1]
    )
    qkv_z1 = swap(added(qkv_sum[1], qkv_x3), attn.first)
    qkv_x2 = swap(qkv_sum[2], attn.second)
    first_rows = attn.scatter_two(*first_back)
    output = (middle + feed.from_rel(out_sum)).astype(bf16)
    up_rows = jnp.stack([up_rows[:, 0], swap(up_send, feed.team_lo)])
    qkv_z1, qkv_x2, first_rows, out_grad, out_sent, output, up_rows, down_rows = tied(
        qkv_z1, qkv_x2, first_rows, out_grad, out_sent, output, up_rows, down_rows
    )
    down_rows = jnp.stack([down_rows[:, :, 0], swap(down_rows[:, :, 1], 1)])
    grad_down, _ = restore(False, by_core_lo_hi, down_rows.reshape(8, shard, n_ff), w_down, gain_two)
    up_rows = jnp.stack([up_rows[:, :, 0], swap(up_rows[:, :, 1], 1)])
    grad_up, grad_gain_two = restore(
        True, by_core_lo_hi, up_rows.reshape(8, shard, n_ff), w_up, gain_two
    )
    qkv_got = attn.octet(added(qkv_sum[0], qkv_x2, qkv_z1))
    grad_first = attn.from_rel(first_rows)
    grad_inputs = grad_middle + layer_norm_back(grad_first, *layer_norm(inputs))
    out_grad = added(out_grad[:, 0], swap(out_sent, attn.second))
    out_grad = out_grad[0].astype(f32) + swap(out_grad[1], attn.first).astype(f32)
    grad_qkv, grad_gain_one = deliver(qkv_columns, qkv_got, w_qkv, gain_one)
    return (
        output[None],
        grad_inputs[None],
        grad_gain_one[:, 0],
        grad_qkv,
        out_grad,
        grad_gain_two[:, 0],
        grad_up,
        grad_down,
    )


def solution(mesh):
    plan = Plan(mesh.shape["tm"], mesh.shape["space"], BLOCK)
    tokens = P("tm", "space", None)
    line = P(("tm", "space"))
    table = P(("tm", "space"), None)
    return jax.shard_map(
        functools.partial(on_device, plan),
        mesh=mesh,
        in_specs=(tokens, P(), line, table, table, line, table, table, tokens),
        out_specs=(tokens, tokens, line, table, table, line, table, table),
        check_vma=False,
    )
```

```python
import functools

import jax
import jax.numpy as jnp
import numpy as np
from jax import lax
from jax.experimental import pallas as pl
from jax.experimental.pallas import tpu as pltpu
from jax.sharding import PartitionSpec as P

HEADS = 16
HEAD = 128
AXES = ("tm", "space")
BLOCK = 128

epsilon = 1e-05
masked_value = -1e30
inv_root = HEAD ** (-0.5)
to_log2 = inv_root * 1.4426950408889634
q_unscale = inv_root / to_log2

bf16 = jnp.bfloat16
f32 = jnp.float32


def matmul(left, right, dims=((1,), (0,))):
    return lax.dot_general(left, right, (dims, ((), ())), preferred_element_type=f32)


def tied(*values):
    return lax.optimization_barrier(values)


class Plan:
    def __init__(self, tm, space, frame_rows):
        self.count = tm * space
        self.space = space
        self.slots = tm
        self.clip = min(16, tm)
        count = self.count
        self.team = (count // 2, count // 16)
        self.heads = (count // 4, count // 8)
        self.feed_team = (count // 4, count // 16)
        bits = [1 << i for i in range(count.bit_length() - 1)]
        taken = set(self.team + self.heads)
        self.parts = [b for b in reversed(bits) if b not in taken]
        rest = [b for b in self.parts if b != 1]
        self.gather = [*self.heads, *rest]
        self.feed_gather = [count // 2, count // 8, *rest]
        self.team_rel = [0, self.team[1], self.team[0], self.team[0] | self.team[1]]
        self.head_rel = [0, self.heads[1], self.heads[0], self.heads[0] | self.heads[1]]
        self.block_rel = [h | t for h in self.head_rel for t in self.team_rel]
        self.part_rel = [
            sum(b for j, b in enumerate(self.parts) if (i >> j) & 1)
            for i in range(1 << len(self.parts))
        ]
        devices = range(count)
        self.octets = self.groups(sum(self.team) | 1)
        self.tile_blocks = 2 if self.team[1] < space else 1
        self.devices = devices

    def groups(self, mask):
        held = {}
        for d in range(self.count):
            held.setdefault(d & ~mask, []).append(d)
        return list(held.values())

    def swap(self, value, mask):
        return lax.ppermute(value, AXES, [(d, d ^ mask) for d in self.devices])


def layer_norm(values):
    center = jnp.mean(values, axis=-1, keepdims=True)
    shifted = values - center
    spread = jnp.mean(shifted * shifted, axis=-1, keepdims=True)
    scale = lax.rsqrt(spread + epsilon)
    return shifted * scale, scale


def layer_norm_back(grads, normed, scale):
    inner = jnp.mean(grads * normed, axis=-1, keepdims=True)
    return (grads - jnp.mean(grads, axis=-1, keepdims=True) - normed * inner) * scale


def transposed(tile):
    return tile.astype(f32).T.astype(tile.dtype)


def attend_kernel(plan, info, real, own, other, out, out_t, lse, keys, values, values_t):
    me = info[0]
    n_blocks = len(plan.block_rel)
    for part, part_rel in enumerate(plan.part_rel):

        def place(b, _, part=part, part_rel=part_rel):
            home = me ^ part_rel ^ info[8 + b]
            if part == 0:
                key, value = own[b, :, HEAD : 2 * HEAD], own[b, :, 2 * HEAD :]
            else:
                key, value = other[part - 1, b, :, :HEAD], other[part - 1, b, :, HEAD:]
            rows = pl.ds(pl.multiple_of(home * BLOCK, BLOCK), BLOCK)
            keys[rows, :] = key
            values[rows, :] = value
            values_t[home] = transposed(value)
            return 0

        lax.fori_loop(0, n_blocks, place, 0, unroll=4)

    frame = plan.space * BLOCK
    per_tile = plan.tile_blocks
    two = per_tile * BLOCK
    lane = lax.broadcasted_iota(jnp.int32, (1, two), 1)
    q_place = jnp.where(lane < BLOCK, info[1] + lane, info[2] + lane - BLOCK)

    def tile(i, _):
        slot, first = info[24 + i], info[40 + i]
        q = jnp.concatenate([own[per_tile * i + j, :, :HEAD] for j in range(per_tile)], axis=0)

        def scores(g):
            key = keys[pl.ds(pl.multiple_of(g * frame, frame), frame), :]
            return matmul(key, q, ((1,), (1,)))

        def value_t(g):
            return jnp.concatenate(
                [values_t[g * plan.space + s] for s in range(plan.space)], axis=1
            )

        def fold(carry, s, g):
            top, total, acc = carry
            new = jnp.maximum(top, jnp.max(s, axis=0, keepdims=True))
            fade = jnp.exp2(top - new)
            p = jnp.exp2(s - new)
            total = total * fade + jnp.sum(p, axis=0, keepdims=True)
            acc = acc * fade + matmul(value_t(g), p.astype(bf16))
            return new, total, acc

        def step(g, carry):
            ahead = scores(g + 1)
            s = carry[3] + jnp.where(real[g] > 0, 0.0, masked_value)
            return (*fold(carry[:3], s, g), ahead)

        first = jnp.where(real[slot] > 0, first, slot)
        start = (
            jnp.full((1, two), masked_value, f32),
            jnp.zeros((1, two), f32),
            jnp.zeros((HEAD, two), f32),
            scores(first),
        )
        *carry, s = lax.fori_loop(first, slot, step, start)
        k_place = lax.broadcasted_iota(jnp.int32, (frame, two), 0)
        top, total, acc = fold(carry, jnp.where(k_place <= q_place, s, masked_value), slot)
        lse[i] = top + jnp.log2(total)
        acc = acc / total
        out_t[i] = acc
        back = acc.T.astype(bf16)
        for j in range(per_tile):
            out[per_tile * i + j] = back[j * BLOCK : (j + 1) * BLOCK]
        return 0

    lax.fori_loop(0, n_blocks // per_tile, tile, 0)


def attend_back_kernel(
    plan, info, real, own, keys, values, grads, out_t, lse, dq, dkv_own, dkv_other, dk, dv, keys_t
):
    me = info[0]
    n_blocks = len(plan.block_rel)

    def clear(b, _):
        rows = pl.ds(pl.multiple_of(b * BLOCK, BLOCK), BLOCK)
        dk[rows, :] = jnp.zeros((BLOCK, HEAD), f32)
        dv[rows, :] = jnp.zeros((BLOCK, HEAD), f32)
        keys_t[b] = transposed(keys[rows, :])
        return 0

    lax.fori_loop(0, plan.count, clear, 0, unroll=4)

    frame = plan.space * BLOCK
    per_tile = plan.tile_blocks
    two = per_tile * BLOCK
    lane = lax.broadcasted_iota(jnp.int32, (1, two), 1)
    q_place = jnp.where(lane < BLOCK, info[1] + lane, info[2] + lane - BLOCK)

    def tile(i, _):
        slot, first = info[24 + i], info[40 + i]
        q = jnp.concatenate([own[per_tile * i + j, :, :HEAD] for j in range(per_tile)], axis=0)
        do = jnp.concatenate([grads[per_tile * i + j] for j in range(per_tile)], axis=0)
        delta = jnp.sum(do.astype(f32).T * out_t[i], axis=0, keepdims=True)
        log_total = lse[i]

        def turn(g, mask):
            rows = pl.ds(pl.multiple_of(g * frame, frame), frame)
            key, value = keys[rows, :], values[rows, :]
            s = matmul(key, q, ((1,), (1,)))
            dp = matmul(value, do, ((1,), (1,)))
            if mask:
                p = jnp.exp2(s - log_total)
            else:
                p = jnp.exp2(s - jnp.where(real[g] > 0, log_total, -masked_value))
            if mask:
                k_place = lax.broadcasted_iota(jnp.int32, (frame, two), 0)
                p = jnp.where(k_place <= q_place, p, 0.0)
            ds = (p * (dp - delta)).astype(bf16)
            dv[rows, :] += matmul(p.astype(bf16), do)
            dk[rows, :] += matmul(ds, q)
            key_t = jnp.concatenate(
                [keys_t[g * plan.space + s] for s in range(plan.space)], axis=1
            )
            return matmul(key_t, ds)

        def step(g, dq_t):
            return dq_t + turn(g, False)

        first = jnp.where(real[slot] > 0, first, slot)
        dq_t = lax.fori_loop(first, slot, step, turn(slot, True))
        back = (dq_t * inv_root).T.astype(bf16)
        for j in range(per_tile):
            dq[per_tile * i + j] = back[j * BLOCK : (j + 1) * BLOCK]
        return 0

    lax.fori_loop(0, n_blocks // per_tile, tile, 0)

    for part, part_rel in enumerate(plan.part_rel):

        def hand_out(b, _, part=part, part_rel=part_rel):
            home = me ^ part_rel ^ info[8 + b]
            rows = pl.ds(pl.multiple_of(home * BLOCK, BLOCK), BLOCK)
            pair = jnp.concatenate([dk[rows, :] * q_unscale, dv[rows, :]], axis=1).astype(bf16)
            if part == 0:
                dkv_own[b] = pair
            else:
                dkv_other[part - 1, b] = pair
            return 0

        lax.fori_loop(0, n_blocks, hand_out, 0, unroll=4)


def call(kernel, n_scalar, n_in, outs, scratch, cost, room=16):
    return pl.pallas_call(
        kernel,
        out_shape=outs,
        in_specs=[pl.BlockSpec(memory_space=pltpu.SMEM)] * n_scalar
        + [pl.BlockSpec(memory_space=pltpu.VMEM)] * n_in,
        out_specs=tuple(pl.BlockSpec(memory_space=pltpu.VMEM) for _ in outs),
        scratch_shapes=scratch,
        cost_estimate=cost,
        compiler_params=pltpu.CompilerParams(vmem_limit_bytes=room << 20),
    )


def moving(n_bytes):
    return pl.CostEstimate(flops=n_bytes, bytes_accessed=n_bytes, transcendentals=0)


def arrange_kernel(normed, chunk, lanes, value, out, held):
    x = value[...].astype(f32)
    if normed:
        x = layer_norm(x)[0]
    held[...] = x.astype(bf16)
    for j in range(x.shape[1] // chunk):
        at = pl.multiple_of(lanes[j], chunk)
        out[:, j * chunk : (j + 1) * chunk] = held[:, pl.ds(at, chunk)]


def arrange(normed, chunk, lanes, value):
    shape = value.shape
    return call(
        functools.partial(arrange_kernel, normed, chunk),
        1,
        1,
        (jax.ShapeDtypeStruct(shape, bf16),),
        [pltpu.VMEM(shape, bf16)],
        moving(4 * value.size),
    )(lanes, value)[0]


def team_rows_kernel(a, b, a_lo, b_hi, a_far, b_far, out):
    one, two = a.shape[0], b.shape[0]
    pieces = (a[...], b[...], a_lo[...], b_far[:two], a_far[:one], b_hi[...], a_far[one:], b_far[two:])
    start = 0
    for piece in pieces:
        out[start : start + piece.shape[0]] = piece
        start += piece.shape[0]


def team_rows(*pieces):
    rows, width = pieces[0].shape[0] + pieces[1].shape[0], pieces[0].shape[1]
    return call(
        team_rows_kernel,
        0,
        6,
        (jax.ShapeDtypeStruct((4 * rows, width), bf16),),
        [],
        moving(16 * rows * width),
    )(*pieces)[0]


def turn_back_kernel(places, cosine, sine, *refs):
    heads, out = refs[:4], refs[4]
    half_dim = HEAD // 2
    cos, sin = cosine[...], sine[...]
    for r in range(4):
        found = []
        for i in range(2):
            t = heads[r][:, i * HEAD : (i + 1) * HEAD].astype(f32)
            scaled = t * sin
            turned = jnp.concatenate([scaled[:, half_dim:], -scaled[:, :half_dim]], axis=-1)
            found.append((t * cos + turned).astype(bf16))
        found.append(heads[r][:, 2 * HEAD :])
        whole = jnp.concatenate(found, axis=1)
        place = places[r]

        @pl.when(place % 2 == 0)
        def _():
            out[place // 2, :, : 3 * HEAD] = whole

        @pl.when(place % 2 == 1)
        def _():
            out[place // 2, :, 3 * HEAD :] = whole


def turn_back(places, cosine, sine, heads):
    rows = cosine.shape[0]
    return call(
        turn_back_kernel,
        1,
        6,
        (jax.ShapeDtypeStruct((2, rows, 6 * HEAD), bf16),),
        [],
        moving(8 * rows * 3 * HEAD * 2),
    )(places, cosine, sine, *heads)[0]


def deal_kernel(columns, weight, gain, out):
    for block, start, end, target in columns:
        value = weight[:, target : target + end - start].astype(f32) * gain[...]
        out[block, :, start:end] = value.astype(bf16)


def deal(columns, weight, gain):
    rows, width = weight.shape
    return call(
        functools.partial(deal_kernel, columns),
        0,
        2,
        (jax.ShapeDtypeStruct((8, rows, width // 8), bf16),),
        [],
        moving(4 * rows * width),
    )(weight, gain)[0]


def deliver_kernel(columns, got, weight, gain, out, gain_grad):
    total = None
    for block, start, end, target in columns:
        value = got[block, :, start:end].astype(f32)
        span = slice(target, target + end - start)
        part = jnp.sum(value * weight[:, span].astype(f32), axis=1, keepdims=True)
        total = part if total is None else total + part
        out[:, span] = value * gain[...]
    gain_grad[...] = jnp.broadcast_to(total, gain_grad.shape)


def deliver(columns, got, weight, gain):
    rows, width = weight.shape
    return call(
        functools.partial(deliver_kernel, columns),
        0,
        3,
        (jax.ShapeDtypeStruct((rows, width), f32), jax.ShapeDtypeStruct((rows, 128), f32)),
        [],
        moving(8 * rows * width),
    )(got, weight, gain)


def spread_kernel(places, up, down, gain, out):
    n = out.shape[2] // 2
    for i in range(8):
        at = pl.ds(pl.multiple_of(places[i] * n, n), n)
        out[i, :, :n] = (up[:, at].astype(f32) * gain[...]).astype(bf16)
        out[i, :, n:] = down[:, at]


def spread(places, up, down, gain):
    rows, width = up.shape
    return call(
        spread_kernel,
        1,
        3,
        (jax.ShapeDtypeStruct((8, rows, width // 4), bf16),),
        [],
        moving(8 * rows * width),
    )(places, up, down, gain)[0]


def settle_kernel(places, kept, got, out):
    rows = kept.shape[1]
    for i in range(8):
        at = pl.ds(pl.multiple_of(places[i] * rows, rows), rows)
        out[at, :] = kept[i] if i < 4 else got[i - 4]


def settle(places, kept, got):
    _, rows, n = kept.shape
    return call(
        settle_kernel,
        1,
        2,
        (jax.ShapeDtypeStruct((8 * rows, n), bf16),),
        [],
        moving(32 * rows * n),
    )(places, kept, got)[0]


def unsettle_kernel(places, block, kept, sent):
    rows = kept.shape[1]
    for i in range(8):
        value = block[pl.ds(pl.multiple_of(places[i] * rows, rows), rows), :]
        if i < 4:
            kept[i] = value
        else:
            sent[i - 4] = value


def unsettle(places, block):
    rows, n = block.shape[0] // 8, block.shape[1]
    half = jax.ShapeDtypeStruct((4, rows, n), bf16)
    return call(unsettle_kernel, 1, 1, (half, half), [], moving(32 * rows * n))(places, block)


def restore_kernel(with_gain, places, got, weight, gain, out, gain_grad):
    n = got.shape[2]
    total = None
    for i in range(8):
        at = pl.ds(pl.multiple_of(places[i] * n, n), n)
        value = got[i].astype(f32)
        if with_gain:
            part = jnp.sum(value * weight[:, at].astype(f32), axis=1, keepdims=True)
            total = part if total is None else total + part
            value = value * gain[...]
        out[:, at] = value
    if with_gain:
        gain_grad[...] = jnp.broadcast_to(total, gain_grad.shape)
    else:
        gain_grad[...] = jnp.zeros(gain_grad.shape, f32)


def restore(with_gain, places, got, weight, gain):
    rows, width = weight.shape
    return call(
        functools.partial(restore_kernel, with_gain),
        1,
        3,
        (jax.ShapeDtypeStruct((rows, width), f32), jax.ShapeDtypeStruct((rows, 128), f32)),
        [],
        moving(8 * rows * width),
    )(places, got, weight, gain)


def attend(plan, info, real, own, other):
    blocks = len(plan.block_rel)
    tokens = plan.count * BLOCK
    work = blocks * BLOCK * min(plan.clip * plan.space * BLOCK, tokens) // 2
    shape = jax.ShapeDtypeStruct
    return call(
        functools.partial(attend_kernel, plan),
        2,
        2,
        (
            shape((blocks, BLOCK, HEAD), bf16),
            shape((blocks // plan.tile_blocks, HEAD, plan.tile_blocks * BLOCK), f32),
            shape((blocks // plan.tile_blocks, 1, plan.tile_blocks * BLOCK), f32),
            shape((tokens, HEAD), bf16),
            shape((tokens, HEAD), bf16),
        ),
        [pltpu.VMEM((plan.count, HEAD, BLOCK), bf16)],
        pl.CostEstimate(flops=8 * work * HEAD, bytes_accessed=8 << 20, transcendentals=work),
        min(56, 8 + plan.count * 3 // 4),
    )(info, real, own, other)


def attend_back(plan, info, real, own, keys, values, grads, out_t, lse):
    blocks = len(plan.block_rel)
    tokens = plan.count * BLOCK
    work = blocks * BLOCK * min(plan.clip * plan.space * BLOCK, tokens) // 2
    shape = jax.ShapeDtypeStruct
    return call(
        functools.partial(attend_back_kernel, plan),
        2,
        6,
        (
            shape((blocks, BLOCK, HEAD), bf16),
            shape((blocks, BLOCK, 2 * HEAD), bf16),
            shape((len(plan.part_rel) - 1, blocks, BLOCK, 2 * HEAD), bf16),
        ),
        [
            pltpu.VMEM((tokens, HEAD), f32),
            pltpu.VMEM((tokens, HEAD), f32),
            pltpu.VMEM((plan.count, HEAD, BLOCK), bf16),
        ],
        pl.CostEstimate(flops=20 * work * HEAD, bytes_accessed=8 << 20, transcendentals=work),
        min(56, 8 + plan.count * 3 // 4),
    )(info, real, own, keys, values, grads, out_t, lse)


def added(*values):
    return sum(v.astype(f32) for v in values).astype(bf16)


class Side:
    def __init__(self, plan, me, team, gather, groups, shard, width, rows, cut):
        self.plan, self.me, self.groups = plan, me, groups
        self.team_hi, self.team_lo = team
        self.gather, self.shard, self.cut = gather, shard, cut
        self.first, self.second = gather[:2]
        low = self.low = min(gather)
        self.chunk = low * shard
        self.n_chunks = width // self.chunk
        self.order = [
            (
                sum(b for j, b in enumerate(gather) if (i >> j) & 1)
                + (self.team_hi if hi else 0)
                + (self.team_lo if lo else 0)
            )
            // low
            for i in range(1 << len(gather))
            for hi in range(2)
            for lo in range(2 if self.team_lo > low else 1)
        ]
        self.inverse = [self.order.index(m) for m in range(self.n_chunks)]
        at = jnp.array(self.order, jnp.int32) ^ ((me & sum(gather)) // low)
        self.lanes = at * self.chunk

    def swap(self, value, bit):
        return self.plan.swap(value, bit)

    def flipped(self, pieces):
        for bit in self.gather:
            step = bit // self.low
            own = (self.me & bit) != 0
            pieces = [jnp.where(own, pieces[m ^ step], pieces[m]) for m in range(self.n_chunks)]
        return pieces

    def pieces(self, value):
        chunk = self.chunk
        return [value[:, m * chunk : (m + 1) * chunk] for m in range(self.n_chunks)]

    def to_rel(self, value, normed):
        if self.chunk % 128 == 0:
            return arrange(normed, self.chunk, self.lanes, value)
        value = layer_norm(value.astype(f32))[0] if normed else value
        pieces = self.flipped(self.pieces(value.astype(bf16)))
        return jnp.concatenate([pieces[m] for m in self.order], axis=1)

    def from_rel(self, value):
        pieces = self.pieces(value)
        return jnp.concatenate(self.flipped([pieces[m] for m in self.inverse]), axis=1)

    def gather_one(self, value):
        a, b = value[: self.cut], value[self.cut :]
        return a, b, self.swap(a, self.team_lo), self.swap(b, self.team_hi)

    def gather_two(self, a, b, a_lo, b_hi):
        return (
            self.swap(jnp.concatenate([a, a_lo]), self.team_hi),
            self.swap(jnp.concatenate([b, b_hi]), self.team_lo),
        )

    def scatter_one(self, parts):
        parts = parts.reshape(4, parts.shape[0] // 4, -1)
        a, b = parts[:, : self.cut], parts[:, self.cut :]
        a_got = self.swap(a[2:], self.team_hi)
        b_got = self.swap(jnp.stack([b[1], b[3]]), self.team_lo)
        return a[:2], jnp.stack([b[0], b[2]]), a_got, b_got

    def scatter_two(self, a, b, a_got, b_got):
        a_last = self.swap(added(a[1], a_got[1]), self.team_lo)
        b_last = self.swap(added(b[1], b_got[1]), self.team_hi)
        a_sum = a[0].astype(f32) + a_got[0].astype(f32) + a_last.astype(f32)
        b_sum = b[0].astype(f32) + b_got[0].astype(f32) + b_last.astype(f32)
        return jnp.concatenate([a_sum, b_sum])

    def octet(self, value):
        value = value.reshape(8, self.shard, -1)
        return lax.all_to_all(value, AXES, 0, 0, axis_index_groups=self.groups)

    def joined(self, *blocks):
        whole = jnp.concatenate(blocks)
        for bit in self.gather[2:]:
            whole = jnp.concatenate([whole, self.swap(whole, bit)])
        return whole

    def first_sum(self, mine, others_swapped):
        block = added(mine, others_swapped)
        for bit in reversed(self.gather[2:]):
            block = block.reshape(2, block.shape[0] // 2, -1)
            block = added(block[0], self.swap(block[1], bit))
        return block.reshape(4, 8 * self.shard, -1)


def on_device(
    plan, layer_input, frame_real, gain_attn, w_qkv, w_out, gain_mlp, w_up, w_down, cotangent
):
    rows = layer_input.shape[1]
    width = layer_input.shape[2]
    shard = w_up.shape[0]
    space = plan.space
    me = lax.axis_index("tm") * space + lax.axis_index("space")
    inputs = layer_input[0].astype(f32)
    grad_out = cotangent[0].astype(f32)
    swap = plan.swap
    attn = Side(plan, me, plan.team, plan.gather, plan.octets, shard, width, rows, rows * 3 // 8)
    feed = Side(
        plan, me, plan.feed_team, plan.feed_gather, None, shard, width, rows, rows // 2
    )

    def has(bit):
        return (me & bit) != 0

    gain_one = gain_attn.astype(f32)[:, None]
    gain_two = gain_mlp.astype(f32)[:, None]
    n_ff = w_up.shape[1] // 8
    qkv_columns = [
        (
            4 * hi + 2 * lo + c,
            (3 * jj + i) * HEAD,
            (3 * jj + i + 1) * HEAD,
            (i * HEADS + 8 * hi + 4 * c + 2 * jj + lo) * HEAD,
        )
        for hi in range(2)
        for lo in range(2)
        for c in range(2)
        for jj in range(2)
        for i in range(3)
    ]
    qkv_sent = deal(qkv_columns, w_qkv, gain_one)
    mine = jnp.where(has(feed.team_hi), 4, 0) + jnp.where(has(feed.team_lo), 2, 0)
    mine = mine + jnp.where(has(1), 1, 0)
    codes = [(4 * hi, 2 * lo, c) for hi in range(2) for lo in range(2) for c in range(2)]

    def placed(*axes):
        ranked = sorted(codes, key=lambda code: [code[i] for i in axes])
        return jnp.array([sum(code) for code in ranked], jnp.int32) ^ mine

    by_lo_core_hi, by_hi_core_lo, by_core_lo_hi = placed(1, 2, 0), placed(0, 2, 1), placed(2, 1, 0)
    by_hi_lo_core = placed(0, 1, 2)

    qkv_sent, tokens, up_in, down_in = tied(qkv_sent, layer_input[0], w_up, w_down)
    feed_sent = spread(by_lo_core_hi, up_in, down_in, gain_two)
    first_rel = attn.to_rel(tokens, True)
    grad_rel = feed.to_rel(cotangent[0], False)
    qkv_block = attn.octet(qkv_sent).reshape(8 * shard, -1)
    out_z = swap(w_out, attn.first)
    grad_near = feed.gather_one(grad_rel)
    qkv_block, first_rel, grad_near, feed_sent, feed_send, out_z, w_out = tied(
        qkv_block, first_rel, grad_near, feed_sent, feed_sent[4:], out_z, w_out
    )
    first_near = attn.gather_one(first_rel)
    qkv_first = swap(qkv_block, attn.first)
    qkv_second = swap(qkv_block, attn.second)
    feed_lo = swap(feed_send, feed.team_lo)
    qkv_first, qkv_second, first_near, feed_sent, feed_lo = tied(
        qkv_first, qkv_second, first_near, feed_sent, feed_lo
    )
    qkv_both = swap(qkv_first, attn.second)
    first_far = attn.gather_two(*first_near)
    feed_core = swap(jnp.stack([feed_sent[2:4], feed_lo[2:]]), 1)
    feed_kept = jnp.stack([jnp.stack([feed_sent[:2], feed_lo[:2]]), feed_core])
    (up_kept, down_kept), (up_send, down_send) = (
        [feed_kept[:, :, h, :, part].reshape(4, shard, n_ff) for part in (slice(n_ff), slice(n_ff, None))]
        for h in range(2)
    )
    up_got = swap(up_send, feed.team_hi)
    qkv_both, first_far, up_got, up_kept, down_kept, down_send, grad_near = tied(
        qkv_both, first_far, up_got, up_kept, down_kept, down_send, grad_near
    )
    down_got = swap(down_send, feed.team_hi)
    up_block = settle(by_hi_core_lo, up_kept, up_got)
    n_block = up_block.shape[0]
    cut_up = n_block // 2
    qkv_mine = attn.joined(qkv_block, qkv_first, qkv_second, qkv_both)
    qkv_other = swap(qkv_mine, 1)
    first_all = team_rows(*first_near, *first_far)
    half = n_block // 2
    up_z = [swap(up_block[:cut_up], feed.first)]
    up_x = swap(up_block, feed.second)

    team_device = me ^ jnp.array(plan.team_rel, jnp.int32)
    row_index = jnp.arange(rows, dtype=jnp.int32)
    positions = (
        ((team_device // space) % plan.clip * (space * rows) + (team_device % space) * rows)[:, None]
        + row_index[None, :]
    ).reshape(4 * rows)
    half_dim = HEAD // 2
    inverse_freq = jnp.exp(-jnp.log(10000.0) * jnp.arange(half_dim, dtype=f32) * 2.0 / HEAD)
    angles = positions.astype(f32)[:, None] * inverse_freq[None, :]
    angles = jnp.concatenate([angles, angles], axis=-1)
    cosine, sine = jnp.cos(angles), jnp.sin(angles)

    def rotate(value):
        turned = jnp.concatenate([-value[:, half_dim:], value[:, :half_dim]], axis=-1)
        return value * cosine + turned * sine

    def rotate_back(value):
        scaled = value * sine
        turned = jnp.concatenate([scaled[:, half_dim:], -scaled[:, :half_dim]], axis=-1)
        return value * cosine + turned

    def head_triples(mixed):
        found = []
        for j in range(2):
            q, k, v = (
                mixed[:, (3 * j + i) * HEAD : (3 * j + i + 1) * HEAD] for i in range(3)
            )
            found.append(
                jnp.concatenate([rotate(q) * to_log2, rotate(k), v], axis=1).astype(bf16)
            )
        return found

    mixed_mine = matmul(first_all, qkv_mine)
    mixed_other = matmul(first_all, qkv_other)
    stack = jnp.stack(head_triples(mixed_mine) + head_triples(mixed_other))
    my_head = jnp.where(has(plan.heads[0]), 2, 0) + jnp.where(has(plan.heads[1]), 1, 0)
    core_flip = jnp.where(has(1), 2, 0)
    pick = [(my_head ^ r) ^ core_flip for r in range(4)]
    sent = [lax.dynamic_index_in_dim(stack, pick[r], 0, keepdims=False) for r in range(4)]
    out_pair = jnp.stack([w_out, out_z])
    sent, up_z, up_x, grad_near, up_block, up_part, down_got, down_kept, out_pair = tied(
        sent, up_z, up_x, grad_near, up_block, up_block[cut_up:], down_got, down_kept, out_pair
    )
    got = [swap(sent[r], plan.head_rel[r]) for r in range(1, 4)]
    up_z += [swap(up_part, feed.first)]
    out_x = swap(out_pair, attn.second)
    cut_z = [0, n_block // 2, n_block * 3 // 4, n_block * 15 // 16, n_block]
    down_block = settle(by_hi_core_lo, down_kept, down_got)
    got, up_z, down_block, grad_near, out_x, down_first = tied(
        got, up_z, down_block, grad_near, out_x, down_block[: cut_z[1]]
    )
    up_za, up_zb = up_z
    own = jnp.stack([sent[0]] + got).reshape(16, rows, 3 * HEAD)
    down_z = [swap(down_first, feed.first)]
    up_both = [swap(up_za, feed.second), swap(up_zb, feed.second)]
    grad_far = feed.gather_two(*grad_near)
    shared = own[:, :, HEAD:]
    other = jnp.stack([swap(shared, rel) for rel in plan.part_rel[1:]])

    block_rel = jnp.array(plan.block_rel, jnp.int32)
    tile_rel = jnp.array(plan.block_rel[:: plan.tile_blocks], jnp.int32)
    tile_slot = (me ^ tile_rel) // space
    no_more = jnp.zeros((16 - tile_slot.shape[0],), jnp.int32)
    info = jnp.concatenate(
        [
            jnp.stack([me, (me % space) * rows, ((me ^ plan.team[1]) % space) * rows]),
            jnp.zeros((5,), jnp.int32),
            block_rel,
            tile_slot,
            no_more,
            tile_slot // plan.clip * plan.clip,
            no_more,
        ]
    ).astype(jnp.int32)

    attended, attended_t, log_total, keys, values = attend(plan, info, frame_real, own, other)
    w_team = jnp.stack([w_out, out_x[0], out_z, out_x[1]])
    attended, down_z, up_both, grad_far, w_team, down_block, up_x, up_za, up_zb, up_block = tied(
        attended, down_z, up_both, grad_far, w_team, down_block, up_x, up_za, up_zb, up_block
    )
    w_got = swap(w_team, plan.parts[-1])
    attended = attended.reshape(4, 4 * rows, HEAD)
    heads_got = [swap(attended[r], plan.head_rel[r]) for r in range(1, 4)]
    down_z += [swap(down_block[cut_z[1] : cut_z[2]], feed.first)]
    for bit in reversed(plan.parts):
        w_got = w_got if bit == plan.parts[-1] else swap(w_team, bit)
        w_team = jnp.where(
            has(bit),
            jnp.concatenate([w_got, w_team], axis=1),
            jnp.concatenate([w_team, w_got], axis=1),
        )
    w_team = w_team.reshape(4 * HEAD, width)
    cut_x = n_block * 5 // 8
    heads_got, w_team, down_z, grad_far, down_block, down_part, up_both, up_block = tied(
        heads_got, w_team, down_z, grad_far, down_block, down_block[:cut_x], up_both, up_block
    )
    attended_team = jnp.concatenate([attended[0]] + heads_got, axis=1)
    branch = matmul(attended_team, w_team).astype(bf16)
    branch_near = attn.scatter_one(branch)
    down_x = [swap(down_part, feed.second)]
    up_mine = feed.joined(up_block, up_za, up_zb, up_x, *up_both)
    cuts = [0, n_block * 5 // 16, n_block * 9 // 16, n_block * 15 // 16, n_block]
    branch_near, down_x, up_mine, down_z, grad_far, down_block, down_part, both_part = tied(
        branch_near,
        down_x,
        up_mine,
        down_z,
        grad_far,
        down_block,
        down_block[cut_x:],
        down_z[0][: cuts[1]],
    )
    middle = attn.scatter_two(*branch_near)
    down_x += [swap(down_part, feed.second)]
    down_both = [swap(both_part, feed.second)]
    up_other = swap(up_mine, 1)
    grad_all = team_rows(*grad_near, *grad_far)
    both_part = jnp.concatenate(down_z)[cuts[1] : cuts[2]]
    middle, down_x, down_z, down_block, up_other, grad_all, down_both, both_part, down_part = tied(
        middle,
        down_x,
        down_z,
        down_block,
        up_other,
        grad_all,
        down_both,
        both_part,
        down_block[cut_z[2] : cut_z[3]],
    )
    middle = inputs + middle
    second_near = feed.gather_one(feed.to_rel(middle, True))
    down_z += [swap(down_part, feed.first)]
    down_both += [swap(both_part, feed.second)]
    second_near, down_both, down_z, down_part = tied(
        second_near, down_both, down_z, down_block[cut_z[3] :]
    )
    second_far = feed.gather_two(*second_near)
    both_part = jnp.concatenate(down_z)[cuts[2] : cuts[3]]
    down_z += [swap(down_part, feed.first)]
    down_both += [swap(both_part, feed.second), swap(down_z[-1], feed.second)]
    down_z = jnp.concatenate(down_z)
    second_far, down_both, down_z = tied(second_far, down_both, down_z)
    down_mine = feed.joined(down_block, down_z, *down_x, *down_both)
    down_other = swap(down_mine, 1)
    second_all = team_rows(*second_near, *second_far)
    normed_two, scale_two = layer_norm(middle)
    gelu = functools.partial(jax.nn.gelu, approximate=True)
    hidden_other = matmul(second_all, up_other)
    hidden_mine = matmul(second_all, up_mine)
    act_other = gelu(hidden_other).astype(bf16)
    act_mine = gelu(hidden_mine).astype(bf16)
    down_other_grad = matmul(grad_all, act_other, ((0,), (0,))).astype(bf16)
    down_other_grad, down_other, down_mine, act_mine, act_other = tied(
        down_other_grad, down_other, down_mine, act_mine, act_other
    )
    down_swapped = swap(down_other_grad, 1)
    down_mine_grad = matmul(grad_all, act_mine, ((0,), (0,))).astype(bf16)

    def back(hidden, down):
        return jax.vjp(gelu, hidden)[1](matmul(grad_all, down))[0].astype(bf16)

    hid_mine, hid_other = back(hidden_mine, down_mine), back(hidden_other, down_other)
    second_parts = matmul(hid_mine, up_mine, ((1,), (1,))) + matmul(hid_other, up_other, ((1,), (1,)))
    second_parts, hid_mine, hid_other, down_swapped, down_mine_grad, act_mine, act_other = tied(
        second_parts.astype(bf16),
        hid_mine,
        hid_other,
        down_swapped,
        down_mine_grad,
        act_mine,
        act_other,
    )
    second_back = feed.scatter_one(second_parts)
    down_sum = feed.first_sum(down_mine_grad, down_swapped)
    c1, c2, c3 = n_block // 4, n_block * 5 // 8, n_block // 4
    down_x3 = [swap(down_sum[3][:c1], feed.second)]
    second_back, down_x3, down_sum, hid_other = tied(second_back, down_x3, down_sum, hid_other)
    grad_second = feed.scatter_two(*second_back)
    z1, z2 = n_block // 4, n_block * 3 // 8
    down_z1 = [swap(added(down_sum[1][:z1], down_x3[0][:z1]), feed.first)]
    down_x3 += [swap(down_sum[3][c1:c2], feed.second)]
    up_other_grad = matmul(second_all, hid_other, ((0,), (0,))).astype(bf16)
    down_x32 = jnp.concatenate([down_sum[3][c2:], down_sum[2][:c3]])
    grad_second, down_z1, down_x3, down_sum, up_other_grad, down_x32, hid_mine = tied(
        grad_second, down_z1, down_x3, down_sum, up_other_grad, down_x32, hid_mine
    )
    grad_second = feed.from_rel(grad_second)
    grad_middle = grad_out + layer_norm_back(grad_second, normed_two, scale_two)
    middle_near = attn.gather_one(grad_middle.astype(bf16))
    down_x32 = swap(down_x32, feed.second)
    up_swapped = swap(up_other_grad, 1)
    (
        middle_near,
        down_x32,
        up_swapped,
        hid_mine,
        down_sum,
        down_x3,
        down_x2,
        act_mine,
        act_other,
        down_mine,
        down_other,
    ) = tied(
        middle_near,
        down_x32,
        up_swapped,
        hid_mine,
        down_sum,
        down_x3,
        down_sum[2][c3:],
        act_mine,
        act_other,
        down_mine,
        down_other,
    )
    middle_far = attn.gather_two(*middle_near)
    down_x3 = jnp.concatenate([*down_x3, down_x32[: n_block - c2]])
    down_x2 = [down_x32[n_block - c2 :], swap(down_x2, feed.second)]
    up_mine_grad = matmul(second_all, hid_mine, ((0,), (0,))).astype(bf16)
    down_z1b = added(down_sum[1][z1:z2], down_x3[z1:z2])
    out_parts = (
        matmul(act_mine, down_mine, ((1,), (1,))) + matmul(act_other, down_other, ((1,), (1,)))
    ).astype(bf16)
    middle_far, up_swapped, up_mine_grad, down_x2, down_x3, down_sum, down_z1b, out_parts = tied(
        middle_far, up_swapped, up_mine_grad, down_x2, down_x3, down_sum, down_z1b, out_parts
    )
    middle_all = team_rows(*middle_near, *middle_far)
    grad_heads = matmul(middle_all, w_team, ((1,), (1,))).astype(bf16)
    grad_own = grad_heads[:, :HEAD]
    grad_got = [
        swap(grad_heads[:, r * HEAD : (r + 1) * HEAD], plan.head_rel[r]) for r in range(1, 4)
    ]
    down_z1 += [swap(down_z1b, feed.first)]
    out_grad = matmul(attended_team, middle_all, ((0,), (0,))).astype(bf16).reshape(4, HEAD, width)
    up_sum = feed.first_sum(up_mine_grad, up_swapped)
    down_z1c = added(down_sum[1][z2:], down_x3[z2:])
    grad_got, up_sum, out_grad, down_z1, down_z1c, out_parts = tied(
        grad_got, up_sum, out_grad, down_z1, down_z1c, out_parts
    )
    up_x3 = swap(up_sum[3], feed.second)
    down_z1 += [swap(down_z1c, feed.first)]
    out_near = feed.scatter_one(out_parts)
    for bit in plan.parts:
        lower, upper = jnp.split(out_grad, 2, axis=1)
        kept = jnp.where(has(bit), upper, lower)
        out_grad = added(kept, swap(jnp.where(has(bit), lower, upper), bit))
    dq, dkv_own, dkv_other = attend_back(
        plan,
        info,
        frame_real,
        own,
        keys,
        values,
        jnp.stack([grad_own] + grad_got).reshape(16, rows, HEAD),
        attended_t,
        log_total,
    )
    dq, dkv_own, dkv_other, up_x3, down_z1, out_near, out_grad = tied(
        dq, dkv_own, dkv_other, up_x3, down_z1, out_near, out_grad
    )
    dkv = dkv_own.astype(f32)
    for i, rel in enumerate(plan.part_rel[1:]):
        dkv = dkv + swap(dkv_other[i], rel).astype(f32)
    triple = jnp.concatenate([dq, dkv.astype(bf16)], axis=2).reshape(4, 4 * rows, 3 * HEAD)
    up_z1 = added(up_sum[1], up_x3)
    za, zb = n_block * 3 // 8, n_block * 5 // 8
    out_grad = out_grad.reshape(2, 2, HEAD // len(plan.part_rel), width)
    triple, up_sum, up_z1, up_z1a, down_z1, out_grad, out_sent = tied(
        triple, up_sum, up_z1, up_z1[:za], down_z1, out_grad, out_grad[:, 1]
    )
    got = [swap(triple[r], plan.head_rel[r]) for r in range(1, 4)]
    up_z1a = swap(up_z1a, feed.first)
    down_done = added(down_sum[0], jnp.concatenate(down_x2), jnp.concatenate(down_z1))
    down_rows, down_rows_hi = unsettle(by_hi_lo_core, down_done)
    got, up_z1a, up_z1b, up_z1c, down_rows, down_rows_hi, up_sum, out_grad, out_near = tied(
        got, up_z1a, up_z1[za:zb], up_z1[zb:], down_rows, down_rows_hi, up_sum, out_grad, out_near
    )
    places = (my_head ^ jnp.arange(4, dtype=jnp.int32)) ^ core_flip
    mixed_grad = turn_back(places, cosine, sine, [triple[0]] + got)
    mixed_grad_mine, mixed_grad_other = mixed_grad[0], mixed_grad[1]
    qkv_other_grad = matmul(first_all, mixed_grad_other, ((0,), (0,))).astype(bf16)
    out_sum = feed.scatter_two(*out_near)
    up_x2a = swap(up_sum[2][:half], feed.second)
    up_z1b = swap(up_z1b, feed.first)
    (
        qkv_other_grad,
        mixed_grad_mine,
        mixed_grad_other,
        up_x2a,
        up_z1b,
        up_z1c,
        up_x2b,
        up_sum,
        down_rows,
        down_rows_hi,
        out_sum,
    ) = tied(
        qkv_other_grad,
        mixed_grad_mine,
        mixed_grad_other,
        up_x2a,
        up_z1b,
        up_z1c,
        up_sum[2][half:],
        up_sum,
        down_rows,
        down_rows_hi,
        out_sum,
    )
    qkv_swapped = swap(qkv_other_grad, 1)
    up_x2b = swap(up_x2b, feed.second)
    up_z1c = swap(up_z1c, feed.first)
    down_rows = jnp.stack([down_rows, swap(down_rows_hi, feed.team_hi)]).reshape(2, 2, 2, shard, n_ff)
    qkv_mine_grad = matmul(first_all, mixed_grad_mine, ((0,), (0,))).astype(bf16)
    first_parts = matmul(mixed_grad_mine, qkv_mine, ((1,), (1,))) + matmul(
        mixed_grad_other, qkv_other, ((1,), (1,))
    )
    qkv_sum = attn.first_sum(qkv_mine_grad, qkv_swapped)
    qkv_sum, first_parts, up_x2b, up_sum, up_z1c, down_rows, down_send, out_grad = tied(
        qkv_sum,
        first_parts.astype(bf16),
        up_x2b,
        up_sum,
        up_z1c,
        down_rows,
        down_rows[:, 1],
        out_grad,
    )
    qkv_x3 = swap(qkv_sum[3], attn.second)
    first_back = attn.scatter_one(first_parts)
    up_done = added(
        up_sum[0],
        jnp.concatenate([up_x2a, up_x2b]),
        jnp.concatenate([up_z1a, up_z1b, up_z1c]),
    )
    down_rows = jnp.stack([down_rows[:, 0], swap(down_send, feed.team_lo)])
    up_rows, up_rows_hi = unsettle(by_hi_lo_core, up_done)
    up_rows = jnp.stack([up_rows, swap(up_rows_hi, feed.team_hi)]).reshape(2, 2, 2, shard, n_ff)
    qkv_x3, first_back, up_rows, qkv_sum, down_rows, up_send = tied(
        qkv_x3, first_back, up_rows, qkv_sum, down_rows, up_rows[:, 1]
    )
    qkv_z1 = swap(added(qkv_sum[1], qkv_x3), attn.first)
    qkv_x2 = swap(qkv_sum[2], attn.second)
    first_rows = attn.scatter_two(*first_back)
    output = (middle + feed.from_rel(out_sum)).astype(bf16)
    up_rows = jnp.stack([up_rows[:, 0], swap(up_send, feed.team_lo)])
    qkv_z1, qkv_x2, first_rows, out_grad, out_sent, output, up_rows, down_rows = tied(
        qkv_z1, qkv_x2, first_rows, out_grad, out_sent, output, up_rows, down_rows
    )
    down_rows = jnp.stack([down_rows[:, :, 0], swap(down_rows[:, :, 1], 1)])
    grad_down, _ = restore(False, by_core_lo_hi, down_rows.reshape(8, shard, n_ff), w_down, gain_two)
    up_rows = jnp.stack([up_rows[:, :, 0], swap(up_rows[:, :, 1], 1)])
    grad_up, grad_gain_two = restore(
        True, by_core_lo_hi, up_rows.reshape(8, shard, n_ff), w_up, gain_two
    )
    qkv_got = attn.octet(added(qkv_sum[0], qkv_x2, qkv_z1))
    grad_first = attn.from_rel(first_rows)
    grad_inputs = grad_middle + layer_norm_back(grad_first, *layer_norm(inputs))
    out_grad = added(out_grad[:, 0], swap(out_sent, attn.second))
    out_grad = out_grad[0].astype(f32) + swap(out_grad[1], attn.first).astype(f32)
    grad_qkv, grad_gain_one = deliver(qkv_columns, qkv_got, w_qkv, gain_one)
    return (
        output[None],
        grad_inputs[None],
        grad_gain_one[:, 0],
        grad_qkv,
        out_grad,
        grad_gain_two[:, 0],
        grad_up,
        grad_down,
    )


def solution(mesh):
    plan = Plan(mesh.shape["tm"], mesh.shape["space"], BLOCK)
    tokens = P("tm", "space", None)
    line = P(("tm", "space"))
    table = P(("tm", "space"), None)
    return jax.shard_map(
        functools.partial(on_device, plan),
        mesh=mesh,
        in_specs=(tokens, P(), line, table, table, line, table, table, tokens),
        out_specs=(tokens, tokens, line, table, table, line, table, table),
        check_vma=False,
    )
```
